128 devices in a mesh: dp: 8 (over z, x_hi), pair: 16 (over x_lo, y, core).
Axes of the slice: x: 4 (x_hi: 2, x_lo: 2; x = x_hi * 2 + x_lo), y: 4, z: 4, core: 2. Of those that a mesh axis runs over, the one named last changes fastest.
Arguments:
- pair_in: bfloat16 [1024, 128, 128], P(('dp', 'pair')), parts along dimension 0, may hold values from -170 to 170
- cotangent: bfloat16 [1024, 128, 128], P(('dp', 'pair')), parts along dimension 0, may hold values from -6 to 6
- in_gain: float32 [2, 128], replicated, may hold values from 0.1 to 1.9
- proj_weight: bfloat16 [2, 128, 512], replicated, may hold values from -0.5 to 0.5
- gate_weight: bfloat16 [2, 128, 128], replicated, may hold values from -0.5 to 0.5
- mid_gain: float32 [2, 128], replicated, may hold values from 0.1 to 1.9
- out_weight: bfloat16 [2, 128, 128], replicated, may hold values from -0.5 to 0.5
Outputs:
- pair_grad: bfloat16 [1024, 128, 128], P(('dp', 'pair')), parts along dimension 0
- proj_grad: float32 [16, 128, 512], P('dp'), parts along dimension 0
- gate_grad: float32 [16, 128, 128], P('dp'), parts along dimension 0
- out_grad: float32 [16, 128, 128], P('dp'), parts along dimension 0
- in_gain_grad: float32 [16, 128], P('dp'), parts along dimension 0
- mid_gain_grad: float32 [16, 128], P('dp'), parts along dimension 0
The draws below stay inside these ranges and needn't reach their ends.
There are 8 independent parts, one for each index of `dp`. The reference program is written for one: setup_inputs(seed, part) draws one part's arguments, and reference() takes and returns one part's arrays. A program takes and returns all parts, laid end to end along the dimension named above; an argument that names none is the same for every part. Nothing has to cross between parts.
All inputs are finite; a program needn't handle non-finite values.
Results may differ from the reference program's by a relative error of at most 0.03.
Values may be sent and summed in bfloat16 or wider, within the bound.
A program may use at most 128 MiB of HBM per device.

```python
import math
import jax
import jax.numpy as jnp
from jax import lax

C = 128
H = 128
N = 128


def draw_pair_in(key, part):
    key = jax.random.fold_in(key, 11)
    subkeys = jax.random.split(key, 3)
    channel_scale = jnp.exp(jax.random.uniform(subkeys[1], (C,), jnp.float32, 0.0, math.log(10.0)))
    cell_scale = jnp.exp(jax.random.uniform(subkeys[2], (N, N, 1), jnp.float32, 0.0, math.log(10.0)))
    pattern = jax.random.truncated_normal(subkeys[0], -4.0, 4.0, (N, N, C), jnp.float32)
    return (pattern * channel_scale * cell_scale / 3.0).astype(jnp.bfloat16)


def block_levels(key, extent, cuts, least, top_value):
    factor_of, own = 1.0, jax.random.fold_in(key, 6)
    for position, parts in cuts:
        steps = jnp.exp(jax.random.uniform(jax.random.fold_in(own, position), (parts,), jnp.float32, least / len(cuts), top_value / len(cuts)))
        factor_of = factor_of * jnp.repeat(steps, extent[position] // parts).reshape([-1 if axis == position else 1 for axis in range(len(extent))])
    return factor_of


def gaussian(own_key, dims, scale, most, cuts=(), dtype=jnp.bfloat16):
    values = scale * jax.random.normal(own_key, dims, jnp.float32)
    if cuts:
        values = values * block_levels(own_key, dims, cuts, -0.22, 0.18)
    return jnp.clip(values, -most, most).astype(dtype)


def setup_inputs(seed: int = 0, part: int = 0) -> dict:
    streams_of = jax.random.split(jax.random.key(seed), 8)
    part_keys = jax.random.split(jax.random.fold_in(streams_of[7], part), 8)
    pair_in = draw_pair_in(jax.random.fold_in(jax.random.fold_in(streams_of[7], part), 71), part)
    cotangent = gaussian(part_keys[1], (N, N, C), 1.0, 6.0, ((0, 16),))
    in_gain = jnp.clip(1.0 + 0.18 * jax.random.normal(streams_of[2], (2, C), jnp.float32), 0.1, 1.9)
    proj_weight = gaussian(streams_of[3], (2, C, 4 * H), C ** -0.5, 0.5)
    gate_weight = gaussian(streams_of[4], (2, C, C), C ** -0.5, 0.5)
    mid_gain = jnp.clip(1.0 + 0.18 * jax.random.normal(streams_of[5], (2, H), jnp.float32), 0.1, 1.9)
    out_weight = gaussian(streams_of[6], (2, H, C), H ** -0.5, 0.5)
    return dict(pair_in=pair_in, cotangent=cotangent, in_gain=in_gain, proj_weight=proj_weight, gate_weight=gate_weight, mid_gain=mid_gain, out_weight=out_weight)


EPSILON = 1e-05

def norm_forward(values, gain_vec):
    centre = lax.optimization_barrier(jnp.mean(values, axis=-1, keepdims=True))
    shifted = values - centre
    inverse = lax.rsqrt(lax.optimization_barrier(jnp.mean(shifted * shifted, axis=-1, keepdims=True)) + EPSILON)
    unit_rows = shifted * inverse
    return (unit_rows * gain_vec, unit_rows, inverse)

def norm_backward(grad_rows, unit_rows, inverse, gain_vec):
    scaled = grad_rows * gain_vec
    mean_one = lax.optimization_barrier(jnp.mean(scaled, axis=-1, keepdims=True))
    mean_two = lax.optimization_barrier(jnp.mean(scaled * unit_rows, axis=-1, keepdims=True))
    grad_input = inverse * (scaled - mean_one - unit_rows * mean_two)
    channels = unit_rows.shape[-1]
    grad_gain = lax.optimization_barrier(jnp.sum((grad_rows * unit_rows).reshape(-1, channels), axis=0))
    return (grad_input, grad_gain)

def cell_contract(first, second):
    flat_first = first.reshape(-1, first.shape[-1])
    flat_second = second.reshape(-1, second.shape[-1])
    return lax.dot_general(flat_first, flat_second, (((0,), (0,)), ((), ())), preferred_element_type=jnp.float32)

def project_rows(state_rows, gain_vec, proj_mat, gate_mat):
    normed, unit_rows, inverse = norm_forward(state_rows.astype(jnp.float32), gain_vec)
    normed_b = normed.astype(jnp.bfloat16)
    projected = jnp.dot(normed_b, proj_mat, preferred_element_type=jnp.float32)
    gate_pre = jnp.dot(normed_b, gate_mat, preferred_element_type=jnp.float32)
    hidden_width = proj_mat.shape[1] // 4
    left_rows = (jax.nn.sigmoid(projected[..., :hidden_width]) * projected[..., hidden_width:2 * hidden_width]).astype(jnp.bfloat16)
    right_rows = (jax.nn.sigmoid(projected[..., 2 * hidden_width:3 * hidden_width]) * projected[..., 3 * hidden_width:]).astype(jnp.bfloat16)
    return (unit_rows, inverse, normed_b, projected, gate_pre, left_rows, right_rows)

def finish_rows(state_rows, product, saved, gain_vec, out_mat):
    mixed, mix_unit, mix_inverse = norm_forward(product, gain_vec)
    mixed_rows = mixed.astype(jnp.bfloat16)
    output = jnp.dot(mixed_rows, out_mat, preferred_element_type=jnp.float32)
    gate_value = jax.nn.sigmoid(saved[4])
    new_state = (state_rows.astype(jnp.float32) + gate_value * output).astype(jnp.bfloat16)
    return (new_state, (mix_unit, mix_inverse, mixed_rows, output, gate_value))

def back_head(gradient, finished, gain_vec, out_mat):
    mix_unit, mix_inverse, mixed_rows, output, gate_value = finished
    gate_back = gradient * output * gate_value * (1.0 - gate_value)
    grad_output = (gradient * gate_value).astype(jnp.bfloat16)
    grad_mixed = jnp.dot(grad_output, out_mat.T, preferred_element_type=jnp.float32)
    weight_part = cell_contract(mixed_rows, grad_output)
    grad_product, gain_part = norm_backward(grad_mixed, mix_unit, mix_inverse, gain_vec)
    return (grad_product.astype(jnp.bfloat16), gate_back, weight_part, gain_part)

def back_tail(gradient, gate_back, grad_left, grad_right, saved, gain_vec, proj_mat, gate_mat):
    unit_rows, inverse, normed_b, projected, gate_pre, left_rows, right_rows = saved
    hidden_width = proj_mat.shape[1] // 4
    sigma_left = jax.nn.sigmoid(projected[..., :hidden_width])
    sigma_right = jax.nn.sigmoid(projected[..., 2 * hidden_width:3 * hidden_width])
    value_left = projected[..., hidden_width:2 * hidden_width]
    value_right = projected[..., 3 * hidden_width:]
    pieces = [grad_left * value_left * sigma_left * (1.0 - sigma_left), grad_left * sigma_left, grad_right * value_right * sigma_right * (1.0 - sigma_right), grad_right * sigma_right]
    grad_proj = jnp.concatenate(pieces, axis=-1).astype(jnp.bfloat16)
    gate_term = gate_back.astype(jnp.bfloat16)
    grad_normed = jnp.dot(grad_proj, proj_mat.T, preferred_element_type=jnp.float32) + jnp.dot(gate_term, gate_mat.T, preferred_element_type=jnp.float32)
    proj_part = cell_contract(normed_b, grad_proj)
    gate_part = cell_contract(normed_b, gate_term)
    grad_input, gain_part = norm_backward(grad_normed, unit_rows, inverse, gain_vec)
    return (gradient + grad_input, proj_part, gate_part, gain_part)

def big_einsum(form, first, second):
    return jnp.einsum(form, first.astype(jnp.float32), second.astype(jnp.float32), precision=lax.Precision.HIGHEST)

def reference(pair_in, cotangent, in_gain, proj_weight, gate_weight, mid_gain, out_weight):
    saved_out = project_rows(pair_in, in_gain[0], proj_weight[0], gate_weight[0])
    left_out, right_out = (saved_out[5], saved_out[6])
    product_out = big_einsum('ikc,jkc->ijc', left_out, right_out)
    state_mid, finish_out = finish_rows(pair_in, product_out, saved_out, mid_gain[0], out_weight[0])
    saved_in = project_rows(state_mid, in_gain[1], proj_weight[1], gate_weight[1])
    left_in, right_in = (saved_in[5], saved_in[6])
    product_in = big_einsum('kic,kjc->ijc', left_in, right_in)
    finish_in = finish_rows(state_mid, product_in, saved_in, mid_gain[1], out_weight[1])[1]
    gradient = cotangent.astype(jnp.float32)
    grad_prod_in, gate_back_in, outw_in, midg_in = back_head(gradient, finish_in, mid_gain[1], out_weight[1])
    grad_left_in = big_einsum('ijc,kjc->kic', grad_prod_in, right_in)
    grad_right_in = big_einsum('ijc,kic->kjc', grad_prod_in, left_in)
    gradient, projg_in, gateg_in, ing_in = back_tail(gradient, gate_back_in, grad_left_in, grad_right_in, saved_in, in_gain[1], proj_weight[1], gate_weight[1])
    grad_prod_out, gate_back_out, outw_out, midg_out = back_head(gradient, finish_out, mid_gain[0], out_weight[0])
    grad_left_out = big_einsum('ijc,jkc->ikc', grad_prod_out, right_out)
    grad_right_out = big_einsum('ijc,ikc->jkc', grad_prod_out, left_out)
    gradient, projg_out, gateg_out, ing_out = back_tail(gradient, gate_back_out, grad_left_out, grad_right_out, saved_out, in_gain[0], proj_weight[0], gate_weight[0])
    scale = 1.0 / N
    return (gradient.astype(jnp.bfloat16), jnp.stack([projg_out, projg_in]) * scale, jnp.stack([gateg_out, gateg_in]) * scale, jnp.stack([outw_out, outw_in]) * scale, jnp.stack([ing_out, ing_in]) * scale, jnp.stack([midg_out, midg_in]) * scale)
```

```python
import functools

import jax
import jax.numpy as jnp
from jax import lax
from jax.experimental import pallas as pl
from jax.experimental.pallas import tpu as pltpu
from jax.sharding import PartitionSpec as P

EPSILON = 1e-05
MESH = pl.DeviceIdType.MESH
F32 = jnp.float32
BF16 = jnp.bfloat16

N = 128
PEERS = 16
ROWS = N // PEERS
CELLS = ROWS * N
WIDE = 2 * N
STEPS = CELLS // WIDE

TO_CH_0, TO_ROW_0, TO_CH_1, TO_ROW_1, GRAD_CH_1, GRAD_ROW_1, GRAD_CH_0, GRAD_ROW_0 = range(8)
SUM_EARLY, ALL_EARLY, SUM_LATE, ALL_LATE, GAINS = range(8, 13)
PHASES = 13


def dot(first, second, dims):
    return lax.dot_general(first, second, (dims, ((), ())), preferred_element_type=F32)


def nn(first, second):
    return dot(first, second, ((1,), (0,)))


def nt(first, second):
    return dot(first, second, ((1,), (1,)))


def tn(first, second):
    return dot(first, second, ((0,), (0,)))


def mean_channels(values):
    return jnp.sum(values, axis=0, keepdims=True) * (1.0 / N)


def norm_forward(values):
    shifted = values - mean_channels(values)
    inverse = lax.rsqrt(mean_channels(shifted * shifted) + EPSILON)
    return shifted * inverse, inverse


def norm_backward(scaled, unit, inverse):
    return inverse * (scaled - mean_channels(scaled) - unit * mean_channels(scaled * unit))


def kernel(
    pair_in, cotangent, in_gain, proj_weight, gate_weight, mid_gain, out_weight,
    pair_grad, proj_grad, gate_grad, out_grad, in_gain_grad, mid_gain_grad,
    gains, weight, weight_t, out_t,
    state0, state1, cot, grad1,
    unit, inverse, normed, sig_l, val_l, sig_r, val_r, gate, output, mix_unit, mix_inverse, mixed,
    go, gp, in_acc, mid_acc,
    turn_a, turn_b, chan_l, chan_r,
    send2, recv2, send1, recv1,
    sum_early_send, sum_early_recv, all_early, sum_late_send, sum_late_recv, all_late, gains_all,
    send_sem, recv_sem,
):
    me = lax.axis_index("pair")
    my_x, my_y, my_core = me // 8, (me // 2) % 4, me % 2

    def peer(o):
        x = (my_x + o // 8) % 2
        y = (my_y + (o // 2) % 4) % 4
        core = (my_core + o % 2) % 2
        return x * 8 + y * 2 + core

    def copy_to(phase, src, dst, target):
        return pltpu.make_async_remote_copy(
            src_ref=src, dst_ref=dst,
            send_sem=send_sem.at[phase, target], recv_sem=recv_sem.at[phase, me],
            device_id={"pair": target}, device_id_type=MESH,
        )

    def send_all(phase, src_of, dst):
        @pl.loop(0, PEERS - 1)
        def _(i):
            target = peer(PEERS - 1 - i)
            copy_to(phase, src_of(target), dst, target).start()

    def wait_all(phase, slot_of):
        @pl.loop(1, PEERS)
        def _(o):
            source = peer(o)
            pltpu.make_async_copy(slot_of(source), slot_of(source), recv_sem.at[phase, source]).wait()

    def wait_sent(phase, src_of):
        @pl.loop(1, PEERS)
        def _(o):
            target = peer(o)
            pltpu.make_async_copy(src_of(target), src_of(target), send_sem.at[phase, target]).wait()

    barrier = pltpu.get_barrier_semaphore()

    @pl.loop(1, PEERS)
    def _(o):
        pl.semaphore_signal(barrier, inc=1, device_id={"pair": peer(o)}, device_id_type=MESH)

    for l in range(2):
        for table, source in ((0, in_gain), (1, mid_gain)):
            row = jnp.broadcast_to(source[l : l + 1, :], (N, N)).T
            gains[2 * l + table] = jnp.concatenate([row, row], axis=1)
        for f in range(4):
            block = proj_weight[l, :, f * N : (f + 1) * N]
            weight[l, :, f * N : (f + 1) * N] = block
            weight_t[l, f * N : (f + 1) * N, :] = block.astype(F32).T.astype(BF16)
        weight[l, :, 4 * N :] = gate_weight[l]
        weight_t[l, 4 * N :, :] = gate_weight[l].astype(F32).T.astype(BF16)
        out_t[l] = out_weight[l].astype(F32).T.astype(BF16)

    for a in range(ROWS):
        state0[:, a * N : (a + 1) * N] = pair_in[a].astype(F32).T

    in_acc[...] = jnp.zeros_like(in_acc)
    mid_acc[...] = jnp.zeros_like(mid_acc)

    def lanes(p):
        return pl.ds(pl.multiple_of(p * WIDE, WIDE), WIDE)

    def put_turned(ref, p, values):
        for h in range(2):
            ref[pl.ds(2 * p + h, N, stride=ROWS), :] = values[:, h * N : (h + 1) * N]

    def get_turned(ref, p):
        return jnp.concatenate([ref[pl.ds(2 * p + h, N, stride=ROWS), :] for h in range(2)], axis=1)

    def project(l, p, state):
        at = lanes(p)
        unit_p, inverse_p = norm_forward(state)
        normed_p = (unit_p * gains[2 * l]).astype(BF16)
        unit[l, :, at] = unit_p
        inverse[l, :, at] = inverse_p
        normed[l, :, at] = normed_p
        projected = nn(weight_t[l], normed_p)
        sig = jax.nn.sigmoid(projected[0:N])
        val = projected[N : 2 * N]
        sig_l[l, :, at] = sig
        val_l[l, :, at] = val
        put_turned(turn_a, p, sig * val)
        sig = jax.nn.sigmoid(projected[2 * N : 3 * N])
        val = projected[3 * N : 4 * N]
        sig_r[l, :, at] = sig
        val_r[l, :, at] = val
        put_turned(turn_b, p, sig * val)
        gate[l, :, at] = jax.nn.sigmoid(projected[4 * N :])

    def send_two(slot, phase):
        @pl.loop(0, PEERS)
        def _(d):
            rows = pl.ds(pl.multiple_of(d * ROWS * ROWS, ROWS * ROWS), ROWS * ROWS)
            send2[slot, d, 0:64, :] = turn_a[rows, :].astype(BF16)
            send2[slot, d, 64:128, :] = turn_b[rows, :].astype(BF16)

        send_all(phase, lambda d: send2.at[slot, d], recv2.at[slot, me])
        recv2[slot, me] = send2[slot, me]

    def send_one(slot, phase):
        @pl.loop(0, PEERS)
        def _(d):
            rows = pl.ds(pl.multiple_of(d * ROWS * ROWS, ROWS * ROWS), ROWS * ROWS)
            send1[slot, d] = turn_a[rows, :].astype(BF16)

        send_all(phase, lambda d: send1.at[slot, d], recv1.at[slot, me])
        recv1[slot, me] = send1[slot, me]

    def take_two(slot, phase):
        wait_all(phase, lambda s: recv2.at[slot, s])

        @pl.loop(0, PEERS)
        def _(s):
            rows = pl.ds(pl.multiple_of(s * ROWS * ROWS, ROWS * ROWS), ROWS * ROWS)
            turn_a[rows, :] = recv2[slot, s, 0:64, :].astype(F32)
            turn_b[rows, :] = recv2[slot, s, 64:128, :].astype(F32)

    def take_one(slot, phase):
        wait_all(phase, lambda s: recv1.at[slot, s])

        @pl.loop(0, PEERS)
        def _(s):
            rows = pl.ds(pl.multiple_of(s * ROWS * ROWS, ROWS * ROWS), ROWS * ROWS)
            turn_a[rows, :] = recv1[slot, s].astype(F32)

    def two_channels(block):
        wide = block.astype(F32).reshape(PEERS, 2, ROWS, N)
        return [wide[:, h].reshape(N, N).astype(BF16) for h in range(2)]

    def join_channels(first, second):
        pair = jnp.stack([first.reshape(PEERS, ROWS, N), second.reshape(PEERS, ROWS, N)], axis=1)
        return pair.reshape(PEERS, 2 * ROWS, N).astype(BF16)

    def channel_forward(l, slot2, slot1, phase_in, phase_out):
        wait_all(phase_in, lambda s: recv2.at[slot2, s])
        for q in range(ROWS // 2):
            lefts = two_channels(recv2[slot2, :, 16 * q : 16 * q + 16, :])
            rights = two_channels(recv2[slot2, :, 64 + 16 * q : 64 + 16 * q + 16, :])
            products = []
            for h in range(2):
                chan_l[l, 2 * q + h] = lefts[h]
                chan_r[l, 2 * q + h] = rights[h]
                products.append(nt(lefts[h], rights[h]) if l == 0 else tn(lefts[h], rights[h]))
            send1[slot1, :, 16 * q : 16 * q + 16, :] = join_channels(*products)
        send_all(phase_out, lambda d: send1.at[slot1, d], recv1.at[slot1, me])
        recv1[slot1, me] = send1[slot1, me]

    def channel_backward(l, slot1, slot2, phase_in, phase_out):
        wait_all(phase_in, lambda s: recv1.at[slot1, s])
        for q in range(ROWS // 2):
            grads = two_channels(recv1[slot1, :, 16 * q : 16 * q + 16, :])
            lefts, rights = [], []
            for h in range(2):
                left, right = chan_l[l, 2 * q + h], chan_r[l, 2 * q + h]
                if l == 0:
                    lefts.append(nn(grads[h], right))
                    rights.append(tn(grads[h], left))
                else:
                    lefts.append(nt(right, grads[h]))
                    rights.append(nn(left, grads[h]))
            send2[slot2, :, 16 * q : 16 * q + 16, :] = join_channels(*lefts)
            send2[slot2, :, 64 + 16 * q : 64 + 16 * q + 16, :] = join_channels(*rights)
        send_all(phase_out, lambda d: send2.at[slot2, d], recv2.at[slot2, me])
        recv2[slot2, me] = send2[slot2, me]

    def finish(l, p):
        at = lanes(p)
        mix_unit_p, mix_inverse_p = norm_forward(get_turned(turn_a, p))
        mixed_p = (mix_unit_p * gains[2 * l + 1]).astype(BF16)
        mix_unit[l, :, at] = mix_unit_p
        mix_inverse[l, :, at] = mix_inverse_p
        mixed[l, :, at] = mixed_p
        output_p = nn(out_t[l], mixed_p)
        output[l, :, at] = output_p
        return output_p

    def fold(values):
        return values[:, :N] + values[:, N:]

    def back_head(l, p, gradient):
        at = lanes(p)
        gate_p = gate[l, :, at]
        go_p = (gradient * gate_p).astype(BF16)
        go[l, :, at] = go_p
        gp[l, 4 * N :, at] = (gradient * output[l, :, at] * gate_p * (1.0 - gate_p)).astype(BF16)
        grad_mixed = nn(out_weight[l], go_p)
        mix_unit_p = mix_unit[l, :, at]
        mid_acc[l] += fold(grad_mixed * mix_unit_p)
        grad_product = norm_backward(grad_mixed * gains[2 * l + 1], mix_unit_p, mix_inverse[l, :, at])
        put_turned(turn_a, p, grad_product)

    def back_tail(l, p, gradient):
        at = lanes(p)
        grad_left = get_turned(turn_a, p)
        grad_right = get_turned(turn_b, p)
        sig = sig_l[l, :, at]
        plain = grad_left * sig
        gp[l, 0:N, at] = (plain * val_l[l, :, at] * (1.0 - sig)).astype(BF16)
        gp[l, N : 2 * N, at] = plain.astype(BF16)
        sig = sig_r[l, :, at]
        plain = grad_right * sig
        gp[l, 2 * N : 3 * N, at] = (plain * val_r[l, :, at] * (1.0 - sig)).astype(BF16)
        gp[l, 3 * N : 4 * N, at] = plain.astype(BF16)
        grad_normed = nn(weight[l], gp[l, :, at])
        unit_p = unit[l, :, at]
        in_acc[l] += fold(grad_normed * unit_p)
        return gradient + norm_backward(grad_normed * gains[2 * l], unit_p, inverse[l, :, at])

    @pl.loop(0, STEPS)
    def _(p):
        project(0, p, state0[:, lanes(p)])

    pl.semaphore_wait(barrier, PEERS - 1)
    send_two(0, TO_CH_0)
    for a in range(ROWS):
        cot[:, a * N : (a + 1) * N] = cotangent[a].astype(F32).T
    channel_forward(0, 0, 0, TO_CH_0, TO_ROW_0)
    take_one(0, TO_ROW_0)

    @pl.loop(0, STEPS)
    def _(p):
        at = lanes(p)
        output_p = finish(0, p)
        state = (state0[:, at] + gate[0, :, at] * output_p).astype(BF16).astype(F32)
        state1[:, at] = state
        project(1, p, state)

    send_two(1, TO_CH_1)
    channel_forward(1, 1, 1, TO_CH_1, TO_ROW_1)
    take_one(1, TO_ROW_1)

    @pl.loop(0, STEPS)
    def _(p):
        finish(1, p)
        back_head(1, p, cot[:, lanes(p)])

    send_one(2, GRAD_CH_1)
    channel_backward(1, 2, 2, GRAD_CH_1, GRAD_ROW_1)
    take_two(2, GRAD_ROW_1)

    @pl.loop(0, STEPS)
    def _(p):
        at = lanes(p)
        gradient = back_tail(1, p, cot[:, at])
        grad1[:, at] = gradient
        back_head(0, p, gradient)

    send_one(3, GRAD_CH_0)

    def put_early(first, values):
        for i in range(N // 64):
            sum_early_send[first + i] = values[64 * i : 64 * i + 64, :].astype(BF16)

    for f in range(5):
        put_early(2 * f, nt(normed[1], gp[1, f * N : (f + 1) * N, :]))
    put_early(10, nt(mixed[1], go[1]))
    put_early(12, nt(normed[0], gp[0, 4 * N :, :]))
    put_early(14, nt(mixed[0], go[0]))
    send_all(SUM_EARLY, lambda d: sum_early_send.at[d], sum_early_recv.at[me])
    sum_early_recv[me] = sum_early_send[me]

    channel_backward(0, 3, 3, GRAD_CH_0, GRAD_ROW_0)

    wait_all(SUM_EARLY, lambda s: sum_early_recv.at[s])
    all_early[me] = jnp.sum(sum_early_recv[...].astype(F32), axis=0).astype(BF16)
    send_all(ALL_EARLY, lambda d: all_early.at[me], all_early.at[me])

    take_two(3, GRAD_ROW_0)

    @pl.loop(0, STEPS)
    def _(p):
        at = lanes(p)
        gradient = back_tail(0, p, grad1[:, at])
        for h in range(2):
            pair_grad[2 * p + h] = gradient[:, h * N : (h + 1) * N].T.astype(BF16)

    for f in range(4):
        values = nt(normed[0], gp[0, f * N : (f + 1) * N, :])
        for i in range(4):
            sum_late_send[4 * f + i] = values[32 * i : 32 * i + 32, :].astype(BF16)
    send_all(SUM_LATE, lambda d: sum_late_send.at[d], sum_late_recv.at[me])
    sum_late_recv[me] = sum_late_send[me]

    gain_rows = [jnp.sum(ref[l].T, axis=0, keepdims=True) for ref in (in_acc, mid_acc) for l in range(2)]
    gains_all[me] = jnp.concatenate(gain_rows + [jnp.zeros((4, N), F32)], axis=0)
    send_all(GAINS, lambda d: gains_all.at[me], gains_all.at[me])

    wait_all(SUM_LATE, lambda s: sum_late_recv.at[s])
    all_late[me] = jnp.sum(sum_late_recv[...].astype(F32), axis=0).astype(BF16)
    send_all(ALL_LATE, lambda d: all_late.at[me], all_late.at[me])

    scale = 1.0 / N
    wait_all(ALL_EARLY, lambda s: all_early.at[s])

    def early(first):
        return all_early[first : first + 2].astype(F32).reshape(N, N) * scale

    for f in range(4):
        proj_grad[1, :, f * N : (f + 1) * N] = early(2 * f)
    gate_grad[1] = early(8)
    out_grad[1] = early(10)
    gate_grad[0] = early(12)
    out_grad[0] = early(14)

    wait_all(GAINS, lambda s: gains_all.at[s])
    total = jnp.sum(gains_all[...], axis=0) * scale
    in_gain_grad[...] = total[0:2]
    mid_gain_grad[...] = total[2:4]

    wait_all(ALL_LATE, lambda s: all_late.at[s])
    for f in range(4):
        proj_grad[0, :, f * N : (f + 1) * N] = all_late[4 * f : 4 * f + 4].astype(F32).reshape(N, N) * scale

    wait_sent(TO_CH_0, lambda d: send2.at[0, d])
    wait_sent(TO_ROW_0, lambda d: send1.at[0, d])
    wait_sent(TO_CH_1, lambda d: send2.at[1, d])
    wait_sent(TO_ROW_1, lambda d: send1.at[1, d])
    wait_sent(GRAD_CH_1, lambda d: send1.at[2, d])
    wait_sent(GRAD_ROW_1, lambda d: send2.at[2, d])
    wait_sent(GRAD_CH_0, lambda d: send1.at[3, d])
    wait_sent(GRAD_ROW_0, lambda d: send2.at[3, d])
    wait_sent(SUM_EARLY, lambda d: sum_early_send.at[d])
    wait_sent(ALL_EARLY, lambda d: all_early.at[me])
    wait_sent(SUM_LATE, lambda d: sum_late_send.at[d])
    wait_sent(ALL_LATE, lambda d: all_late.at[me])
    wait_sent(GAINS, lambda d: gains_all.at[me])


def on_device(*arrays):
    layer_f32 = pltpu.VMEM((2, N, CELLS), F32)
    layer_bf16 = pltpu.VMEM((2, N, CELLS), BF16)
    plain_f32 = pltpu.VMEM((N, CELLS), F32)
    return pl.pallas_call(
        kernel,
        out_shape=(
            jax.ShapeDtypeStruct((ROWS, N, N), BF16),
            jax.ShapeDtypeStruct((2, N, 4 * N), F32),
            jax.ShapeDtypeStruct((2, N, N), F32),
            jax.ShapeDtypeStruct((2, N, N), F32),
            jax.ShapeDtypeStruct((2, N), F32),
            jax.ShapeDtypeStruct((2, N), F32),
        ),
        in_specs=[pl.BlockSpec(memory_space=pltpu.VMEM)] * 7,
        out_specs=[pl.BlockSpec(memory_space=pltpu.VMEM)] * 6,
        scratch_shapes=[
            pltpu.VMEM((4, N, WIDE), F32),
            pltpu.VMEM((2, N, 5 * N), BF16),
            pltpu.VMEM((2, 5 * N, N), BF16),
            pltpu.VMEM((2, N, N), BF16),
            plain_f32, plain_f32, plain_f32, plain_f32,
            layer_f32,
            pltpu.VMEM((2, 1, CELLS), F32),
            layer_bf16,
            layer_f32, layer_f32, layer_f32, layer_f32,
            layer_f32, layer_f32, layer_f32,
            pltpu.VMEM((2, 1, CELLS), F32),
            layer_bf16,
            layer_bf16,
            pltpu.VMEM((2, 5 * N, CELLS), BF16),
            pltpu.VMEM((2, N, N), F32),
            pltpu.VMEM((2, N, N), F32),
            pltpu.VMEM((CELLS, N), F32),
            pltpu.VMEM((CELLS, N), F32),
            pltpu.VMEM((2, ROWS, N, N), BF16),
            pltpu.VMEM((2, ROWS, N, N), BF16),
            pltpu.VMEM((4, PEERS, 128, N), BF16),
            pltpu.VMEM((4, PEERS, 128, N), BF16),
            pltpu.VMEM((4, PEERS, 64, N), BF16),
            pltpu.VMEM((4, PEERS, 64, N), BF16),
            pltpu.VMEM((PEERS, 64, N), BF16),
            pltpu.VMEM((PEERS, 64, N), BF16),
            pltpu.VMEM((PEERS, 64, N), BF16),
            pltpu.VMEM((PEERS, 32, N), BF16),
            pltpu.VMEM((PEERS, 32, N), BF16),
            pltpu.VMEM((PEERS, 32, N), BF16),
            pltpu.VMEM((PEERS, 8, N), F32),
            pltpu.SemaphoreType.DMA((PHASES, PEERS)),
            pltpu.SemaphoreType.DMA((PHASES, PEERS)),
        ],
        compiler_params=pltpu.CompilerParams(
            collective_id=0, has_side_effects=True, vmem_limit_bytes=56 * 1024 * 1024
        ),
    )(*arrays)


def solution(mesh):
    return jax.shard_map(
        on_device,
        mesh=mesh,
        in_specs=(
            P(("dp", "pair"), None, None),
            P(("dp", "pair"), None, None),
            P(),
            P(),
            P(),
            P(),
            P(),
        ),
        out_specs=(
            P(("dp", "pair"), None, None),
            P("dp", None, None),
            P("dp", None, None),
            P("dp", None, None),
            P("dp", None),
            P("dp", None),
        ),
        check_vma=False,
    )
```

```python
import functools

import jax
import jax.numpy as jnp
from jax import lax
from jax.experimental import pallas as pl
from jax.experimental.pallas import tpu as pltpu
from jax.sharding import PartitionSpec as P

EPSILON = 1e-05
MESH = pl.DeviceIdType.MESH
F32 = jnp.float32
BF16 = jnp.bfloat16

N = 128
PEERS = 16
ROWS = N // PEERS
CELLS = ROWS * N
WIDE = 2 * N
STEPS = CELLS // WIDE
CHUNKS = 2
PER = STEPS // CHUNKS
PART = ROWS * ROWS // CHUNKS

TO_CH_0, TO_ROW_0, TO_CH_1, TO_ROW_1, GRAD_CH_1, GRAD_ROW_1, GRAD_CH_0, GRAD_ROW_0 = range(8)
SUM_EARLY, ALL_EARLY, SUM_LATE, ALL_LATE, GAINS = range(8, 13)
PHASES = 13


def dot(first, second, dims):
    return lax.dot_general(first, second, (dims, ((), ())), preferred_element_type=F32)


def nn(first, second):
    return dot(first, second, ((1,), (0,)))


def nt(first, second):
    return dot(first, second, ((1,), (1,)))


def tn(first, second):
    return dot(first, second, ((0,), (0,)))


def mean_channels(values):
    return jnp.sum(values, axis=0, keepdims=True) * (1.0 / N)


def norm_forward(values):
    shifted = values - mean_channels(values)
    inverse = lax.rsqrt(mean_channels(shifted * shifted) + EPSILON)
    return shifted * inverse, inverse


def norm_backward(scaled, unit, inverse):
    return inverse * (scaled - mean_channels(scaled) - unit * mean_channels(scaled * unit))


def kernel(
    pair_hbm, cot_hbm, in_gain_hbm, proj_weight_hbm, gate_weight_hbm, mid_gain_hbm, out_weight_hbm,
    pair_grad, early_out, late_out, gains_out,
    pair_in, cotangent, in_gain, proj_weight, gate_weight, mid_gain, out_weight,
    gains, weight, weight_t, out_t,
    state0, state1, cot, grad1,
    unit, inverse, normed, sig_l, val_l, sig_r, val_r, gate, output, mix_unit, mix_inverse, mixed,
    go, gp, in_acc, mid_acc,
    turn_a, turn_b, chan_l, chan_r,
    send2, recv2, send1, recv1,
    sum_early_send, sum_early_recv, all_early, sum_late_send, sum_late_recv, all_late, gains_all,
    load_sem, send_sem, recv_sem,
):
    me = lax.axis_index("pair")
    my_x, my_y, my_core = me // 8, (me // 2) % 4, me % 2

    def peer(o):
        x = (my_x + o // 8) % 2
        y = (my_y + (o // 2) % 4) % 4
        core = (my_core + o % 2) % 2
        return x * 8 + y * 2 + core

    barrier = pltpu.get_barrier_semaphore()

    peers = [peer(o) for o in range(PEERS - 1, 0, -1)]
    for target in peers:
        pl.semaphore_signal(barrier, inc=1, device_id={"pair": target}, device_id_type=MESH)

    loads = [
        pltpu.make_async_copy(source, target, load_sem.at[i])
        for i, (source, target) in enumerate((
            (pair_hbm, pair_in), (in_gain_hbm, in_gain), (proj_weight_hbm, proj_weight), (gate_weight_hbm, gate_weight),
            (mid_gain_hbm, mid_gain), (out_weight_hbm, out_weight), (cot_hbm, cotangent),
        ))
    ]
    for load in loads:
        load.start()

    def send_part(phase, h, src_of, dst):
        sem = phase * CHUNKS + h
        for target in peers:
            pltpu.make_async_remote_copy(
                src_ref=src_of(target), dst_ref=dst,
                send_sem=send_sem.at[sem], recv_sem=recv_sem.at[sem],
                device_id={"pair": target}, device_id_type=MESH,
            ).start()

    def wait_part(phase, h, slots):
        fifteen = slots.at[pl.ds(0, PEERS - 1)]
        pltpu.make_async_copy(fifteen, fifteen, recv_sem.at[phase * CHUNKS + h]).wait()

    def wait_sent(phase, h, slots):
        fifteen = slots.at[pl.ds(0, PEERS - 1)]
        pltpu.make_async_copy(fifteen, fifteen, send_sem.at[phase * CHUNKS + h]).wait()

    in_acc[...] = jnp.zeros_like(in_acc)
    mid_acc[...] = jnp.zeros_like(mid_acc)

    def lanes(p):
        return slice(p * WIDE, (p + 1) * WIDE)

    def put_rows(ref, first, values):
        parts = [values[:, i * N : (i + 1) * N].reshape(PEERS, ROWS, N) for i in range(2)]
        ref[:, first : first + 2 * ROWS, :] = jnp.concatenate(parts, axis=1).astype(BF16)

    def get_rows(ref, first):
        block = ref[:, first : first + 2 * ROWS, :].astype(F32)
        return jnp.concatenate([block[:, i * ROWS : (i + 1) * ROWS].reshape(N, N) for i in range(2)], axis=1)

    def project(l, p, state, ref):
        at = lanes(p)
        unit_p, inverse_p = norm_forward(state)
        normed_p = (unit_p * gains[2 * l]).astype(BF16)
        unit[l, :, at] = unit_p
        inverse[l, :, at] = inverse_p
        normed[l, :, at] = normed_p
        projected = nn(weight_t[l], normed_p)
        row = 2 * ROWS * (p % PER)
        sig = jax.nn.sigmoid(projected[0:N])
        val = projected[N : 2 * N]
        sig_l[l, :, at] = sig
        val_l[l, :, at] = val
        put_rows(ref, row, sig * val)
        sig = jax.nn.sigmoid(projected[2 * N : 3 * N])
        val = projected[3 * N : 4 * N]
        sig_r[l, :, at] = sig
        val_r[l, :, at] = val
        put_rows(ref, PART + row, sig * val)
        gate[l, :, at] = jax.nn.sigmoid(projected[4 * N :])

    def steps(h):
        return range(h * PER, (h + 1) * PER)

    def send2_part(slot, phase, h):
        send_part(phase, h, lambda d: send2.at[slot, h, d], recv2.at[slot, h, me])
        recv2[slot, h, me] = send2[slot, h, me]

    def send1_part(slot, phase, h):
        send_part(phase, h, lambda d: send1.at[slot, h, d], recv1.at[slot, h, me])
        recv1[slot, h, me] = send1[slot, h, me]

    def wait2_part(slot, phase, h):
        wait_part(phase, h, recv2.at[slot, h])

    def wait1_part(slot, phase, h):
        wait_part(phase, h, recv1.at[slot, h])

    def part_rows(d, h):
        return slice(d * ROWS * ROWS + h * PART, d * ROWS * ROWS + (h + 1) * PART)

    def channel(c):
        return pl.ds(c, N, stride=ROWS)

    def channel_forward(l, slot2, slot1, phase_in, phase_out):
        for h in range(CHUNKS):
            wait2_part(slot2, phase_in, h)
            for s in range(PEERS):
                turn_a[part_rows(s, h), :] = recv2[slot2, h, s, :PART].astype(F32)
                turn_b[part_rows(s, h), :] = recv2[slot2, h, s, PART:].astype(F32)
        for c in range(ROWS):
            left = turn_a[channel(c), :].astype(BF16)
            right = turn_b[channel(c), :].astype(BF16)
            chan_l[l, c] = left
            chan_r[l, c] = right
            turn_a[channel(c), :] = nt(left, right) if l == 0 else tn(left, right)
        for h in range(CHUNKS):
            for d in range(PEERS):
                send1[slot1, h, d] = turn_a[part_rows(d, h), :].astype(BF16)
            send1_part(slot1, phase_out, h)

    def channel_backward(l, slot1, slot2, phase_in, phase_out):
        for h in range(CHUNKS):
            wait1_part(slot1, phase_in, h)
            for s in range(PEERS):
                turn_a[part_rows(s, h), :] = recv1[slot1, h, s].astype(F32)
        for c in range(ROWS):
            grad = turn_a[channel(c), :].astype(BF16)
            left, right = chan_l[l, c], chan_r[l, c]
            turn_a[channel(c), :] = nn(grad, right) if l == 0 else nt(right, grad)
            turn_b[channel(c), :] = tn(grad, left) if l == 0 else nn(left, grad)
        for h in range(CHUNKS):
            for d in range(PEERS):
                send2[slot2, h, d, :PART] = turn_a[part_rows(d, h), :].astype(BF16)
                send2[slot2, h, d, PART:] = turn_b[part_rows(d, h), :].astype(BF16)
            send2_part(slot2, phase_out, h)

    def finish(l, p, product):
        at = lanes(p)
        mix_unit_p, mix_inverse_p = norm_forward(product)
        mixed_p = (mix_unit_p * gains[2 * l + 1]).astype(BF16)
        mix_unit[l, :, at] = mix_unit_p
        mix_inverse[l, :, at] = mix_inverse_p
        mixed[l, :, at] = mixed_p
        output_p = nn(out_t[l], mixed_p)
        output[l, :, at] = output_p
        return output_p

    def fold(values):
        return values[:, :N] + values[:, N:]

    def back_head(l, p, gradient, ref):
        at = lanes(p)
        gate_p = gate[l, :, at]
        go_p = (gradient * gate_p).astype(BF16)
        go[l, :, at] = go_p
        gp[l, 4 * N :, at] = (gradient * output[l, :, at] * gate_p * (1.0 - gate_p)).astype(BF16)
        grad_mixed = nn(out_weight[l], go_p)
        mix_unit_p = mix_unit[l, :, at]
        mid_acc[l] += fold(grad_mixed * mix_unit_p)
        grad_product = norm_backward(grad_mixed * gains[2 * l + 1], mix_unit_p, mix_inverse[l, :, at])
        put_rows(ref, 2 * ROWS * (p % PER), grad_product)

    def back_pieces(l, p, ref):
        at = lanes(p)
        row = 2 * ROWS * (p % PER)
        sig = sig_l[l, :, at]
        plain = get_rows(ref, row) * sig
        gp[l, 0:N, at] = (plain * val_l[l, :, at] * (1.0 - sig)).astype(BF16)
        gp[l, N : 2 * N, at] = plain.astype(BF16)
        sig = sig_r[l, :, at]
        plain = get_rows(ref, PART + row) * sig
        gp[l, 2 * N : 3 * N, at] = (plain * val_r[l, :, at] * (1.0 - sig)).astype(BF16)
        gp[l, 3 * N : 4 * N, at] = plain.astype(BF16)

    def back_tail(l, p, gradient):
        at = lanes(p)
        grad_normed = nn(weight[l], gp[l, :, at])
        unit_p = unit[l, :, at]
        in_acc[l] += fold(grad_normed * unit_p)
        return gradient + norm_backward(grad_normed * gains[2 * l], unit_p, inverse[l, :, at])

    loads[0].wait()
    for a in range(ROWS):
        state0[:, a * N : (a + 1) * N] = pair_in[a].astype(F32).T
    for load in loads[1:4]:
        load.wait()

    def set_gain(index, source, l):
        row = jnp.broadcast_to(source[l : l + 1, :], (N, N)).T
        gains[index] = jnp.concatenate([row, row], axis=1)

    def set_weights(l):
        set_gain(2 * l, in_gain, l)
        for f in range(4):
            block = proj_weight[l, :, f * N : (f + 1) * N]
            weight[l, :, f * N : (f + 1) * N] = block
            weight_t[l, f * N : (f + 1) * N, :] = block.astype(F32).T.astype(BF16)
        weight[l, :, 4 * N :] = gate_weight[l]
        weight_t[l, 4 * N :, :] = gate_weight[l].astype(F32).T.astype(BF16)

    set_weights(0)
    for h in range(CHUNKS):
        for p in steps(h):
            project(0, p, state0[:, lanes(p)], send2.at[0, h])
        if h == 0:
            pl.semaphore_wait(barrier, PEERS - 1)
        send2_part(0, TO_CH_0, h)

    for load in loads[4:]:
        load.wait()
    set_weights(1)
    for l in range(2):
        set_gain(2 * l + 1, mid_gain, l)
        out_t[l] = out_weight[l].astype(F32).T.astype(BF16)
    for a in range(ROWS):
        cot[:, a * N : (a + 1) * N] = cotangent[a].astype(F32).T

    channel_forward(0, 0, 0, TO_CH_0, TO_ROW_0)

    for h in range(CHUNKS):
        wait1_part(0, TO_ROW_0, h)
        for p in steps(h):
            at = lanes(p)
            output_p = finish(0, p, get_rows(recv1.at[0, h], 2 * ROWS * (p % PER)))
            state = (state0[:, at] + gate[0, :, at] * output_p).astype(BF16).astype(F32)
            state1[:, at] = state
            project(1, p, state, send2.at[1, h])
        send2_part(1, TO_CH_1, h)

    channel_forward(1, 1, 1, TO_CH_1, TO_ROW_1)

    for h in range(CHUNKS):
        wait1_part(1, TO_ROW_1, h)
        for p in steps(h):
            finish(1, p, get_rows(recv1.at[1, h], 2 * ROWS * (p % PER)))
            back_head(1, p, cot[:, lanes(p)], send1.at[2, h])
        send1_part(2, GRAD_CH_1, h)

    channel_backward(1, 2, 2, GRAD_CH_1, GRAD_ROW_1)

    for h in range(CHUNKS):
        wait2_part(2, GRAD_ROW_1, h)
        for p in steps(h):
            at = lanes(p)
            back_pieces(1, p, recv2.at[2, h])
            gradient = back_tail(1, p, cot[:, at])
            grad1[:, at] = gradient
            back_head(0, p, gradient, send1.at[3, h])
        send1_part(3, GRAD_CH_0, h)

    def put_early(first, values):
        for i in range(N // 64):
            sum_early_send[first + i] = values[64 * i : 64 * i + 64, :].astype(BF16)

    for f in range(5):
        put_early(2 * f, nt(normed[1], gp[1, f * N : (f + 1) * N, :]))
    put_early(10, nt(mixed[1], go[1]))
    put_early(12, nt(normed[0], gp[0, 4 * N :, :]))
    put_early(14, nt(mixed[0], go[0]))
    send_part(SUM_EARLY, 0, lambda d: sum_early_send.at[d], sum_early_recv.at[me])
    sum_early_recv[me] = sum_early_send[me]

    channel_backward(0, 3, 3, GRAD_CH_0, GRAD_ROW_0)

    wait_part(SUM_EARLY, 0, sum_early_recv)
    all_early[me] = jnp.sum(sum_early_recv[...].astype(F32), axis=0).astype(BF16)
    send_part(ALL_EARLY, 0, lambda d: all_early.at[me], all_early.at[me])

    def last_rows(p):
        gradient = back_tail(0, p, grad1[:, lanes(p)])
        for i in range(2):
            pair_grad[2 * p + i] = gradient[:, i * N : (i + 1) * N].T.astype(BF16)

    for h in range(CHUNKS):
        wait2_part(3, GRAD_ROW_0, h)
        for p in steps(h):
            back_pieces(0, p, recv2.at[3, h])
        if h < CHUNKS - 1:
            for p in steps(h):
                last_rows(p)

    for f in range(4):
        values = nt(normed[0], gp[0, f * N : (f + 1) * N, :])
        for i in range(4):
            sum_late_send[4 * f + i] = values[32 * i : 32 * i + 32, :].astype(BF16)
    send_part(SUM_LATE, 0, lambda d: sum_late_send.at[d], sum_late_recv.at[me])
    sum_late_recv[me] = sum_late_send[me]

    for p in steps(CHUNKS - 1):
        last_rows(p)

    gain_rows = [jnp.sum(ref[l].T, axis=0, keepdims=True) for ref in (in_acc, mid_acc) for l in range(2)]
    gains_all[me] = jnp.concatenate(gain_rows + [jnp.zeros((4, N), F32)], axis=0)
    send_part(GAINS, 0, lambda d: gains_all.at[me], gains_all.at[me])

    wait_part(SUM_LATE, 0, sum_late_recv)
    all_late[me] = jnp.sum(sum_late_recv[...].astype(F32), axis=0).astype(BF16)
    send_part(ALL_LATE, 0, lambda d: all_late.at[me], all_late.at[me])

    wait_part(ALL_EARLY, 0, all_early)
    early_out[...] = all_early[...]
    for h in range(CHUNKS):
        for slot, two, one in ((0, TO_CH_0, TO_ROW_0), (1, TO_CH_1, TO_ROW_1), (2, GRAD_ROW_1, GRAD_CH_1), (3, GRAD_ROW_0, GRAD_CH_0)):
            wait_sent(two, h, send2.at[slot, h])
            wait_sent(one, h, send1.at[slot, h])
    wait_sent(SUM_EARLY, 0, sum_early_send)
    wait_sent(ALL_EARLY, 0, all_early)
    wait_sent(SUM_LATE, 0, sum_late_send)
    wait_sent(GAINS, 0, gains_all)

    wait_part(GAINS, 0, gains_all)
    gains_out[...] = jnp.sum(gains_all[...], axis=0)

    wait_part(ALL_LATE, 0, all_late)
    late_out[...] = all_late[...]
    wait_sent(ALL_LATE, 0, all_late)


def write_kernel(
    pair, early_in, late_in, gains_in,
    pair_grad, proj_grad, gate_grad, out_grad, in_gain_grad, mid_gain_grad,
):
    scale = 1.0 / N
    pair_grad[...] = pair[...]

    def early(first):
        return early_in[first : first + 2].astype(F32).reshape(N, N) * scale

    for f in range(4):
        proj_grad[0, :, f * N : (f + 1) * N] = late_in[4 * f : 4 * f + 4].astype(F32).reshape(N, N) * scale
        proj_grad[1, :, f * N : (f + 1) * N] = early(2 * f)
    gate_grad[1] = early(8)
    out_grad[1] = early(10)
    gate_grad[0] = early(12)
    out_grad[0] = early(14)
    in_gain_grad[...] = gains_in[0:2, :] * scale
    mid_gain_grad[...] = gains_in[2:4, :] * scale


def on_device(*arrays):
    layer_f32 = pltpu.VMEM((2, N, CELLS), F32)
    layer_bf16 = pltpu.VMEM((2, N, CELLS), BF16)
    plain_f32 = pltpu.VMEM((N, CELLS), F32)
    vmem = pl.BlockSpec(memory_space=pltpu.VMEM)
    results = pl.pallas_call(
        kernel,
        out_shape=(
            jax.ShapeDtypeStruct((ROWS, N, N), BF16),
            jax.ShapeDtypeStruct((PEERS, 64, N), BF16),
            jax.ShapeDtypeStruct((PEERS, 32, N), BF16),
            jax.ShapeDtypeStruct((8, N), F32),
        ),
        in_specs=[pl.BlockSpec(memory_space=pl.ANY)] * 7,
        out_specs=[vmem] * 4,
        scratch_shapes=[pltpu.VMEM(array.shape, array.dtype) for array in arrays] + [
            pltpu.VMEM((4, N, WIDE), F32),
            pltpu.VMEM((2, N, 5 * N), BF16),
            pltpu.VMEM((2, 5 * N, N), BF16),
            pltpu.VMEM((2, N, N), BF16),
            plain_f32, plain_f32, plain_f32, plain_f32,
            layer_f32,
            pltpu.VMEM((2, 1, CELLS), F32),
            layer_bf16,
            layer_f32, layer_f32, layer_f32, layer_f32,
            layer_f32, layer_f32, layer_f32,
            pltpu.VMEM((2, 1, CELLS), F32),
            layer_bf16,
            layer_bf16,
            pltpu.VMEM((2, 5 * N, CELLS), BF16),
            pltpu.VMEM((2, N, N), F32),
            pltpu.VMEM((2, N, N), F32),
            pltpu.VMEM((CELLS, N), F32),
            pltpu.VMEM((CELLS, N), F32),
            pltpu.VMEM((2, ROWS, N, N), BF16),
            pltpu.VMEM((2, ROWS, N, N), BF16),
            pltpu.VMEM((4, CHUNKS, PEERS, 2 * PART, N), BF16),
            pltpu.VMEM((4, CHUNKS, PEERS, 2 * PART, N), BF16),
            pltpu.VMEM((4, CHUNKS, PEERS, PART, N), BF16),
            pltpu.VMEM((4, CHUNKS, PEERS, PART, N), BF16),
            pltpu.VMEM((PEERS, 64, N), BF16),
            pltpu.VMEM((PEERS, 64, N), BF16),
            pltpu.VMEM((PEERS, 64, N), BF16),
            pltpu.VMEM((PEERS, 32, N), BF16),
            pltpu.VMEM((PEERS, 32, N), BF16),
            pltpu.VMEM((PEERS, 32, N), BF16),
            pltpu.VMEM((PEERS, 8, N), F32),
            pltpu.SemaphoreType.DMA((7,)),
            pltpu.SemaphoreType.DMA((PHASES * CHUNKS,)),
            pltpu.SemaphoreType.DMA((PHASES * CHUNKS,)),
        ],
        compiler_params=pltpu.CompilerParams(
            collective_id=0, has_side_effects=True, vmem_limit_bytes=56 * 1024 * 1024
        ),
    )(*arrays)
    return pl.pallas_call(
        write_kernel,
        out_shape=(
            jax.ShapeDtypeStruct((ROWS, N, N), BF16),
            jax.ShapeDtypeStruct((2, N, 4 * N), F32),
            jax.ShapeDtypeStruct((2, N, N), F32),
            jax.ShapeDtypeStruct((2, N, N), F32),
            jax.ShapeDtypeStruct((2, N), F32),
            jax.ShapeDtypeStruct((2, N), F32),
        ),
        in_specs=[vmem] * 4,
        out_specs=[vmem] * 6,
    )(*results)


def solution(mesh):
    return jax.shard_map(
        on_device,
        mesh=mesh,
        in_specs=(
            P(("dp", "pair"), None, None),
            P(("dp", "pair"), None, None),
            P(),
            P(),
            P(),
            P(),
            P(),
        ),
        out_specs=(
            P(("dp", "pair"), None, None),
            P("dp", None, None),
            P("dp", None, None),
            P("dp", None, None),
            P("dp", None),
            P("dp", None),
        ),
        check_vma=False,
    )
```

```python
import functools

import jax
import jax.numpy as jnp
from jax import lax
from jax.experimental import pallas as pl
from jax.experimental.pallas import tpu as pltpu
from jax.sharding import PartitionSpec as P

EPSILON = 1e-05
MESH = pl.DeviceIdType.MESH
F32 = jnp.float32
BF16 = jnp.bfloat16

N = 128
PEERS = 16
ROWS = N // PEERS
CELLS = ROWS * N
WIDE = 2 * N
STEPS = CELLS // WIDE
CHUNKS = 2
PER = STEPS // CHUNKS
PART = ROWS * ROWS // CHUNKS

TO_CH_0, TO_ROW_0, TO_CH_1, TO_ROW_1, GRAD_CH_1, GRAD_ROW_1, GRAD_CH_0, GRAD_ROW_0 = range(8)
SUM_EARLY, ALL_EARLY, SUM_LATE, ALL_LATE, GAINS = range(8, 13)
PHASES = 13


def dot(first, second, dims):
    return lax.dot_general(first, second, (dims, ((), ())), preferred_element_type=F32)


def nn(first, second):
    return dot(first, second, ((1,), (0,)))


def nt(first, second):
    return dot(first, second, ((1,), (1,)))


def tn(first, second):
    return dot(first, second, ((0,), (0,)))


def sigmoid(values):
    return 0.5 * jnp.tanh(0.5 * values) + 0.5


def mean_channels(values):
    return jnp.sum(values, axis=0, keepdims=True) * (1.0 / N)


def norm_forward(values):
    shifted = values - mean_channels(values)
    inverse = lax.rsqrt(mean_channels(shifted * shifted) + EPSILON)
    return shifted * inverse, inverse


def norm_backward(scaled, unit, inverse):
    return inverse * (scaled - mean_channels(scaled) - unit * mean_channels(scaled * unit))


def kernel(
    pair_hbm, cot_hbm, in_gain_hbm, proj_weight_hbm, gate_weight_hbm, mid_gain_hbm, out_weight_hbm,
    pair_grad, early_out, late_out, gains_out,
    pair_in, cotangent, in_gain, proj_weight, gate_weight, mid_gain, out_weight,
    gains, weight, weight_t, out_t,
    state0, state1, cot, grad1,
    unit, inverse, normed, sig_l, val_l, sig_r, val_r, gate, output, mix_unit, mix_inverse, mixed,
    go, gp, in_acc, mid_acc,
    turn_a, turn_b, chan_l, chan_r,
    send2, recv2, send1, recv1,
    sum_early_send, sum_early_recv, all_early, sum_late_send, sum_late_recv, all_late, gains_all,
    load_sem, send_sem, recv_sem,
):
    me = lax.axis_index("pair")
    my_x, my_y, my_core = me // 8, (me // 2) % 4, me % 2

    def peer(o):
        x = (my_x + o // 8) % 2
        y = (my_y + (o // 2) % 4) % 4
        core = (my_core + o % 2) % 2
        return x * 8 + y * 2 + core

    barrier = pltpu.get_barrier_semaphore()

    peers = [peer(o) for o in (12, 4, 13, 5, 10, 2, 14, 6, 11, 3, 15, 7, 8, 9, 1)]
    for target in peers:
        pl.semaphore_signal(barrier, inc=1, device_id={"pair": target}, device_id_type=MESH)

    loads = [
        pltpu.make_async_copy(source, target, load_sem.at[i])
        for i, (source, target) in enumerate((
            (pair_hbm, pair_in), (in_gain_hbm, in_gain), (proj_weight_hbm, proj_weight), (gate_weight_hbm, gate_weight),
            (mid_gain_hbm, mid_gain), (out_weight_hbm, out_weight), (cot_hbm, cotangent),
        ))
    ]
    for load in loads:
        load.start()

    def send_part(phase, h, src_of, dst):
        sem = phase * CHUNKS + h
        for target in peers:
            pltpu.make_async_remote_copy(
                src_ref=src_of(target), dst_ref=dst,
                send_sem=send_sem.at[sem], recv_sem=recv_sem.at[sem],
                device_id={"pair": target}, device_id_type=MESH,
            ).start()

    def wait_part(phase, h, slots):
        fifteen = slots.at[pl.ds(0, PEERS - 1)]
        pltpu.make_async_copy(fifteen, fifteen, recv_sem.at[phase * CHUNKS + h]).wait()

    def wait_sent(phase, h, slots):
        fifteen = slots.at[pl.ds(0, PEERS - 1)]
        pltpu.make_async_copy(fifteen, fifteen, send_sem.at[phase * CHUNKS + h]).wait()

    in_acc[...] = jnp.zeros_like(in_acc)
    mid_acc[...] = jnp.zeros_like(mid_acc)

    def lanes(p):
        return slice(p * WIDE, (p + 1) * WIDE)

    def put_rows(ref, first, values):
        parts = [values[:, i * N : (i + 1) * N].reshape(PEERS, ROWS, N) for i in range(2)]
        ref[:, first : first + 2 * ROWS, :] = jnp.concatenate(parts, axis=1).astype(BF16)

    def get_rows(ref, first):
        block = ref[:, first : first + 2 * ROWS, :].astype(F32)
        return jnp.concatenate([block[:, i * ROWS : (i + 1) * ROWS].reshape(N, N) for i in range(2)], axis=1)

    def project(l, p, state, ref):
        at = lanes(p)
        unit_p, inverse_p = norm_forward(state)
        normed_p = (unit_p * gains[2 * l]).astype(BF16)
        unit[l, :, at] = unit_p
        inverse[l, :, at] = inverse_p
        normed[l, :, at] = normed_p
        projected = nn(weight_t[l], normed_p)
        row = 2 * ROWS * (p % PER)
        sig = sigmoid(projected[0:N])
        val = projected[N : 2 * N]
        sig_l[l, :, at] = sig
        val_l[l, :, at] = val
        put_rows(ref, row, sig * val)
        sig = sigmoid(projected[2 * N : 3 * N])
        val = projected[3 * N : 4 * N]
        sig_r[l, :, at] = sig
        val_r[l, :, at] = val
        put_rows(ref, PART + row, sig * val)
        gate[l, :, at] = sigmoid(projected[4 * N :])

    def steps(h):
        return range(h * PER, (h + 1) * PER)

    def send2_part(slot, phase, h):
        send_part(phase, h, lambda d: send2.at[slot, h, d], recv2.at[slot, h, me])
        recv2[slot, h, me] = send2[slot, h, me]

    def send1_part(slot, phase, h):
        send_part(phase, h, lambda d: send1.at[slot, h, d], recv1.at[slot, h, me])
        recv1[slot, h, me] = send1[slot, h, me]

    def wait2_part(slot, phase, h):
        wait_part(phase, h, recv2.at[slot, h])

    def wait1_part(slot, phase, h):
        wait_part(phase, h, recv1.at[slot, h])

    def part_rows(d, h):
        return slice(d * ROWS * ROWS + h * PART, d * ROWS * ROWS + (h + 1) * PART)

    def channel(c):
        return pl.ds(c, N, stride=ROWS)

    def channel_forward(l, slot2, slot1, phase_in, phase_out):
        for h in range(CHUNKS):
            wait2_part(slot2, phase_in, h)
            for s in range(PEERS):
                turn_a[part_rows(s, h), :] = recv2[slot2, h, s, :PART].astype(F32)
                turn_b[part_rows(s, h), :] = recv2[slot2, h, s, PART:].astype(F32)
        for c in range(ROWS):
            left = turn_a[channel(c), :].astype(BF16)
            right = turn_b[channel(c), :].astype(BF16)
            chan_l[l, c] = left
            chan_r[l, c] = right
            turn_a[channel(c), :] = nt(left, right) if l == 0 else tn(left, right)
        for h in range(CHUNKS):
            for d in range(PEERS):
                send1[slot1, h, d] = turn_a[part_rows(d, h), :].astype(BF16)
            send1_part(slot1, phase_out, h)

    def channel_backward(l, slot1, slot2, phase_in, phase_out):
        for h in range(CHUNKS):
            wait1_part(slot1, phase_in, h)
            for s in range(PEERS):
                turn_a[part_rows(s, h), :] = recv1[slot1, h, s].astype(F32)
        for c in range(ROWS):
            grad = turn_a[channel(c), :].astype(BF16)
            left, right = chan_l[l, c], chan_r[l, c]
            turn_a[channel(c), :] = nn(grad, right) if l == 0 else nt(right, grad)
            turn_b[channel(c), :] = tn(grad, left) if l == 0 else nn(left, grad)
        for h in range(CHUNKS):
            for d in range(PEERS):
                send2[slot2, h, d, :PART] = turn_a[part_rows(d, h), :].astype(BF16)
                send2[slot2, h, d, PART:] = turn_b[part_rows(d, h), :].astype(BF16)
            send2_part(slot2, phase_out, h)

    def finish(l, p, product):
        at = lanes(p)
        mix_unit_p, mix_inverse_p = norm_forward(product)
        mixed_p = (mix_unit_p * gains[2 * l + 1]).astype(BF16)
        mix_unit[l, :, at] = mix_unit_p
        mix_inverse[l, :, at] = mix_inverse_p
        mixed[l, :, at] = mixed_p
        output_p = nn(out_t[l], mixed_p)
        output[l, :, at] = output_p
        return output_p

    def fold(values):
        return values[:, :N] + values[:, N:]

    def back_head(l, p, gradient, ref):
        at = lanes(p)
        gate_p = gate[l, :, at]
        go_p = (gradient * gate_p).astype(BF16)
        go[l, :, at] = go_p
        gp[l, 4 * N :, at] = (gradient * output[l, :, at] * gate_p * (1.0 - gate_p)).astype(BF16)
        grad_mixed = nn(out_weight[l], go_p)
        mix_unit_p = mix_unit[l, :, at]
        mid_acc[l] += fold(grad_mixed * mix_unit_p)
        grad_product = norm_backward(grad_mixed * gains[2 * l + 1], mix_unit_p, mix_inverse[l, :, at])
        put_rows(ref, 2 * ROWS * (p % PER), grad_product)

    def back_pieces(l, p, ref):
        at = lanes(p)
        row = 2 * ROWS * (p % PER)
        sig = sig_l[l, :, at]
        plain = get_rows(ref, row) * sig
        gp[l, 0:N, at] = (plain * val_l[l, :, at] * (1.0 - sig)).astype(BF16)
        gp[l, N : 2 * N, at] = plain.astype(BF16)
        sig = sig_r[l, :, at]
        plain = get_rows(ref, PART + row) * sig
        gp[l, 2 * N : 3 * N, at] = (plain * val_r[l, :, at] * (1.0 - sig)).astype(BF16)
        gp[l, 3 * N : 4 * N, at] = plain.astype(BF16)

    def back_tail(l, p, gradient):
        at = lanes(p)
        grad_normed = nn(weight[l], gp[l, :, at])
        unit_p = unit[l, :, at]
        in_acc[l] += fold(grad_normed * unit_p)
        return gradient + norm_backward(grad_normed * gains[2 * l], unit_p, inverse[l, :, at])

    loads[0].wait()
    for a in range(ROWS):
        state0[:, a * N : (a + 1) * N] = pair_in[a].astype(F32).T
    for load in loads[1:4]:
        load.wait()

    def set_gain(index, source, l):
        row = jnp.broadcast_to(source[l : l + 1, :], (N, N)).T
        gains[index] = jnp.concatenate([row, row], axis=1)

    def set_weights(l):
        set_gain(2 * l, in_gain, l)
        for f in range(4):
            block = proj_weight[l, :, f * N : (f + 1) * N]
            weight[l, :, f * N : (f + 1) * N] = block
            weight_t[l, f * N : (f + 1) * N, :] = block.astype(F32).T.astype(BF16)
        weight[l, :, 4 * N :] = gate_weight[l]
        weight_t[l, 4 * N :, :] = gate_weight[l].astype(F32).T.astype(BF16)

    set_weights(0)
    for h in range(CHUNKS):
        for p in steps(h):
            project(0, p, state0[:, lanes(p)], send2.at[0, h])
        if h == 0:
            pl.semaphore_wait(barrier, PEERS - 1)
        send2_part(0, TO_CH_0, h)

    for load in loads[4:]:
        load.wait()
    set_weights(1)
    for l in range(2):
        set_gain(2 * l + 1, mid_gain, l)
        out_t[l] = out_weight[l].astype(F32).T.astype(BF16)
    for a in range(ROWS):
        cot[:, a * N : (a + 1) * N] = cotangent[a].astype(F32).T

    channel_forward(0, 0, 0, TO_CH_0, TO_ROW_0)

    for h in range(CHUNKS):
        wait1_part(0, TO_ROW_0, h)
        for p in steps(h):
            at = lanes(p)
            output_p = finish(0, p, get_rows(recv1.at[0, h], 2 * ROWS * (p % PER)))
            state = (state0[:, at] + gate[0, :, at] * output_p).astype(BF16).astype(F32)
            state1[:, at] = state
            project(1, p, state, send2.at[1, h])
        send2_part(1, TO_CH_1, h)

    channel_forward(1, 1, 1, TO_CH_1, TO_ROW_1)

    for h in range(CHUNKS):
        wait1_part(1, TO_ROW_1, h)
        for p in steps(h):
            finish(1, p, get_rows(recv1.at[1, h], 2 * ROWS * (p % PER)))
            back_head(1, p, cot[:, lanes(p)], send1.at[2, h])
        send1_part(2, GRAD_CH_1, h)

    channel_backward(1, 2, 2, GRAD_CH_1, GRAD_ROW_1)

    for h in range(CHUNKS):
        wait2_part(2, GRAD_ROW_1, h)
        for p in steps(h):
            at = lanes(p)
            back_pieces(1, p, recv2.at[2, h])
            gradient = back_tail(1, p, cot[:, at])
            grad1[:, at] = gradient
            back_head(0, p, gradient, send1.at[3, h])
        send1_part(3, GRAD_CH_0, h)

    def put_early(first, values):
        for i in range(N // 64):
            sum_early_send[first + i] = values[64 * i : 64 * i + 64, :].astype(BF16)

    for f in range(5):
        put_early(2 * f, nt(normed[1], gp[1, f * N : (f + 1) * N, :]))
    put_early(10, nt(mixed[1], go[1]))
    put_early(12, nt(normed[0], gp[0, 4 * N :, :]))
    put_early(14, nt(mixed[0], go[0]))
    send_part(SUM_EARLY, 0, lambda d: sum_early_send.at[d], sum_early_recv.at[me])
    sum_early_recv[me] = sum_early_send[me]

    channel_backward(0, 3, 3, GRAD_CH_0, GRAD_ROW_0)

    wait_part(SUM_EARLY, 0, sum_early_recv)
    all_early[me] = jnp.sum(sum_early_recv[...].astype(F32), axis=0).astype(BF16)
    send_part(ALL_EARLY, 0, lambda d: all_early.at[me], all_early.at[me])

    def last_rows(p):
        gradient = back_tail(0, p, grad1[:, lanes(p)])
        for i in range(2):
            pair_grad[2 * p + i] = gradient[:, i * N : (i + 1) * N].T.astype(BF16)

    for h in range(CHUNKS):
        wait2_part(3, GRAD_ROW_0, h)
        for p in steps(h):
            back_pieces(0, p, recv2.at[3, h])
        if h < CHUNKS - 1:
            for p in steps(h):
                last_rows(p)

    for f in range(4):
        values = nt(normed[0], gp[0, f * N : (f + 1) * N, :])
        for i in range(4):
            sum_late_send[4 * f + i] = values[32 * i : 32 * i + 32, :].astype(BF16)
    send_part(SUM_LATE, 0, lambda d: sum_late_send.at[d], sum_late_recv.at[me])
    sum_late_recv[me] = sum_late_send[me]

    for p in steps(CHUNKS - 1):
        last_rows(p)

    gain_rows = [jnp.sum(ref[l].T, axis=0, keepdims=True) for ref in (in_acc, mid_acc) for l in range(2)]
    gains_all[me] = jnp.concatenate(gain_rows + [jnp.zeros((4, N), F32)], axis=0)
    send_part(GAINS, 0, lambda d: gains_all.at[me], gains_all.at[me])

    wait_part(SUM_LATE, 0, sum_late_recv)
    all_late[me] = jnp.sum(sum_late_recv[...].astype(F32), axis=0).astype(BF16)
    send_part(ALL_LATE, 0, lambda d: all_late.at[me], all_late.at[me])

    wait_part(ALL_EARLY, 0, all_early)
    early_out[...] = all_early[...]
    for h in range(CHUNKS):
        for slot, two, one in ((0, TO_CH_0, TO_ROW_0), (1, TO_CH_1, TO_ROW_1), (2, GRAD_ROW_1, GRAD_CH_1), (3, GRAD_ROW_0, GRAD_CH_0)):
            wait_sent(two, h, send2.at[slot, h])
            wait_sent(one, h, send1.at[slot, h])
    wait_sent(SUM_EARLY, 0, sum_early_send)
    wait_sent(ALL_EARLY, 0, all_early)
    wait_sent(SUM_LATE, 0, sum_late_send)
    wait_sent(GAINS, 0, gains_all)

    wait_part(GAINS, 0, gains_all)
    gains_out[...] = jnp.sum(gains_all[...], axis=0)

    wait_part(ALL_LATE, 0, all_late)
    late_out[...] = all_late[...]
    wait_sent(ALL_LATE, 0, all_late)


def write_kernel(
    pair, early_in, late_in, gains_in,
    pair_grad, proj_grad, gate_grad, out_grad, in_gain_grad, mid_gain_grad,
):
    scale = 1.0 / N
    pair_grad[...] = pair[...]

    def early(first):
        return early_in[first : first + 2].astype(F32).reshape(N, N) * scale

    for f in range(4):
        proj_grad[0, :, f * N : (f + 1) * N] = late_in[4 * f : 4 * f + 4].astype(F32).reshape(N, N) * scale
        proj_grad[1, :, f * N : (f + 1) * N] = early(2 * f)
    gate_grad[1] = early(8)
    out_grad[1] = early(10)
    gate_grad[0] = early(12)
    out_grad[0] = early(14)
    in_gain_grad[...] = gains_in[0:2, :] * scale
    mid_gain_grad[...] = gains_in[2:4, :] * scale


def on_device(*arrays):
    layer_f32 = pltpu.VMEM((2, N, CELLS), F32)
    layer_bf16 = pltpu.VMEM((2, N, CELLS), BF16)
    plain_f32 = pltpu.VMEM((N, CELLS), F32)
    vmem = pl.BlockSpec(memory_space=pltpu.VMEM)
    results = pl.pallas_call(
        kernel,
        out_shape=(
            pltpu.VMEM((ROWS, N, N), BF16),
            pltpu.VMEM((PEERS, 64, N), BF16),
            pltpu.VMEM((PEERS, 32, N), BF16),
            pltpu.VMEM((8, N), F32),
        ),
        in_specs=[pl.BlockSpec(memory_space=pl.ANY)] * 7,
        out_specs=[vmem] * 4,
        scratch_shapes=[pltpu.VMEM(array.shape, array.dtype) for array in arrays] + [
            pltpu.VMEM((4, N, WIDE), F32),
            pltpu.VMEM((2, N, 5 * N), BF16),
            pltpu.VMEM((2, 5 * N, N), BF16),
            pltpu.VMEM((2, N, N), BF16),
            plain_f32, plain_f32, plain_f32, plain_f32,
            layer_f32,
            pltpu.VMEM((2, 1, CELLS), F32),
            layer_bf16,
            layer_f32, layer_f32, layer_f32, layer_f32,
            layer_f32, layer_f32, layer_f32,
            pltpu.VMEM((2, 1, CELLS), F32),
            layer_bf16,
            layer_bf16,
            pltpu.VMEM((2, 5 * N, CELLS), BF16),
            pltpu.VMEM((2, N, N), F32),
            pltpu.VMEM((2, N, N), F32),
            pltpu.VMEM((CELLS, N), F32),
            pltpu.VMEM((CELLS, N), F32),
            pltpu.VMEM((2, ROWS, N, N), BF16),
            pltpu.VMEM((2, ROWS, N, N), BF16),
            pltpu.VMEM((4, CHUNKS, PEERS, 2 * PART, N), BF16),
            pltpu.VMEM((4, CHUNKS, PEERS, 2 * PART, N), BF16),
            pltpu.VMEM((4, CHUNKS, PEERS, PART, N), BF16),
            pltpu.VMEM((4, CHUNKS, PEERS, PART, N), BF16),
            pltpu.VMEM((PEERS, 64, N), BF16),
            pltpu.VMEM((PEERS, 64, N), BF16),
            pltpu.VMEM((PEERS, 64, N), BF16),
            pltpu.VMEM((PEERS, 32, N), BF16),
            pltpu.VMEM((PEERS, 32, N), BF16),
            pltpu.VMEM((PEERS, 32, N), BF16),
            pltpu.VMEM((PEERS, 8, N), F32),
            pltpu.SemaphoreType.DMA((7,)),
            pltpu.SemaphoreType.DMA((PHASES * CHUNKS,)),
            pltpu.SemaphoreType.DMA((PHASES * CHUNKS,)),
        ],
        compiler_params=pltpu.CompilerParams(
            collective_id=0, has_side_effects=True, vmem_limit_bytes=56 * 1024 * 1024
        ),
    )(*arrays)
    return pl.pallas_call(
        write_kernel,
        out_shape=(
            jax.ShapeDtypeStruct((ROWS, N, N), BF16),
            jax.ShapeDtypeStruct((2, N, 4 * N), F32),
            jax.ShapeDtypeStruct((2, N, N), F32),
            jax.ShapeDtypeStruct((2, N, N), F32),
            jax.ShapeDtypeStruct((2, N), F32),
            jax.ShapeDtypeStruct((2, N), F32),
        ),
        in_specs=[vmem] * 4,
        out_specs=[vmem] * 6,
        compiler_params=pltpu.CompilerParams(vmem_limit_bytes=4 * 1024 * 1024),
    )(*results)


def solution(mesh):
    return jax.shard_map(
        on_device,
        mesh=mesh,
        in_specs=(
            P(("dp", "pair"), None, None),
            P(("dp", "pair"), None, None),
            P(),
            P(),
            P(),
            P(),
            P(),
        ),
        out_specs=(
            P(("dp", "pair"), None, None),
            P("dp", None, None),
            P("dp", None, None),
            P("dp", None, None),
            P("dp", None),
            P("dp", None),
        ),
        check_vma=False,
    )
```

```python
import functools

import jax
import jax.numpy as jnp
from jax import lax
from jax.experimental import pallas as pl
from jax.experimental.pallas import tpu as pltpu
from jax.sharding import PartitionSpec as P

EPSILON = 1e-05
MESH = pl.DeviceIdType.MESH
F32 = jnp.float32
BF16 = jnp.bfloat16

N = 128
PEERS = 16
ROWS = N // PEERS
CELLS = ROWS * N
WIDE = 2 * N
STEPS = CELLS // WIDE
CHUNKS = 2
PER = STEPS // CHUNKS
PART = ROWS * ROWS // CHUNKS

TO_CH_0, TO_ROW_0, TO_CH_1, TO_ROW_1, GRAD_CH_1, GRAD_ROW_1, GRAD_CH_0, GRAD_ROW_0 = range(8)
SUM_EARLY, ALL_EARLY, SUM_LATE, ALL_LATE, GAINS = range(8, 13)
PHASES = 13


def dot(first, second, dims):
    return lax.dot_general(first, second, (dims, ((), ())), preferred_element_type=F32)


def nn(first, second):
    return dot(first, second, ((1,), (0,)))


def nt(first, second):
    return dot(first, second, ((1,), (1,)))


def tn(first, second):
    return dot(first, second, ((0,), (0,)))


def sigmoid(values):
    return 0.5 * jnp.tanh(0.5 * values) + 0.5


def mean_channels(values):
    return jnp.sum(values, axis=0, keepdims=True) * (1.0 / N)


def norm_forward(values):
    shifted = values - mean_channels(values)
    inverse = lax.rsqrt(mean_channels(shifted * shifted) + EPSILON)
    return shifted * inverse, inverse


def norm_backward(scaled, unit, inverse):
    return inverse * (scaled - mean_channels(scaled) - unit * mean_channels(scaled * unit))


def kernel(
    pair_hbm, cot_hbm, in_gain_hbm, proj_weight_hbm, gate_weight_hbm, mid_gain_hbm, out_weight_hbm,
    pair_grad, early_out, late_out, gains_out,
    pair_in, cotangent, in_gain, proj_weight, gate_weight, mid_gain, out_weight,
    gains, weight, weight_t, out_t,
    state0, cot, grad1,
    unit, inverse, normed, sig_l, val_l, sig_r, val_r, gate, gate_der, output, mix_unit, mix_inverse, mixed,
    grad_mixed, scaled, scaled_mean, grad_normed,
    go, gp, in_acc, mid_acc,
    turn_a, turn_b, chan_l, chan_r,
    send2, recv2, send1, recv1,
    sum_early_send, sum_early_recv, all_early, sum_late_send, sum_late_recv, all_late, gains_all,
    load_sem, send_sem, recv_sem,
):
    me = lax.axis_index("pair")
    my_x, my_y, my_core = me // 8, (me // 2) % 4, me % 2

    def peer(o):
        x = (my_x + o // 8) % 2
        y = (my_y + (o // 2) % 4) % 4
        core = (my_core + o % 2) % 2
        return x * 8 + y * 2 + core

    barrier = pltpu.get_barrier_semaphore()

    peers = [peer(o) for o in (4, 12, 5, 13, 2, 10, 6, 14, 3, 11, 7, 15, 8, 9, 1)]
    for target in peers:
        pl.semaphore_signal(barrier, inc=1, device_id={"pair": target}, device_id_type=MESH)

    loads = [
        pltpu.make_async_copy(source, target, load_sem.at[i])
        for i, (source, target) in enumerate((
            (pair_hbm, pair_in), (in_gain_hbm, in_gain), (proj_weight_hbm, proj_weight), (gate_weight_hbm, gate_weight),
            (mid_gain_hbm, mid_gain), (out_weight_hbm, out_weight), (cot_hbm, cotangent),
        ))
    ]
    for load in loads:
        load.start()

    def send_part(phase, h, src_of, dst):
        sem = phase * CHUNKS + h
        for target in peers:
            pltpu.make_async_remote_copy(
                src_ref=src_of(target), dst_ref=dst,
                send_sem=send_sem.at[sem], recv_sem=recv_sem.at[sem],
                device_id={"pair": target}, device_id_type=MESH,
            ).start()

    def wait_part(phase, h, slots):
        fifteen = slots.at[pl.ds(0, PEERS - 1)]
        pltpu.make_async_copy(fifteen, fifteen, recv_sem.at[phase * CHUNKS + h]).wait()

    def wait_sent(phase, h, slots):
        fifteen = slots.at[pl.ds(0, PEERS - 1)]
        pltpu.make_async_copy(fifteen, fifteen, send_sem.at[phase * CHUNKS + h]).wait()

    in_acc[...] = jnp.zeros_like(in_acc)
    mid_acc[...] = jnp.zeros_like(mid_acc)

    def lanes(p):
        return slice(p * WIDE, (p + 1) * WIDE)

    def put_rows(ref, first, values):
        parts = [values[:, i * N : (i + 1) * N].reshape(PEERS, ROWS, N) for i in range(2)]
        ref[:, first : first + 2 * ROWS, :] = jnp.concatenate(parts, axis=1).astype(BF16)

    def get_rows(ref, first):
        block = ref[:, first : first + 2 * ROWS, :].astype(F32)
        return jnp.concatenate([block[:, i * ROWS : (i + 1) * ROWS].reshape(N, N) for i in range(2)], axis=1)

    def project(l, p, state, ref):
        at = lanes(p)
        unit_p, inverse_p = norm_forward(state)
        normed_p = (unit_p * gains[2 * l]).astype(BF16)
        unit[l, :, at] = unit_p
        inverse[l, :, at] = inverse_p
        normed[l, :, at] = normed_p
        projected = nn(weight_t[l], normed_p)
        row = 2 * ROWS * (p % PER)
        sig = sigmoid(projected[0:N])
        val = projected[N : 2 * N]
        sig_l[l, :, at] = sig
        val_l[l, :, at] = val
        put_rows(ref, row, sig * val)
        sig = sigmoid(projected[2 * N : 3 * N])
        val = projected[3 * N : 4 * N]
        sig_r[l, :, at] = sig
        val_r[l, :, at] = val
        put_rows(ref, PART + row, sig * val)
        gate[l, :, at] = projected[4 * N :]

    def after_project(l):
        for p in range(STEPS):
            at = lanes(p)
            gate_p = sigmoid(gate[l, :, at])
            gate[l, :, at] = gate_p
            for sig, val in ((sig_l, val_l), (sig_r, val_r)):
                sig_p = sig[l, :, at]
                val[l, :, at] = val[l, :, at] * sig_p * (1.0 - sig_p)
            if l == 1:
                gate_der[0, :, at] = output[:, at] * gate[0, :, at] * (1.0 - gate[0, :, at])
                cot_p = cot[:, at]
                gate_der[1, :, at] = cot_p * gate_p * (1.0 - gate_p)
                go_p = (cot_p * gate_p).astype(BF16)
                go[1, :, at] = go_p
                grad_mixed_p = nn(out_weight[1], go_p)
                grad_mixed[:, at] = grad_mixed_p
                scaled_p = grad_mixed_p * gains[3]
                scaled[:, at] = scaled_p
                scaled_mean[:, at] = mean_channels(scaled_p)

    def steps(h):
        return range(h * PER, (h + 1) * PER)

    def send2_part(slot, phase, h):
        send_part(phase, h, lambda d: send2.at[slot, h, d], recv2.at[slot, h, me])
        recv2[slot, h, me] = send2[slot, h, me]

    def send1_part(slot, phase, h):
        send_part(phase, h, lambda d: send1.at[slot, h, d], recv1.at[slot, h, me])
        recv1[slot, h, me] = send1[slot, h, me]

    def wait2_part(slot, phase, h):
        wait_part(phase, h, recv2.at[slot, h])

    def wait1_part(slot, phase, h):
        wait_part(phase, h, recv1.at[slot, h])

    def part_rows(d, h):
        return slice(d * ROWS * ROWS + h * PART, d * ROWS * ROWS + (h + 1) * PART)

    def channel(c):
        return pl.ds(c, N, stride=ROWS)

    def channel_forward(l, slot2, slot1, phase_in, phase_out):
        for h in range(CHUNKS):
            wait2_part(slot2, phase_in, h)
            for s in range(PEERS):
                turn_a[part_rows(s, h), :] = recv2[slot2, h, s, :PART].astype(F32)
                turn_b[part_rows(s, h), :] = recv2[slot2, h, s, PART:].astype(F32)
        for c in range(ROWS):
            left = turn_a[channel(c), :].astype(BF16)
            right = turn_b[channel(c), :].astype(BF16)
            chan_l[l, c] = left
            chan_r[l, c] = right
            turn_a[channel(c), :] = nt(left, right) if l == 0 else tn(left, right)
        for h in range(CHUNKS):
            for d in range(PEERS):
                send1[slot1, h, d] = turn_a[part_rows(d, h), :].astype(BF16)
            send1_part(slot1, phase_out, h)

    def channel_backward(l, slot1, slot2, phase_in, phase_out):
        for h in range(CHUNKS):
            wait1_part(slot1, phase_in, h)
            for s in range(PEERS):
                turn_a[part_rows(s, h), :] = recv1[slot1, h, s].astype(F32)
        for c in range(ROWS):
            grad = turn_a[channel(c), :].astype(BF16)
            left, right = chan_l[l, c], chan_r[l, c]
            turn_a[channel(c), :] = nn(grad, right) if l == 0 else nt(right, grad)
            turn_b[channel(c), :] = tn(grad, left) if l == 0 else nn(left, grad)
        for h in range(CHUNKS):
            for d in range(PEERS):
                send2[slot2, h, d, :PART] = turn_a[part_rows(d, h), :].astype(BF16)
                send2[slot2, h, d, PART:] = turn_b[part_rows(d, h), :].astype(BF16)
            send2_part(slot2, phase_out, h)

    def fold(values):
        return values[:, :N] + values[:, N:]

    def back_pieces(l, p, ref):
        at = lanes(p)
        row = 2 * ROWS * (p % PER)
        for side, (sig, val) in enumerate(((sig_l, val_l), (sig_r, val_r))):
            grad = get_rows(ref, side * PART + row)
            first = 2 * N * side
            gp[l, first : first + N, at] = (grad * val[l, :, at]).astype(BF16)
            gp[l, first + N : first + 2 * N, at] = (grad * sig[l, :, at]).astype(BF16)

    def back_tail(l, p, gradient):
        at = lanes(p)
        grad_normed_p = nn(weight[l], gp[l, :, at])
        unit_p = unit[l, :, at]
        if l == 1:
            grad_normed[:, at] = grad_normed_p
        else:
            in_acc[l] += fold(grad_normed_p * unit_p)
        return gradient + norm_backward(grad_normed_p * gains[2 * l], unit_p, inverse[l, :, at])

    loads[0].wait()
    for a in range(ROWS):
        state0[:, a * N : (a + 1) * N] = pair_in[a].astype(F32).T
    for load in loads[1:4]:
        load.wait()

    def set_gain(index, source, l):
        row = jnp.broadcast_to(source[l : l + 1, :], (N, N)).T
        gains[index] = jnp.concatenate([row, row], axis=1)

    def set_weights(l):
        set_gain(2 * l, in_gain, l)
        for f in range(4):
            block = proj_weight[l, :, f * N : (f + 1) * N]
            weight[l, :, f * N : (f + 1) * N] = block
            weight_t[l, f * N : (f + 1) * N, :] = block.astype(F32).T.astype(BF16)
        weight[l, :, 4 * N :] = gate_weight[l]
        weight_t[l, 4 * N :, :] = gate_weight[l].astype(F32).T.astype(BF16)

    set_weights(0)
    for h in range(CHUNKS):
        for p in steps(h):
            project(0, p, state0[:, lanes(p)], send2.at[0, h])
        if h == 0:
            pl.semaphore_wait(barrier, PEERS - 1)
        send2_part(0, TO_CH_0, h)

    for load in loads[4:]:
        load.wait()
    set_weights(1)
    for l in range(2):
        set_gain(2 * l + 1, mid_gain, l)
        out_t[l] = out_weight[l].astype(F32).T.astype(BF16)
    for a in range(ROWS):
        cot[:, a * N : (a + 1) * N] = cotangent[a].astype(F32).T

    after_project(0)

    channel_forward(0, 0, 0, TO_CH_0, TO_ROW_0)

    for h in range(CHUNKS):
        wait1_part(0, TO_ROW_0, h)
        for p in steps(h):
            at = lanes(p)
            mix_unit_p, mix_inverse_p = norm_forward(get_rows(recv1.at[0, h], 2 * ROWS * (p % PER)))
            mixed_p = (mix_unit_p * gains[1]).astype(BF16)
            mix_unit[0, :, at] = mix_unit_p
            mix_inverse[:, at] = mix_inverse_p
            mixed[0, :, at] = mixed_p
            output_p = nn(out_t[0], mixed_p)
            output[:, at] = output_p
            state = (state0[:, at] + gate[0, :, at] * output_p).astype(BF16).astype(F32)
            project(1, p, state, send2.at[1, h])
        send2_part(1, TO_CH_1, h)

    after_project(1)

    channel_forward(1, 1, 1, TO_CH_1, TO_ROW_1)

    for h in range(CHUNKS):
        wait1_part(1, TO_ROW_1, h)
        for p in steps(h):
            at = lanes(p)
            row = 2 * ROWS * (p % PER)
            mix_unit_p, mix_inverse_p = norm_forward(get_rows(recv1.at[1, h], row))
            mix_unit[1, :, at] = mix_unit_p
            scaled_p = scaled[:, at]
            mean_two = mean_channels(scaled_p * mix_unit_p)
            put_rows(send1.at[2, h], row, mix_inverse_p * (scaled_p - scaled_mean[:, at] - mix_unit_p * mean_two))
        send1_part(2, GRAD_CH_1, h)

    for p in range(STEPS):
        at = lanes(p)
        mix_unit_p = mix_unit[1, :, at]
        mixed_p = (mix_unit_p * gains[3]).astype(BF16)
        mixed[1, :, at] = mixed_p
        gp[1, 4 * N :, at] = (gate_der[1, :, at] * nn(out_t[1], mixed_p)).astype(BF16)
        mid_acc[1] += fold(grad_mixed[:, at] * mix_unit_p)

    channel_backward(1, 2, 2, GRAD_CH_1, GRAD_ROW_1)

    for h in range(CHUNKS):
        wait2_part(2, GRAD_ROW_1, h)
        for p in steps(h):
            at = lanes(p)
            back_pieces(1, p, recv2.at[2, h])
            gradient = back_tail(1, p, cot[:, at])
            grad1[:, at] = gradient
            go_p = (gradient * gate[0, :, at]).astype(BF16)
            go[0, :, at] = go_p
            grad_mixed_p = nn(out_weight[0], go_p)
            grad_mixed[:, at] = grad_mixed_p
            grad_product = norm_backward(grad_mixed_p * gains[1], mix_unit[0, :, at], mix_inverse[:, at])
            put_rows(send1.at[3, h], 2 * ROWS * (p % PER), grad_product)
        send1_part(3, GRAD_CH_0, h)

    for p in range(STEPS):
        at = lanes(p)
        gp[0, 4 * N :, at] = (grad1[:, at] * gate_der[0, :, at]).astype(BF16)
        mid_acc[0] += fold(grad_mixed[:, at] * mix_unit[0, :, at])
        in_acc[1] += fold(grad_normed[:, at] * unit[1, :, at])

    def put_early(first, values):
        for i in range(N // 64):
            sum_early_send[first + i] = values[64 * i : 64 * i + 64, :].astype(BF16)

    for f in range(5):
        put_early(2 * f, nt(normed[1], gp[1, f * N : (f + 1) * N, :]))
    put_early(10, nt(mixed[1], go[1]))
    put_early(12, nt(normed[0], gp[0, 4 * N :, :]))
    put_early(14, nt(mixed[0], go[0]))
    for h in range(CHUNKS):
        wait_sent(GRAD_CH_0, h, send1.at[3, h])
    send_part(SUM_EARLY, 0, lambda d: sum_early_send.at[d], sum_early_recv.at[me])
    sum_early_recv[me] = sum_early_send[me]

    channel_backward(0, 3, 3, GRAD_CH_0, GRAD_ROW_0)

    wait_part(SUM_EARLY, 0, sum_early_recv)
    all_early[me] = jnp.sum(sum_early_recv[...].astype(F32), axis=0).astype(BF16)
    for h in range(CHUNKS):
        wait_sent(GRAD_ROW_0, h, send2.at[3, h])
    send_part(ALL_EARLY, 0, lambda d: all_early.at[me], all_early.at[me])

    def last_rows(p):
        gradient = back_tail(0, p, grad1[:, lanes(p)])
        for i in range(2):
            pair_grad[2 * p + i] = gradient[:, i * N : (i + 1) * N].T.astype(BF16)

    for h in range(CHUNKS):
        wait2_part(3, GRAD_ROW_0, h)
        for p in steps(h):
            back_pieces(0, p, recv2.at[3, h])
        if h < CHUNKS - 1:
            for p in steps(h):
                last_rows(p)

    for f in range(4):
        values = nt(normed[0], gp[0, f * N : (f + 1) * N, :])
        for i in range(4):
            sum_late_send[4 * f + i] = values[32 * i : 32 * i + 32, :].astype(BF16)
    send_part(SUM_LATE, 0, lambda d: sum_late_send.at[d], sum_late_recv.at[me])
    sum_late_recv[me] = sum_late_send[me]

    for p in steps(CHUNKS - 1):
        last_rows(p)

    gain_rows = [jnp.sum(ref[l].T, axis=0, keepdims=True) for ref in (in_acc, mid_acc) for l in range(2)]
    gains_all[me] = jnp.concatenate(gain_rows + [jnp.zeros((4, N), F32)], axis=0)
    send_part(GAINS, 0, lambda d: gains_all.at[me], gains_all.at[me])

    wait_part(SUM_LATE, 0, sum_late_recv)
    all_late[me] = jnp.sum(sum_late_recv[...].astype(F32), axis=0).astype(BF16)
    send_part(ALL_LATE, 0, lambda d: all_late.at[me], all_late.at[me])

    wait_part(ALL_EARLY, 0, all_early)
    early_out[...] = all_early[...]
    for h in range(CHUNKS):
        for slot, two, one in ((0, TO_CH_0, TO_ROW_0), (1, TO_CH_1, TO_ROW_1), (2, GRAD_ROW_1, GRAD_CH_1)):
            wait_sent(two, h, send2.at[slot, h])
            wait_sent(one, h, send1.at[slot, h])
    wait_sent(SUM_EARLY, 0, sum_early_send)
    wait_sent(ALL_EARLY, 0, all_early)
    wait_sent(SUM_LATE, 0, sum_late_send)
    wait_sent(GAINS, 0, gains_all)

    wait_part(GAINS, 0, gains_all)
    gains_out[...] = jnp.sum(gains_all[...], axis=0)

    wait_part(ALL_LATE, 0, all_late)
    late_out[...] = all_late[...]
    wait_sent(ALL_LATE, 0, all_late)


def write_kernel(
    pair, early_in, late_in, gains_in,
    pair_grad, proj_grad, gate_grad, out_grad, in_gain_grad, mid_gain_grad,
):
    scale = 1.0 / N
    pair_grad[...] = pair[...]

    def early(first):
        return early_in[first : first + 2].astype(F32).reshape(N, N) * scale

    for f in range(4):
        proj_grad[0, :, f * N : (f + 1) * N] = late_in[4 * f : 4 * f + 4].astype(F32).reshape(N, N) * scale
        proj_grad[1, :, f * N : (f + 1) * N] = early(2 * f)
    gate_grad[1] = early(8)
    out_grad[1] = early(10)
    gate_grad[0] = early(12)
    out_grad[0] = early(14)
    in_gain_grad[...] = gains_in[0:2, :] * scale
    mid_gain_grad[...] = gains_in[2:4, :] * scale


def on_device(*arrays):
    layer_f32 = pltpu.VMEM((2, N, CELLS), F32)
    layer_bf16 = pltpu.VMEM((2, N, CELLS), BF16)
    plain_f32 = pltpu.VMEM((N, CELLS), F32)
    vmem = pl.BlockSpec(memory_space=pltpu.VMEM)
    results = pl.pallas_call(
        kernel,
        out_shape=(
            pltpu.VMEM((ROWS, N, N), BF16),
            pltpu.VMEM((PEERS, 64, N), BF16),
            pltpu.VMEM((PEERS, 32, N), BF16),
            pltpu.VMEM((8, N), F32),
        ),
        in_specs=[pl.BlockSpec(memory_space=pl.ANY)] * 7,
        out_specs=[vmem] * 4,
        scratch_shapes=[pltpu.VMEM(array.shape, array.dtype) for array in arrays] + [
            pltpu.VMEM((4, N, WIDE), F32),
            pltpu.VMEM((2, N, 5 * N), BF16),
            pltpu.VMEM((2, 5 * N, N), BF16),
            pltpu.VMEM((2, N, N), BF16),
            plain_f32, plain_f32, plain_f32,
            layer_f32,
            pltpu.VMEM((2, 1, CELLS), F32),
            layer_bf16,
            layer_f32, layer_f32, layer_f32, layer_f32,
            layer_f32, layer_f32, plain_f32, layer_f32,
            pltpu.VMEM((1, CELLS), F32),
            layer_bf16,
            plain_f32, plain_f32,
            pltpu.VMEM((1, CELLS), F32),
            plain_f32,
            layer_bf16,
            pltpu.VMEM((2, 5 * N, CELLS), BF16),
            pltpu.VMEM((2, N, N), F32),
            pltpu.VMEM((2, N, N), F32),
            pltpu.VMEM((CELLS, N), F32),
            pltpu.VMEM((CELLS, N), F32),
            pltpu.VMEM((2, ROWS, N, N), BF16),
            pltpu.VMEM((2, ROWS, N, N), BF16),
            pltpu.VMEM((4, CHUNKS, PEERS, 2 * PART, N), BF16),
            pltpu.VMEM((4, CHUNKS, PEERS, 2 * PART, N), BF16),
            pltpu.VMEM((4, CHUNKS, PEERS, PART, N), BF16),
            pltpu.VMEM((4, CHUNKS, PEERS, PART, N), BF16),
            pltpu.VMEM((PEERS, 64, N), BF16),
            pltpu.VMEM((PEERS, 64, N), BF16),
            pltpu.VMEM((PEERS, 64, N), BF16),
            pltpu.VMEM((PEERS, 32, N), BF16),
            pltpu.VMEM((PEERS, 32, N), BF16),
            pltpu.VMEM((PEERS, 32, N), BF16),
            pltpu.VMEM((PEERS, 8, N), F32),
            pltpu.SemaphoreType.DMA((7,)),
            pltpu.SemaphoreType.DMA((PHASES * CHUNKS,)),
            pltpu.SemaphoreType.DMA((PHASES * CHUNKS,)),
        ],
        compiler_params=pltpu.CompilerParams(
            collective_id=0, has_side_effects=True, vmem_limit_bytes=56 * 1024 * 1024
        ),
    )(*arrays)
    return pl.pallas_call(
        write_kernel,
        out_shape=(
            jax.ShapeDtypeStruct((ROWS, N, N), BF16),
            jax.ShapeDtypeStruct((2, N, 4 * N), F32),
            jax.ShapeDtypeStruct((2, N, N), F32),
            jax.ShapeDtypeStruct((2, N, N), F32),
            jax.ShapeDtypeStruct((2, N), F32),
            jax.ShapeDtypeStruct((2, N), F32),
        ),
        in_specs=[vmem] * 4,
        out_specs=[vmem] * 6,
        compiler_params=pltpu.CompilerParams(vmem_limit_bytes=4 * 1024 * 1024),
    )(*results)


def solution(mesh):
    return jax.shard_map(
        on_device,
        mesh=mesh,
        in_specs=(
            P(("dp", "pair"), None, None),
            P(("dp", "pair"), None, None),
            P(),
            P(),
            P(),
            P(),
            P(),
        ),
        out_specs=(
            P(("dp", "pair"), None, None),
            P("dp", None, None),
            P("dp", None, None),
            P("dp", None, None),
            P("dp", None),
            P("dp", None),
        ),
        check_vma=False,
    )
```

```python
import functools

import jax
import jax.numpy as jnp
from jax import lax
from jax.experimental import pallas as pl
from jax.experimental.pallas import tpu as pltpu
from jax.sharding import PartitionSpec as P

EPSILON = 1e-05
MESH = pl.DeviceIdType.MESH
F32 = jnp.float32
BF16 = jnp.bfloat16

N = 128
PEERS = 16
ROWS = N // PEERS
CELLS = ROWS * N
WIDE = 2 * N
STEPS = CELLS // WIDE
CHUNKS = 2
PER = STEPS // CHUNKS
PART = ROWS * ROWS // CHUNKS

TO_CH_0, TO_ROW_0, TO_CH_1, TO_ROW_1, GRAD_CH_1, GRAD_ROW_1, GRAD_CH_0, GRAD_ROW_0 = range(8)
SUM_EARLY, ALL_EARLY, SUM_LATE, ALL_LATE, GAINS, RIGHT_0, GRAD_LEFT_0 = range(8, 15)
PHASES = 15


def dot(first, second, dims):
    return lax.dot_general(first, second, (dims, ((), ())), preferred_element_type=F32)


def nn(first, second):
    return dot(first, second, ((1,), (0,)))


def nt(first, second):
    return dot(first, second, ((1,), (1,)))


def tn(first, second):
    return dot(first, second, ((0,), (0,)))


def sigmoid(values):
    return 0.5 * jnp.tanh(0.5 * values) + 0.5


def mean_channels(values):
    return jnp.sum(values, axis=0, keepdims=True) * (1.0 / N)


def norm_forward(values):
    shifted = values - mean_channels(values)
    inverse = lax.rsqrt(mean_channels(shifted * shifted) + EPSILON)
    return shifted * inverse, inverse


def norm_backward(scaled, unit, inverse):
    return inverse * (scaled - mean_channels(scaled) - unit * mean_channels(scaled * unit))


def kernel(
    pair_hbm, cot_hbm, in_gain_hbm, proj_weight_hbm, gate_weight_hbm, mid_gain_hbm, out_weight_hbm,
    pair_grad, early_out, late_out, gains_out,
    pair_in, cotangent, in_gain, proj_weight, gate_weight, mid_gain, out_weight,
    gains, weight, weight_t, out_t,
    state0, cot, grad1,
    unit, inverse, normed, sig_l, val_l, sig_r, val_r, gate, gate_der, output, mix_unit, mix_inverse, mixed,
    grad_mixed, scaled, scaled_mean, grad_normed,
    go, gp, in_acc, mid_acc,
    turn_a, turn_b, chan_l, chan_r, chan_g,
    send2, recv2, send1, recv1,
    sum_early_send, sum_early_recv, all_early, sum_late_send, sum_late_recv, all_late, gains_all,
    load_sem, send_sem, recv_sem,
):
    me = lax.axis_index("pair")
    my_x, my_y, my_core = me // 8, (me // 2) % 4, me % 2

    def peer(o):
        x = (my_x + o // 8) % 2
        y = (my_y + (o // 2) % 4) % 4
        core = (my_core + o % 2) % 2
        return x * 8 + y * 2 + core

    barrier = pltpu.get_barrier_semaphore()

    peers = [peer(o) for o in (4, 12, 5, 13, 2, 10, 6, 14, 3, 11, 7, 15, 8, 9, 1)]
    for target in peers:
        pl.semaphore_signal(barrier, inc=1, device_id={"pair": target}, device_id_type=MESH)

    loads = [
        pltpu.make_async_copy(source, target, load_sem.at[i])
        for i, (source, target) in enumerate((
            (pair_hbm, pair_in), (in_gain_hbm, in_gain), (proj_weight_hbm, proj_weight), (gate_weight_hbm, gate_weight),
            (mid_gain_hbm, mid_gain), (out_weight_hbm, out_weight), (cot_hbm, cotangent),
        ))
    ]
    for load in loads:
        load.start()

    def send_part(phase, h, src_of, dst):
        sem = phase * CHUNKS + h
        for target in peers:
            pltpu.make_async_remote_copy(
                src_ref=src_of(target), dst_ref=dst,
                send_sem=send_sem.at[sem], recv_sem=recv_sem.at[sem],
                device_id={"pair": target}, device_id_type=MESH,
            ).start()

    def wait_part(phase, h, slots):
        fifteen = slots.at[pl.ds(0, PEERS - 1)]
        pltpu.make_async_copy(fifteen, fifteen, recv_sem.at[phase * CHUNKS + h]).wait()

    def wait_sent(phase, h, slots):
        fifteen = slots.at[pl.ds(0, PEERS - 1)]
        pltpu.make_async_copy(fifteen, fifteen, send_sem.at[phase * CHUNKS + h]).wait()

    in_acc[...] = jnp.zeros_like(in_acc)
    mid_acc[...] = jnp.zeros_like(mid_acc)

    def lanes(p):
        return slice(p * WIDE, (p + 1) * WIDE)

    def put_rows(ref, first, values):
        parts = [values[:, i * N : (i + 1) * N].reshape(PEERS, ROWS, N) for i in range(2)]
        ref[:, first : first + 2 * ROWS, :] = jnp.concatenate(parts, axis=1).astype(BF16)

    def get_rows(ref, first):
        block = ref[:, first : first + 2 * ROWS, :].astype(F32)
        return jnp.concatenate([block[:, i * ROWS : (i + 1) * ROWS].reshape(N, N) for i in range(2)], axis=1)

    def project(l, p, state, left_ref, right_ref, left_row, right_row):
        at = lanes(p)
        unit_p, inverse_p = norm_forward(state)
        normed_p = (unit_p * gains[2 * l]).astype(BF16)
        unit[l, :, at] = unit_p
        inverse[l, :, at] = inverse_p
        normed[l, :, at] = normed_p
        projected = nn(weight_t[l], normed_p)
        sig = sigmoid(projected[0:N])
        val = projected[N : 2 * N]
        sig_l[l, :, at] = sig
        val_l[l, :, at] = val
        put_rows(left_ref, left_row, sig * val)
        sig = sigmoid(projected[2 * N : 3 * N])
        val = projected[3 * N : 4 * N]
        sig_r[l, :, at] = sig
        val_r[l, :, at] = val
        put_rows(right_ref, right_row, sig * val)
        gate[l, :, at] = projected[4 * N :]

    def after_project(l):
        for p in range(STEPS):
            at = lanes(p)
            gate_p = sigmoid(gate[l, :, at])
            gate[l, :, at] = gate_p
            for sig, val in ((sig_l, val_l), (sig_r, val_r)):
                sig_p = sig[l, :, at]
                val[l, :, at] = val[l, :, at] * sig_p * (1.0 - sig_p)
            if l == 1:
                gate_der[0, :, at] = output[:, at] * gate[0, :, at] * (1.0 - gate[0, :, at])
                cot_p = cot[:, at]
                gate_der[1, :, at] = cot_p * gate_p * (1.0 - gate_p)
                go_p = (cot_p * gate_p).astype(BF16)
                go[1, :, at] = go_p
                grad_mixed_p = nn(out_weight[1], go_p)
                grad_mixed[:, at] = grad_mixed_p
                scaled_p = grad_mixed_p * gains[3]
                scaled[:, at] = scaled_p
                scaled_mean[:, at] = mean_channels(scaled_p)

    def steps(h):
        return range(h * PER, (h + 1) * PER)

    def send2_part(slot, phase, h):
        send_part(phase, h, lambda d: send2.at[slot, h, d], recv2.at[slot, h, me])
        recv2[slot, h, me] = send2[slot, h, me]

    def send1_part(slot, phase, h):
        send_part(phase, h, lambda d: send1.at[slot, h, d], recv1.at[slot, h, me])
        recv1[slot, h, me] = send1[slot, h, me]

    def wait2_part(slot, phase, h):
        wait_part(phase, h, recv2.at[slot, h])

    def wait1_part(slot, phase, h):
        wait_part(phase, h, recv1.at[slot, h])

    def part_rows(d, h):
        return slice(d * ROWS * ROWS + h * PART, d * ROWS * ROWS + (h + 1) * PART)

    def part_of(h):
        return pl.ds(h * PART, PART)

    def own_part(d, h):
        first = h * PEERS * PART + d * PART
        return slice(first, first + PART)

    def channel_part(c, h):
        return pl.ds(h * PEERS * PART + c, N // CHUNKS, stride=ROWS)

    def half(h):
        return slice(h * N // CHUNKS, (h + 1) * N // CHUNKS)

    def channel(c):
        return pl.ds(c, N, stride=ROWS)

    def channel_forward_0():
        wait_part(RIGHT_0, 0, recv2.at[0, 0])
        for s in range(PEERS):
            turn_b[s * 64 : s * 64 + 64, :] = recv2[0, 0, s].astype(F32)
        for c in range(ROWS):
            chan_r[0, c] = turn_b[channel(c), :].astype(BF16)
        for h in range(CHUNKS):
            wait_part(TO_CH_0, h, recv2.at[0, 1, :, part_of(h)])
            for s in range(PEERS):
                turn_a[own_part(s, h), :] = recv2[0, 1, s, h * PART : (h + 1) * PART].astype(F32)
            for c in range(ROWS):
                left = turn_a[channel_part(c, h), :].astype(BF16)
                chan_l[0, c, half(h)] = left
                turn_a[channel_part(c, h), :] = nt(left, chan_r[0, c])
            for d in range(PEERS):
                send1[0, h, d] = turn_a[own_part(d, h), :].astype(BF16)
            send1_part(0, TO_ROW_0, h)

    def channel_forward_1():
        for h in range(CHUNKS):
            wait2_part(1, TO_CH_1, h)
            for s in range(PEERS):
                turn_a[part_rows(s, h), :] = recv2[1, h, s, :PART].astype(F32)
                turn_b[part_rows(s, h), :] = recv2[1, h, s, PART:].astype(F32)
        for c in range(ROWS):
            left = turn_a[channel(c), :].astype(BF16)
            right = turn_b[channel(c), :].astype(BF16)
            chan_l[1, c] = left
            chan_r[1, c] = right
            turn_a[channel(c), :] = tn(left, right)
        for h in range(CHUNKS):
            for d in range(PEERS):
                send1[1, h, d] = turn_a[part_rows(d, h), :].astype(BF16)
            send1_part(1, TO_ROW_1, h)

    def channel_backward_1():
        for h in range(CHUNKS):
            wait1_part(2, GRAD_CH_1, h)
            for s in range(PEERS):
                turn_a[part_rows(s, h), :] = recv1[2, h, s].astype(F32)
        for c in range(ROWS):
            grad = turn_a[channel(c), :].astype(BF16)
            turn_a[channel(c), :] = nt(chan_r[1, c], grad)
            turn_b[channel(c), :] = nn(chan_l[1, c], grad)
        for h in range(CHUNKS):
            for d in range(PEERS):
                send2[2, h, d, :PART] = turn_a[part_rows(d, h), :].astype(BF16)
                send2[2, h, d, PART:] = turn_b[part_rows(d, h), :].astype(BF16)
            send2_part(2, GRAD_ROW_1, h)

    def channel_backward_0():
        left_rows = pl.ds(0, PART)
        for h in range(CHUNKS):
            wait1_part(3, GRAD_CH_0, h)
            for s in range(PEERS):
                turn_a[own_part(s, h), :] = recv1[3, h, s].astype(F32)
            for c in range(ROWS):
                grad = turn_a[channel_part(c, h), :].astype(BF16)
                chan_g[c, half(h)] = grad
                turn_b[channel_part(c, h), :] = nn(grad, chan_r[0, c])
            for d in range(PEERS):
                send2[3, h, d, :PART] = turn_b[own_part(d, h), :].astype(BF16)
            if h == 0:
                send_part(GRAD_LEFT_0, 0, lambda d: send2.at[3, 0, d, left_rows], recv2.at[3, 0, me, left_rows])
        for c in range(ROWS):
            turn_a[channel(c), :] = tn(chan_g[c], chan_l[0, c])
        for h in range(CHUNKS):
            for d in range(PEERS):
                send2[3, h, d, PART:] = turn_a[part_rows(d, h), :].astype(BF16)
            if h == 0:
                right_rows = pl.ds(PART, PART)
                send_part(GRAD_ROW_0, 0, lambda d: send2.at[3, 0, d, right_rows], recv2.at[3, 0, me, right_rows])
                recv2[3, 0, me] = send2[3, 0, me]
            else:
                send2_part(3, GRAD_ROW_0, h)

    def fold(values):
        return values[:, :N] + values[:, N:]

    def back_pieces(l, p, ref):
        at = lanes(p)
        row = 2 * ROWS * (p % PER)
        for side, (sig, val) in enumerate(((sig_l, val_l), (sig_r, val_r))):
            grad = get_rows(ref, side * PART + row)
            first = 2 * N * side
            gp[l, first : first + N, at] = (grad * val[l, :, at]).astype(BF16)
            gp[l, first + N : first + 2 * N, at] = (grad * sig[l, :, at]).astype(BF16)

    def back_tail(l, p, gradient):
        at = lanes(p)
        grad_normed_p = nn(weight[l], gp[l, :, at])
        unit_p = unit[l, :, at]
        if l == 1:
            grad_normed[:, at] = grad_normed_p
        else:
            in_acc[l] += fold(grad_normed_p * unit_p)
        return gradient + norm_backward(grad_normed_p * gains[2 * l], unit_p, inverse[l, :, at])

    loads[0].wait()
    for a in range(ROWS):
        state0[:, a * N : (a + 1) * N] = pair_in[a].astype(F32).T
    for load in loads[1:4]:
        load.wait()

    def set_gain(index, source, l):
        row = jnp.broadcast_to(source[l : l + 1, :], (N, N)).T
        gains[index] = jnp.concatenate([row, row], axis=1)

    def set_weights(l):
        set_gain(2 * l, in_gain, l)
        for f in range(4):
            block = proj_weight[l, :, f * N : (f + 1) * N]
            weight[l, :, f * N : (f + 1) * N] = block
            weight_t[l, f * N : (f + 1) * N, :] = block.astype(F32).T.astype(BF16)
        weight[l, :, 4 * N :] = gate_weight[l]
        weight_t[l, 4 * N :, :] = gate_weight[l].astype(F32).T.astype(BF16)

    set_weights(0)
    for p in range(STEPS):
        project(0, p, state0[:, lanes(p)], send2.at[0, 1], send2.at[0, 0], 2 * ROWS * p, 2 * ROWS * p)
    pl.semaphore_wait(barrier, PEERS - 1)
    send_part(RIGHT_0, 0, lambda d: send2.at[0, 0, d], recv2.at[0, 0, me])
    for h in range(CHUNKS):
        rows = part_of(h)
        send_part(TO_CH_0, h, lambda d: send2.at[0, 1, d, rows], recv2.at[0, 1, me, rows])
    for i in range(2):
        recv2[0, i, me] = send2[0, i, me]

    for load in loads[4:]:
        load.wait()
    set_weights(1)
    for l in range(2):
        set_gain(2 * l + 1, mid_gain, l)
        out_t[l] = out_weight[l].astype(F32).T.astype(BF16)
    for a in range(ROWS):
        cot[:, a * N : (a + 1) * N] = cotangent[a].astype(F32).T

    after_project(0)

    channel_forward_0()

    for h in range(CHUNKS):
        wait1_part(0, TO_ROW_0, h)
        for p in steps(h):
            at = lanes(p)
            mix_unit_p, mix_inverse_p = norm_forward(get_rows(recv1.at[0, h], 2 * ROWS * (p % PER)))
            mixed_p = (mix_unit_p * gains[1]).astype(BF16)
            mix_unit[0, :, at] = mix_unit_p
            mix_inverse[:, at] = mix_inverse_p
            mixed[0, :, at] = mixed_p
            output_p = nn(out_t[0], mixed_p)
            output[:, at] = output_p
            state = (state0[:, at] + gate[0, :, at] * output_p).astype(BF16).astype(F32)
            row = 2 * ROWS * (p % PER)
            project(1, p, state, send2.at[1, h], send2.at[1, h], row, PART + row)
        send2_part(1, TO_CH_1, h)

    after_project(1)

    channel_forward_1()

    for h in range(CHUNKS):
        wait1_part(1, TO_ROW_1, h)
        for p in steps(h):
            at = lanes(p)
            row = 2 * ROWS * (p % PER)
            mix_unit_p, mix_inverse_p = norm_forward(get_rows(recv1.at[1, h], row))
            mix_unit[1, :, at] = mix_unit_p
            scaled_p = scaled[:, at]
            mean_two = mean_channels(scaled_p * mix_unit_p)
            put_rows(send1.at[2, h], row, mix_inverse_p * (scaled_p - scaled_mean[:, at] - mix_unit_p * mean_two))
        send1_part(2, GRAD_CH_1, h)

    for p in range(STEPS):
        at = lanes(p)
        mix_unit_p = mix_unit[1, :, at]
        mixed_p = (mix_unit_p * gains[3]).astype(BF16)
        mixed[1, :, at] = mixed_p
        gp[1, 4 * N :, at] = (gate_der[1, :, at] * nn(out_t[1], mixed_p)).astype(BF16)
        mid_acc[1] += fold(grad_mixed[:, at] * mix_unit_p)

    channel_backward_1()

    for h in range(CHUNKS):
        wait2_part(2, GRAD_ROW_1, h)
        for p in steps(h):
            at = lanes(p)
            back_pieces(1, p, recv2.at[2, h])
            gradient = back_tail(1, p, cot[:, at])
            grad1[:, at] = gradient
            go_p = (gradient * gate[0, :, at]).astype(BF16)
            go[0, :, at] = go_p
            grad_mixed_p = nn(out_weight[0], go_p)
            grad_mixed[:, at] = grad_mixed_p
            grad_product = norm_backward(grad_mixed_p * gains[1], mix_unit[0, :, at], mix_inverse[:, at])
            put_rows(send1.at[3, h], 2 * ROWS * (p % PER), grad_product)
        send1_part(3, GRAD_CH_0, h)

    for p in range(STEPS):
        at = lanes(p)
        gp[0, 4 * N :, at] = (grad1[:, at] * gate_der[0, :, at]).astype(BF16)
        mid_acc[0] += fold(grad_mixed[:, at] * mix_unit[0, :, at])
        in_acc[1] += fold(grad_normed[:, at] * unit[1, :, at])

    def put_early(first, values):
        for i in range(N // 64):
            sum_early_send[first + i] = values[64 * i : 64 * i + 64, :].astype(BF16)

    for f in range(5):
        put_early(2 * f, nt(normed[1], gp[1, f * N : (f + 1) * N, :]))
    put_early(10, nt(mixed[1], go[1]))
    put_early(12, nt(normed[0], gp[0, 4 * N :, :]))
    put_early(14, nt(mixed[0], go[0]))

    channel_backward_0()
    send_part(SUM_EARLY, 0, lambda d: sum_early_send.at[d], sum_early_recv.at[me])
    sum_early_recv[me] = sum_early_send[me]

    def last_rows(p):
        gradient = back_tail(0, p, grad1[:, lanes(p)])
        for i in range(2):
            pair_grad[2 * p + i] = gradient[:, i * N : (i + 1) * N].T.astype(BF16)

    for h in range(CHUNKS):
        if h == 0:
            wait_part(GRAD_LEFT_0, 0, recv2.at[3, 0, :, pl.ds(0, PART)])
            wait_part(GRAD_ROW_0, 0, recv2.at[3, 0, :, pl.ds(PART, PART)])
        else:
            wait2_part(3, GRAD_ROW_0, h)
        for p in steps(h):
            back_pieces(0, p, recv2.at[3, h])
        if h < CHUNKS - 1:
            for p in steps(h):
                last_rows(p)

    for f in range(4):
        values = nt(normed[0], gp[0, f * N : (f + 1) * N, :])
        for i in range(4):
            sum_late_send[4 * f + i] = values[32 * i : 32 * i + 32, :].astype(BF16)
    send_part(SUM_LATE, 0, lambda d: sum_late_send.at[d], sum_late_recv.at[me])
    sum_late_recv[me] = sum_late_send[me]

    wait_part(SUM_EARLY, 0, sum_early_recv)
    all_early[me] = jnp.sum(sum_early_recv[...].astype(F32), axis=0).astype(BF16)
    send_part(ALL_EARLY, 0, lambda d: all_early.at[me], all_early.at[me])

    for p in steps(CHUNKS - 1):
        last_rows(p)

    gain_rows = [jnp.sum(ref[l].T, axis=0, keepdims=True) for ref in (in_acc, mid_acc) for l in range(2)]
    gains_all[me] = jnp.concatenate(gain_rows + [jnp.zeros((4, N), F32)], axis=0)
    send_part(GAINS, 0, lambda d: gains_all.at[me], gains_all.at[me])

    wait_part(SUM_LATE, 0, sum_late_recv)
    all_late[me] = jnp.sum(sum_late_recv[...].astype(F32), axis=0).astype(BF16)
    send_part(ALL_LATE, 0, lambda d: all_late.at[me], all_late.at[me])

    wait_part(ALL_EARLY, 0, all_early)
    early_out[...] = all_early[...]
    for h in range(CHUNKS):
        wait_sent(TO_CH_0, h, send2.at[0, 1, :, part_of(h)])
        wait_sent(TO_ROW_0, h, send1.at[0, h])
        for slot, two, one in ((1, TO_CH_1, TO_ROW_1), (2, GRAD_ROW_1, GRAD_CH_1)):
            wait_sent(two, h, send2.at[slot, h])
            wait_sent(one, h, send1.at[slot, h])
    wait_sent(RIGHT_0, 0, send2.at[0, 0])
    wait_sent(GRAD_LEFT_0, 0, send2.at[3, 0, :, pl.ds(0, PART)])
    wait_sent(GRAD_ROW_0, 0, send2.at[3, 0, :, pl.ds(PART, PART)])
    wait_sent(GRAD_ROW_0, 1, send2.at[3, 1])
    for h in range(CHUNKS):
        wait_sent(GRAD_CH_0, h, send1.at[3, h])
    wait_sent(SUM_EARLY, 0, sum_early_send)
    wait_sent(ALL_EARLY, 0, all_early)
    wait_sent(SUM_LATE, 0, sum_late_send)
    wait_sent(GAINS, 0, gains_all)

    wait_part(GAINS, 0, gains_all)
    gains_out[...] = jnp.sum(gains_all[...], axis=0)

    wait_part(ALL_LATE, 0, all_late)
    late_out[...] = all_late[...]
    wait_sent(ALL_LATE, 0, all_late)


def write_kernel(
    pair, early_in, late_in, gains_in,
    pair_grad, proj_grad, gate_grad, out_grad, in_gain_grad, mid_gain_grad,
):
    scale = 1.0 / N
    pair_grad[...] = pair[...]

    def early(first):
        return early_in[first : first + 2].astype(F32).reshape(N, N) * scale

    for f in range(4):
        proj_grad[0, :, f * N : (f + 1) * N] = late_in[4 * f : 4 * f + 4].astype(F32).reshape(N, N) * scale
        proj_grad[1, :, f * N : (f + 1) * N] = early(2 * f)
    gate_grad[1] = early(8)
    out_grad[1] = early(10)
    gate_grad[0] = early(12)
    out_grad[0] = early(14)
    in_gain_grad[...] = gains_in[0:2, :] * scale
    mid_gain_grad[...] = gains_in[2:4, :] * scale


def on_device(*arrays):
    layer_f32 = pltpu.VMEM((2, N, CELLS), F32)
    layer_bf16 = pltpu.VMEM((2, N, CELLS), BF16)
    plain_f32 = pltpu.VMEM((N, CELLS), F32)
    vmem = pl.BlockSpec(memory_space=pltpu.VMEM)
    results = pl.pallas_call(
        kernel,
        out_shape=(
            pltpu.VMEM((ROWS, N, N), BF16),
            pltpu.VMEM((PEERS, 64, N), BF16),
            pltpu.VMEM((PEERS, 32, N), BF16),
            pltpu.VMEM((8, N), F32),
        ),
        in_specs=[pl.BlockSpec(memory_space=pl.ANY)] * 7,
        out_specs=[vmem] * 4,
        scratch_shapes=[pltpu.VMEM(array.shape, array.dtype) for array in arrays] + [
            pltpu.VMEM((4, N, WIDE), F32),
            pltpu.VMEM((2, N, 5 * N), BF16),
            pltpu.VMEM((2, 5 * N, N), BF16),
            pltpu.VMEM((2, N, N), BF16),
            plain_f32, plain_f32, plain_f32,
            layer_f32,
            pltpu.VMEM((2, 1, CELLS), F32),
            layer_bf16,
            layer_f32, layer_f32, layer_f32, layer_f32,
            layer_f32, layer_f32, plain_f32, layer_f32,
            pltpu.VMEM((1, CELLS), F32),
            layer_bf16,
            plain_f32, plain_f32,
            pltpu.VMEM((1, CELLS), F32),
            plain_f32,
            layer_bf16,
            pltpu.VMEM((2, 5 * N, CELLS), BF16),
            pltpu.VMEM((2, N, N), F32),
            pltpu.VMEM((2, N, N), F32),
            pltpu.VMEM((CELLS, N), F32),
            pltpu.VMEM((CELLS, N), F32),
            pltpu.VMEM((2, ROWS, N, N), BF16),
            pltpu.VMEM((2, ROWS, N, N), BF16),
            pltpu.VMEM((ROWS, N, N), BF16),
            pltpu.VMEM((4, CHUNKS, PEERS, 2 * PART, N), BF16),
            pltpu.VMEM((4, CHUNKS, PEERS, 2 * PART, N), BF16),
            pltpu.VMEM((4, CHUNKS, PEERS, PART, N), BF16),
            pltpu.VMEM((4, CHUNKS, PEERS, PART, N), BF16),
            pltpu.VMEM((PEERS, 64, N), BF16),
            pltpu.VMEM((PEERS, 64, N), BF16),
            pltpu.VMEM((PEERS, 64, N), BF16),
            pltpu.VMEM((PEERS, 32, N), BF16),
            pltpu.VMEM((PEERS, 32, N), BF16),
            pltpu.VMEM((PEERS, 32, N), BF16),
            pltpu.VMEM((PEERS, 8, N), F32),
            pltpu.SemaphoreType.DMA((7,)),
            pltpu.SemaphoreType.DMA((PHASES * CHUNKS,)),
            pltpu.SemaphoreType.DMA((PHASES * CHUNKS,)),
        ],
        compiler_params=pltpu.CompilerParams(
            collective_id=0, has_side_effects=True, vmem_limit_bytes=56 * 1024 * 1024
        ),
    )(*arrays)
    return pl.pallas_call(
        write_kernel,
        out_shape=(
            jax.ShapeDtypeStruct((ROWS, N, N), BF16),
            jax.ShapeDtypeStruct((2, N, 4 * N), F32),
            jax.ShapeDtypeStruct((2, N, N), F32),
            jax.ShapeDtypeStruct((2, N, N), F32),
            jax.ShapeDtypeStruct((2, N), F32),
            jax.ShapeDtypeStruct((2, N), F32),
        ),
        in_specs=[vmem] * 4,
        out_specs=[vmem] * 6,
        compiler_params=pltpu.CompilerParams(vmem_limit_bytes=4 * 1024 * 1024),
    )(*results)


def solution(mesh):
    return jax.shard_map(
        on_device,
        mesh=mesh,
        in_specs=(
            P(("dp", "pair"), None, None),
            P(("dp", "pair"), None, None),
            P(),
            P(),
            P(),
            P(),
            P(),
        ),
        out_specs=(
            P(("dp", "pair"), None, None),
            P("dp", None, None),
            P("dp", None, None),
            P("dp", None, None),
            P("dp", None),
            P("dp", None),
        ),
        check_vma=False,
    )
```

```python
import functools

import jax
import jax.numpy as jnp
from jax import lax
from jax.experimental import pallas as pl
from jax.experimental.pallas import tpu as pltpu
from jax.sharding import PartitionSpec as P

EPSILON = 1e-05
MESH = pl.DeviceIdType.MESH
F32 = jnp.float32
BF16 = jnp.bfloat16

N = 128
PEERS = 16
ROWS = N // PEERS
CELLS = ROWS * N
WIDE = 2 * N
STEPS = CELLS // WIDE
CHUNKS = 2
PER = STEPS // CHUNKS
PART = ROWS * ROWS // CHUNKS

TO_CH_0, TO_ROW_0, TO_CH_1, TO_ROW_1, GRAD_CH_1, GRAD_ROW_1, GRAD_CH_0, GRAD_ROW_0 = range(8)
SUM_EARLY, ALL_EARLY, SUM_LATE, ALL_LATE, GAINS, RIGHT_0, GRAD_LEFT_0, PRE_EARLY, SHARE_EARLY = range(8, 17)
PHASES = 17


def dot(first, second, dims):
    return lax.dot_general(first, second, (dims, ((), ())), preferred_element_type=F32)


def nn(first, second):
    return dot(first, second, ((1,), (0,)))


def nt(first, second):
    return dot(first, second, ((1,), (1,)))


def tn(first, second):
    return dot(first, second, ((0,), (0,)))


def sigmoid(values):
    return 0.5 * jnp.tanh(0.5 * values) + 0.5


def mean_channels(values):
    return jnp.sum(values, axis=0, keepdims=True) * (1.0 / N)


def norm_forward(values):
    shifted = values - mean_channels(values)
    inverse = lax.rsqrt(mean_channels(shifted * shifted) + EPSILON)
    return shifted * inverse, inverse


def norm_backward(scaled, unit, inverse):
    return inverse * (scaled - mean_channels(scaled) - unit * mean_channels(scaled * unit))


def kernel(
    pair_hbm, cot_hbm, in_gain_hbm, proj_weight_hbm, gate_weight_hbm, mid_gain_hbm, out_weight_hbm,
    pair_grad, early_out, late_out, gains_out,
    pair_in, cotangent, in_gain, proj_weight, gate_weight, mid_gain, out_weight,
    gains, weight, weight_t, out_t,
    state0, cot, grad1,
    unit, inverse, normed, sig_l, val_l, sig_r, val_r, gate, gate_der, output, mix_unit, mix_inverse, mixed,
    grad_mixed, scaled, scaled_mean, grad_normed,
    go, gp, in_acc, mid_acc,
    turn_a, turn_b, chan_l, chan_r, chan_g,
    send2, recv2, send1, recv1,
    sum_early_send, pre_early, sum_early_mid, sum_early_recv, all_early, sum_late_send, sum_late_recv, all_late, gains_all,
    load_sem, send_sem, recv_sem,
):
    me = lax.axis_index("pair")
    my_x, my_y, my_core = me // 8, (me // 2) % 4, me % 2

    def peer(o):
        x = (my_x + o // 8) % 2
        y = (my_y + (o // 2) % 4) % 4
        core = (my_core + o % 2) % 2
        return x * 8 + y * 2 + core

    barrier = pltpu.get_barrier_semaphore()

    peers = [peer(o) for o in (4, 12, 5, 13, 2, 10, 6, 14, 3, 11, 7, 15, 8, 9, 1)]
    same_core = [peer(o) for o in (4, 12, 2, 10, 6, 14, 8)]
    chip = me // 2
    for target in peers:
        pl.semaphore_signal(barrier, inc=1, device_id={"pair": target}, device_id_type=MESH)

    loads = [
        pltpu.make_async_copy(source, target, load_sem.at[i])
        for i, (source, target) in enumerate((
            (pair_hbm, pair_in), (in_gain_hbm, in_gain), (proj_weight_hbm, proj_weight), (gate_weight_hbm, gate_weight),
            (mid_gain_hbm, mid_gain), (out_weight_hbm, out_weight), (cot_hbm, cotangent),
        ))
    ]
    for load in loads:
        load.start()

    def send_part(phase, h, src_of, dst, targets=None):
        sem = phase * CHUNKS + h
        for target in targets or peers:
            pltpu.make_async_remote_copy(
                src_ref=src_of(target), dst_ref=dst,
                send_sem=send_sem.at[sem], recv_sem=recv_sem.at[sem],
                device_id={"pair": target}, device_id_type=MESH,
            ).start()

    def wait_part(phase, h, slots):
        fifteen = slots.at[pl.ds(0, PEERS - 1)]
        pltpu.make_async_copy(fifteen, fifteen, recv_sem.at[phase * CHUNKS + h]).wait()

    def wait_bytes(phase, sems, some):
        pltpu.make_async_copy(some, some, sems.at[phase * CHUNKS]).wait()

    def wait_sent(phase, h, slots):
        fifteen = slots.at[pl.ds(0, PEERS - 1)]
        pltpu.make_async_copy(fifteen, fifteen, send_sem.at[phase * CHUNKS + h]).wait()

    in_acc[...] = jnp.zeros_like(in_acc)
    mid_acc[...] = jnp.zeros_like(mid_acc)

    def lanes(p):
        return slice(p * WIDE, (p + 1) * WIDE)

    def put_rows(ref, first, values):
        parts = [values[:, i * N : (i + 1) * N].reshape(PEERS, ROWS, N) for i in range(2)]
        ref[:, first : first + 2 * ROWS, :] = jnp.concatenate(parts, axis=1).astype(BF16)

    def get_rows(ref, first):
        block = ref[:, first : first + 2 * ROWS, :].astype(F32)
        return jnp.concatenate([block[:, i * ROWS : (i + 1) * ROWS].reshape(N, N) for i in range(2)], axis=1)

    def project(l, p, state, left_ref, right_ref, left_row, right_row):
        at = lanes(p)
        unit_p, inverse_p = norm_forward(state)
        normed_p = (unit_p * gains[2 * l]).astype(BF16)
        unit[l, :, at] = unit_p
        inverse[l, :, at] = inverse_p
        normed[l, :, at] = normed_p
        projected = nn(weight_t[l], normed_p)
        sig = sigmoid(projected[0:N])
        val = projected[N : 2 * N]
        sig_l[l, :, at] = sig
        val_l[l, :, at] = val
        put_rows(left_ref, left_row, sig * val)
        sig = sigmoid(projected[2 * N : 3 * N])
        val = projected[3 * N : 4 * N]
        sig_r[l, :, at] = sig
        val_r[l, :, at] = val
        put_rows(right_ref, right_row, sig * val)
        gate[l, :, at] = projected[4 * N :]

    def after_project(l):
        for p in range(STEPS):
            at = lanes(p)
            gate_p = sigmoid(gate[l, :, at])
            gate[l, :, at] = gate_p
            for sig, val in ((sig_l, val_l), (sig_r, val_r)):
                sig_p = sig[l, :, at]
                val[l, :, at] = val[l, :, at] * sig_p * (1.0 - sig_p)
            if l == 1:
                gate_der[0, :, at] = output[:, at] * gate[0, :, at] * (1.0 - gate[0, :, at])
                cot_p = cot[:, at]
                gate_der[1, :, at] = cot_p * gate_p * (1.0 - gate_p)
                go_p = (cot_p * gate_p).astype(BF16)
                go[1, :, at] = go_p
                grad_mixed_p = nn(out_weight[1], go_p)
                grad_mixed[:, at] = grad_mixed_p
                scaled_p = grad_mixed_p * gains[3]
                scaled[:, at] = scaled_p
                scaled_mean[:, at] = mean_channels(scaled_p)

    def steps(h):
        return range(h * PER, (h + 1) * PER)

    def send2_part(slot, phase, h):
        send_part(phase, h, lambda d: send2.at[slot, h, d], recv2.at[slot, h, me])
        recv2[slot, h, me] = send2[slot, h, me]

    def send1_part(slot, phase, h):
        send_part(phase, h, lambda d: send1.at[slot, h, d], recv1.at[slot, h, me])
        recv1[slot, h, me] = send1[slot, h, me]

    def wait2_part(slot, phase, h):
        wait_part(phase, h, recv2.at[slot, h])

    def wait1_part(slot, phase, h):
        wait_part(phase, h, recv1.at[slot, h])

    def part_rows(d, h):
        return slice(d * ROWS * ROWS + h * PART, d * ROWS * ROWS + (h + 1) * PART)

    def part_of(h):
        return pl.ds(h * PART, PART)

    def own_part(d, h):
        first = h * PEERS * PART + d * PART
        return slice(first, first + PART)

    def channel_part(c, h):
        return pl.ds(h * PEERS * PART + c, N // CHUNKS, stride=ROWS)

    def half(h):
        return slice(h * N // CHUNKS, (h + 1) * N // CHUNKS)

    def channel(c):
        return pl.ds(c, N, stride=ROWS)

    def channel_forward_0():
        wait_part(RIGHT_0, 0, recv2.at[0, 0])
        for s in range(PEERS):
            turn_b[s * 64 : s * 64 + 64, :] = recv2[0, 0, s].astype(F32)
        for c in range(ROWS):
            chan_r[0, c] = turn_b[channel(c), :].astype(BF16)
        for h in range(CHUNKS):
            wait_part(TO_CH_0, h, recv2.at[0, 1, :, part_of(h)])
            for s in range(PEERS):
                turn_a[own_part(s, h), :] = recv2[0, 1, s, h * PART : (h + 1) * PART].astype(F32)
            for c in range(ROWS):
                left = turn_a[channel_part(c, h), :].astype(BF16)
                chan_l[0, c, half(h)] = left
                turn_a[channel_part(c, h), :] = nt(left, chan_r[0, c])
            for d in range(PEERS):
                send1[0, h, d] = turn_a[own_part(d, h), :].astype(BF16)
            send1_part(0, TO_ROW_0, h)

    def channel_forward_1():
        for h in range(CHUNKS):
            wait2_part(1, TO_CH_1, h)
            for s in range(PEERS):
                turn_a[part_rows(s, h), :] = recv2[1, h, s, :PART].astype(F32)
                turn_b[part_rows(s, h), :] = recv2[1, h, s, PART:].astype(F32)
        for c in range(ROWS):
            left = turn_a[channel(c), :].astype(BF16)
            right = turn_b[channel(c), :].astype(BF16)
            chan_l[1, c] = left
            chan_r[1, c] = right
            turn_a[channel(c), :] = tn(left, right)
        for h in range(CHUNKS):
            for d in range(PEERS):
                send1[1, h, d] = turn_a[part_rows(d, h), :].astype(BF16)
            send1_part(1, TO_ROW_1, h)

    def channel_backward_1():
        for h in range(CHUNKS):
            wait1_part(2, GRAD_CH_1, h)
            for s in range(PEERS):
                turn_a[part_rows(s, h), :] = recv1[2, h, s].astype(F32)
        for c in range(ROWS):
            grad = turn_a[channel(c), :].astype(BF16)
            turn_a[channel(c), :] = nt(chan_r[1, c], grad)
            turn_b[channel(c), :] = nn(chan_l[1, c], grad)
        for h in range(CHUNKS):
            for d in range(PEERS):
                send2[2, h, d, :PART] = turn_a[part_rows(d, h), :].astype(BF16)
                send2[2, h, d, PART:] = turn_b[part_rows(d, h), :].astype(BF16)
            send2_part(2, GRAD_ROW_1, h)

    def channel_backward_0():
        left_rows = pl.ds(0, PART)
        for h in range(CHUNKS):
            wait1_part(3, GRAD_CH_0, h)
            for s in range(PEERS):
                turn_a[own_part(s, h), :] = recv1[3, h, s].astype(F32)
            for c in range(ROWS):
                grad = turn_a[channel_part(c, h), :].astype(BF16)
                chan_g[c, half(h)] = grad
                turn_b[channel_part(c, h), :] = nn(grad, chan_r[0, c])
            for d in range(PEERS):
                send2[3, h, d, :PART] = turn_b[own_part(d, h), :].astype(BF16)
            if h == 0:
                send_part(GRAD_LEFT_0, 0, lambda d: send2.at[3, 0, d, left_rows], recv2.at[3, 0, me, left_rows])
        for c in range(ROWS):
            turn_a[channel(c), :] = tn(chan_g[c], chan_l[0, c])
        for h in range(CHUNKS):
            for d in range(PEERS):
                send2[3, h, d, PART:] = turn_a[part_rows(d, h), :].astype(BF16)
            if h == 0:
                right_rows = pl.ds(PART, PART)
                send_part(GRAD_ROW_0, 0, lambda d: send2.at[3, 0, d, right_rows], recv2.at[3, 0, me, right_rows])
                recv2[3, 0, me] = send2[3, 0, me]
            else:
                send2_part(3, GRAD_ROW_0, h)

    def fold(values):
        return values[:, :N] + values[:, N:]

    def back_pieces(l, p, ref):
        at = lanes(p)
        row = 2 * ROWS * (p % PER)
        for side, (sig, val) in enumerate(((sig_l, val_l), (sig_r, val_r))):
            grad = get_rows(ref, side * PART + row)
            first = 2 * N * side
            gp[l, first : first + N, at] = (grad * val[l, :, at]).astype(BF16)
            gp[l, first + N : first + 2 * N, at] = (grad * sig[l, :, at]).astype(BF16)

    def back_tail(l, p, gradient):
        at = lanes(p)
        grad_normed_p = nn(weight[l], gp[l, :, at])
        unit_p = unit[l, :, at]
        if l == 1:
            grad_normed[:, at] = grad_normed_p
        else:
            in_acc[l] += fold(grad_normed_p * unit_p)
        return gradient + norm_backward(grad_normed_p * gains[2 * l], unit_p, inverse[l, :, at])

    loads[0].wait()
    for a in range(ROWS):
        state0[:, a * N : (a + 1) * N] = pair_in[a].astype(F32).T
    for load in loads[1:4]:
        load.wait()

    def set_gain(index, source, l):
        row = jnp.broadcast_to(source[l : l + 1, :], (N, N)).T
        gains[index] = jnp.concatenate([row, row], axis=1)

    def set_weights(l):
        set_gain(2 * l, in_gain, l)
        for f in range(4):
            block = proj_weight[l, :, f * N : (f + 1) * N]
            weight[l, :, f * N : (f + 1) * N] = block
            weight_t[l, f * N : (f + 1) * N, :] = block.astype(F32).T.astype(BF16)
        weight[l, :, 4 * N :] = gate_weight[l]
        weight_t[l, 4 * N :, :] = gate_weight[l].astype(F32).T.astype(BF16)

    set_weights(0)
    for p in range(STEPS):
        project(0, p, state0[:, lanes(p)], send2.at[0, 1], send2.at[0, 0], 2 * ROWS * p, 2 * ROWS * p)
    pl.semaphore_wait(barrier, PEERS - 1)
    send_part(RIGHT_0, 0, lambda d: send2.at[0, 0, d], recv2.at[0, 0, me])
    for h in range(CHUNKS):
        rows = part_of(h)
        send_part(TO_CH_0, h, lambda d: send2.at[0, 1, d, rows], recv2.at[0, 1, me, rows])
    for i in range(2):
        recv2[0, i, me] = send2[0, i, me]

    for load in loads[4:]:
        load.wait()
    set_weights(1)
    for l in range(2):
        set_gain(2 * l + 1, mid_gain, l)
        out_t[l] = out_weight[l].astype(F32).T.astype(BF16)
    for a in range(ROWS):
        cot[:, a * N : (a + 1) * N] = cotangent[a].astype(F32).T

    after_project(0)

    channel_forward_0()

    for h in range(CHUNKS):
        wait1_part(0, TO_ROW_0, h)
        for p in steps(h):
            at = lanes(p)
            mix_unit_p, mix_inverse_p = norm_forward(get_rows(recv1.at[0, h], 2 * ROWS * (p % PER)))
            mixed_p = (mix_unit_p * gains[1]).astype(BF16)
            mix_unit[0, :, at] = mix_unit_p
            mix_inverse[:, at] = mix_inverse_p
            mixed[0, :, at] = mixed_p
            output_p = nn(out_t[0], mixed_p)
            output[:, at] = output_p
            state = (state0[:, at] + gate[0, :, at] * output_p).astype(BF16).astype(F32)
            row = 2 * ROWS * (p % PER)
            project(1, p, state, send2.at[1, h], send2.at[1, h], row, PART + row)
        send2_part(1, TO_CH_1, h)

    after_project(1)

    channel_forward_1()

    for h in range(CHUNKS):
        wait1_part(1, TO_ROW_1, h)
        for p in steps(h):
            at = lanes(p)
            row = 2 * ROWS * (p % PER)
            mix_unit_p, mix_inverse_p = norm_forward(get_rows(recv1.at[1, h], row))
            mix_unit[1, :, at] = mix_unit_p
            scaled_p = scaled[:, at]
            mean_two = mean_channels(scaled_p * mix_unit_p)
            put_rows(send1.at[2, h], row, mix_inverse_p * (scaled_p - scaled_mean[:, at] - mix_unit_p * mean_two))
        send1_part(2, GRAD_CH_1, h)

    for p in range(STEPS):
        at = lanes(p)
        mix_unit_p = mix_unit[1, :, at]
        mixed_p = (mix_unit_p * gains[3]).astype(BF16)
        mixed[1, :, at] = mixed_p
        gp[1, 4 * N :, at] = (gate_der[1, :, at] * nn(out_t[1], mixed_p)).astype(BF16)
        mid_acc[1] += fold(grad_mixed[:, at] * mix_unit_p)

    channel_backward_1()

    for h in range(CHUNKS):
        wait2_part(2, GRAD_ROW_1, h)
        for p in steps(h):
            at = lanes(p)
            back_pieces(1, p, recv2.at[2, h])
            gradient = back_tail(1, p, cot[:, at])
            grad1[:, at] = gradient
            go_p = (gradient * gate[0, :, at]).astype(BF16)
            go[0, :, at] = go_p
            grad_mixed_p = nn(out_weight[0], go_p)
            grad_mixed[:, at] = grad_mixed_p
            grad_product = norm_backward(grad_mixed_p * gains[1], mix_unit[0, :, at], mix_inverse[:, at])
            put_rows(send1.at[3, h], 2 * ROWS * (p % PER), grad_product)
        send1_part(3, GRAD_CH_0, h)

    for p in range(STEPS):
        at = lanes(p)
        gp[0, 4 * N :, at] = (grad1[:, at] * gate_der[0, :, at]).astype(BF16)
        mid_acc[0] += fold(grad_mixed[:, at] * mix_unit[0, :, at])
        in_acc[1] += fold(grad_normed[:, at] * unit[1, :, at])

    def put_early(first, values):
        for i in range(N // 64):
            sum_early_send[i, first // 2] = values[64 * i : 64 * i + 64, :].astype(BF16)

    for f in range(5):
        put_early(2 * f, nt(normed[1], gp[1, f * N : (f + 1) * N, :]))
    put_early(10, nt(mixed[1], go[1]))
    put_early(12, nt(normed[0], gp[0, 4 * N :, :]))
    put_early(14, nt(mixed[0], go[0]))
    send_part(PRE_EARLY, 0, lambda d: sum_early_send.at[1 - my_core], pre_early, [peer(1)])

    channel_backward_0()
    wait_bytes(PRE_EARLY, recv_sem, pre_early)
    sum_early_mid[...] = (sum_early_send[my_core].astype(F32) + pre_early[...].astype(F32)).astype(BF16)
    send_part(SUM_EARLY, 0, lambda d: sum_early_mid.at[d // 2], sum_early_recv.at[chip], same_core)
    sum_early_recv[chip] = sum_early_mid[chip]

    def last_rows(p):
        gradient = back_tail(0, p, grad1[:, lanes(p)])
        for i in range(2):
            pair_grad[2 * p + i] = gradient[:, i * N : (i + 1) * N].T.astype(BF16)

    for h in range(CHUNKS):
        if h == 0:
            wait_part(GRAD_LEFT_0, 0, recv2.at[3, 0, :, pl.ds(0, PART)])
            wait_part(GRAD_ROW_0, 0, recv2.at[3, 0, :, pl.ds(PART, PART)])
        else:
            wait2_part(3, GRAD_ROW_0, h)
        for p in steps(h):
            back_pieces(0, p, recv2.at[3, h])
        if h < CHUNKS - 1:
            for p in steps(h):
                last_rows(p)

    for f in range(4):
        values = nt(normed[0], gp[0, f * N : (f + 1) * N, :])
        for i in range(4):
            sum_late_send[4 * f + i] = values[32 * i : 32 * i + 32, :].astype(BF16)
    send_part(SUM_LATE, 0, lambda d: sum_late_send.at[d], sum_late_recv.at[me])
    sum_late_recv[me] = sum_late_send[me]

    wait_bytes(SUM_EARLY, recv_sem, sum_early_recv.at[pl.ds(0, 7)])
    all_early[my_core, chip] = jnp.sum(sum_early_recv[...].astype(F32), axis=0).astype(BF16)
    mine = all_early.at[my_core, chip]
    send_part(ALL_EARLY, 0, lambda d: mine, mine, same_core)

    for p in steps(CHUNKS - 1):
        last_rows(p)

    gain_rows = [jnp.sum(ref[l].T, axis=0, keepdims=True) for ref in (in_acc, mid_acc) for l in range(2)]
    gains_all[me] = jnp.concatenate(gain_rows + [jnp.zeros((4, N), F32)], axis=0)
    send_part(GAINS, 0, lambda d: gains_all.at[me], gains_all.at[me])

    wait_part(SUM_LATE, 0, sum_late_recv)
    all_late[me] = jnp.sum(sum_late_recv[...].astype(F32), axis=0).astype(BF16)
    send_part(ALL_LATE, 0, lambda d: all_late.at[me], all_late.at[me])

    wait_bytes(ALL_EARLY, recv_sem, all_early.at[0, pl.ds(0, 7)])
    send_part(SHARE_EARLY, 0, lambda d: all_early.at[my_core], all_early.at[my_core], [peer(1)])
    for h in range(CHUNKS):
        wait_sent(TO_CH_0, h, send2.at[0, 1, :, part_of(h)])
        wait_sent(TO_ROW_0, h, send1.at[0, h])
        for slot, two, one in ((1, TO_CH_1, TO_ROW_1), (2, GRAD_ROW_1, GRAD_CH_1)):
            wait_sent(two, h, send2.at[slot, h])
            wait_sent(one, h, send1.at[slot, h])
    wait_sent(RIGHT_0, 0, send2.at[0, 0])
    wait_sent(GRAD_LEFT_0, 0, send2.at[3, 0, :, pl.ds(0, PART)])
    wait_sent(GRAD_ROW_0, 0, send2.at[3, 0, :, pl.ds(PART, PART)])
    wait_sent(GRAD_ROW_0, 1, send2.at[3, 1])
    for h in range(CHUNKS):
        wait_sent(GRAD_CH_0, h, send1.at[3, h])
    wait_bytes(PRE_EARLY, send_sem, pre_early)
    wait_bytes(SUM_EARLY, send_sem, sum_early_mid.at[pl.ds(0, 7)])
    wait_bytes(ALL_EARLY, send_sem, all_early.at[0, pl.ds(0, 7)])
    wait_sent(SUM_LATE, 0, sum_late_send)
    wait_sent(GAINS, 0, gains_all)

    wait_bytes(SHARE_EARLY, recv_sem, all_early.at[0])
    early_out[...] = all_early[...]
    wait_bytes(SHARE_EARLY, send_sem, all_early.at[0])

    wait_part(GAINS, 0, gains_all)
    gains_out[...] = jnp.sum(gains_all[...], axis=0)

    wait_part(ALL_LATE, 0, all_late)
    late_out[...] = all_late[...]
    wait_sent(ALL_LATE, 0, all_late)


def write_kernel(
    pair, early_in, late_in, gains_in,
    pair_grad, proj_grad, gate_grad, out_grad, in_gain_grad, mid_gain_grad,
):
    scale = 1.0 / N
    pair_grad[...] = pair[...]

    def early(first):
        return early_in[:, first // 2].astype(F32).reshape(N, N) * scale

    for f in range(4):
        proj_grad[0, :, f * N : (f + 1) * N] = late_in[4 * f : 4 * f + 4].astype(F32).reshape(N, N) * scale
        proj_grad[1, :, f * N : (f + 1) * N] = early(2 * f)
    gate_grad[1] = early(8)
    out_grad[1] = early(10)
    gate_grad[0] = early(12)
    out_grad[0] = early(14)
    in_gain_grad[...] = gains_in[0:2, :] * scale
    mid_gain_grad[...] = gains_in[2:4, :] * scale


def on_device(*arrays):
    layer_f32 = pltpu.VMEM((2, N, CELLS), F32)
    layer_bf16 = pltpu.VMEM((2, N, CELLS), BF16)
    plain_f32 = pltpu.VMEM((N, CELLS), F32)
    vmem = pl.BlockSpec(memory_space=pltpu.VMEM)
    results = pl.pallas_call(
        kernel,
        out_shape=(
            pltpu.VMEM((ROWS, N, N), BF16),
            pltpu.VMEM((2, PEERS // 2, 64, N), BF16),
            pltpu.VMEM((PEERS, 32, N), BF16),
            pltpu.VMEM((8, N), F32),
        ),
        in_specs=[pl.BlockSpec(memory_space=pl.ANY)] * 7,
        out_specs=[vmem] * 4,
        scratch_shapes=[pltpu.VMEM(array.shape, array.dtype) for array in arrays] + [
            pltpu.VMEM((4, N, WIDE), F32),
            pltpu.VMEM((2, N, 5 * N), BF16),
            pltpu.VMEM((2, 5 * N, N), BF16),
            pltpu.VMEM((2, N, N), BF16),
            plain_f32, plain_f32, plain_f32,
            layer_f32,
            pltpu.VMEM((2, 1, CELLS), F32),
            layer_bf16,
            layer_f32, layer_f32, layer_f32, layer_f32,
            layer_f32, layer_f32, plain_f32, layer_f32,
            pltpu.VMEM((1, CELLS), F32),
            layer_bf16,
            plain_f32, plain_f32,
            pltpu.VMEM((1, CELLS), F32),
            plain_f32,
            layer_bf16,
            pltpu.VMEM((2, 5 * N, CELLS), BF16),
            pltpu.VMEM((2, N, N), F32),
            pltpu.VMEM((2, N, N), F32),
            pltpu.VMEM((CELLS, N), F32),
            pltpu.VMEM((CELLS, N), F32),
            pltpu.VMEM((2, ROWS, N, N), BF16),
            pltpu.VMEM((2, ROWS, N, N), BF16),
            pltpu.VMEM((ROWS, N, N), BF16),
            pltpu.VMEM((4, CHUNKS, PEERS, 2 * PART, N), BF16),
            pltpu.VMEM((4, CHUNKS, PEERS, 2 * PART, N), BF16),
            pltpu.VMEM((4, CHUNKS, PEERS, PART, N), BF16),
            pltpu.VMEM((4, CHUNKS, PEERS, PART, N), BF16),
            pltpu.VMEM((2, PEERS // 2, 64, N), BF16),
            pltpu.VMEM((PEERS // 2, 64, N), BF16),
            pltpu.VMEM((PEERS // 2, 64, N), BF16),
            pltpu.VMEM((PEERS // 2, 64, N), BF16),
            pltpu.VMEM((2, PEERS // 2, 64, N), BF16),
            pltpu.VMEM((PEERS, 32, N), BF16),
            pltpu.VMEM((PEERS, 32, N), BF16),
            pltpu.VMEM((PEERS, 32, N), BF16),
            pltpu.VMEM((PEERS, 8, N), F32),
            pltpu.SemaphoreType.DMA((7,)),
            pltpu.SemaphoreType.DMA((PHASES * CHUNKS,)),
            pltpu.SemaphoreType.DMA((PHASES * CHUNKS,)),
        ],
        compiler_params=pltpu.CompilerParams(
            collective_id=0, has_side_effects=True, vmem_limit_bytes=56 * 1024 * 1024
        ),
    )(*arrays)
    return pl.pallas_call(
        write_kernel,
        out_shape=(
            jax.ShapeDtypeStruct((ROWS, N, N), BF16),
            jax.ShapeDtypeStruct((2, N, 4 * N), F32),
            jax.ShapeDtypeStruct((2, N, N), F32),
            jax.ShapeDtypeStruct((2, N, N), F32),
            jax.ShapeDtypeStruct((2, N), F32),
            jax.ShapeDtypeStruct((2, N), F32),
        ),
        in_specs=[vmem] * 4,
        out_specs=[vmem] * 6,
        compiler_params=pltpu.CompilerParams(vmem_limit_bytes=4 * 1024 * 1024),
    )(*results)


def solution(mesh):
    return jax.shard_map(
        on_device,
        mesh=mesh,
        in_specs=(
            P(("dp", "pair"), None, None),
            P(("dp", "pair"), None, None),
            P(),
            P(),
            P(),
            P(),
            P(),
        ),
        out_specs=(
            P(("dp", "pair"), None, None),
            P("dp", None, None),
            P("dp", None, None),
            P("dp", None, None),
            P("dp", None),
            P("dp", None),
        ),
        check_vma=False,
    )
```

```python
import functools

import jax
import jax.numpy as jnp
from jax import lax
from jax.experimental import pallas as pl
from jax.experimental.pallas import tpu as pltpu
from jax.sharding import PartitionSpec as P

EPSILON = 1e-05
MESH = pl.DeviceIdType.MESH
F32 = jnp.float32
BF16 = jnp.bfloat16

N = 128
PEERS = 16
ROWS = N // PEERS
CELLS = ROWS * N
WIDE = 2 * N
STEPS = CELLS // WIDE
CHUNKS = 2
PER = STEPS // CHUNKS
PART = ROWS * ROWS // CHUNKS

TO_CH_0, TO_ROW_0, TO_CH_1, TO_ROW_1, GRAD_CH_1, GRAD_ROW_1, GRAD_CH_0, GRAD_ROW_0 = range(8)
SUM_EARLY, ALL_EARLY, SUM_LATE, ALL_LATE, GAINS, RIGHT_0, GRAD_LEFT_0, PRE_EARLY, SHARE_EARLY = range(8, 17)
PHASES = 17


def dot(first, second, dims):
    return lax.dot_general(first, second, (dims, ((), ())), preferred_element_type=F32)


def nn(first, second):
    return dot(first, second, ((1,), (0,)))


def nt(first, second):
    return dot(first, second, ((1,), (1,)))


def tn(first, second):
    return dot(first, second, ((0,), (0,)))


def sigmoid(values):
    return 0.5 * jnp.tanh(0.5 * values) + 0.5


def mean_channels(values):
    return jnp.sum(values, axis=0, keepdims=True) * (1.0 / N)


def norm_forward(values):
    shifted = values - mean_channels(values)
    inverse = lax.rsqrt(mean_channels(shifted * shifted) + EPSILON)
    return shifted * inverse, inverse


def norm_backward(scaled, unit, inverse):
    return inverse * (scaled - mean_channels(scaled) - unit * mean_channels(scaled * unit))


def kernel(
    pair_hbm, cot_hbm, in_gain_hbm, proj_weight_hbm, gate_weight_hbm, mid_gain_hbm, out_weight_hbm,
    pair_grad, early_out, late_out, gains_out,
    pair_in, cotangent, in_gain, proj_weight, gate_weight, mid_gain, out_weight,
    gains, weight, weight_t, out_t,
    state0, cot, grad1,
    unit, inverse, normed, sig_l, val_l, sig_r, val_r, gate, gate_der, output, mix_unit, mix_inverse, mixed,
    grad_mixed, scaled, scaled_mean, grad_normed,
    go, gp, in_acc, mid_acc,
    turn_a, turn_b, chan_l, chan_r, chan_g,
    send2, recv2, send1, recv1,
    sum_early_send, pre_early, sum_early_mid, sum_early_recv, all_early, sum_late_send, sum_late_recv, all_late, gains_all,
    load_sem, send_sem, recv_sem,
):
    me = lax.axis_index("pair")
    my_x, my_y, my_core = me // 8, (me // 2) % 4, me % 2

    def peer(o):
        x = (my_x + o // 8) % 2
        y = (my_y + (o // 2) % 4) % 4
        core = (my_core + o % 2) % 2
        return x * 8 + y * 2 + core

    barrier = pltpu.get_barrier_semaphore()

    peers = [peer(o) for o in (4, 12, 5, 13, 2, 10, 6, 14, 3, 11, 7, 15, 8, 9, 1)]
    same_core = [peer(o) for o in (4, 12, 2, 10, 6, 14, 8)]
    chip = me // 2
    for target in peers:
        pl.semaphore_signal(barrier, inc=1, device_id={"pair": target}, device_id_type=MESH)

    loads = [
        pltpu.make_async_copy(source, target, load_sem.at[i])
        for i, (source, target) in enumerate((
            (pair_hbm, pair_in), (in_gain_hbm, in_gain), (proj_weight_hbm, proj_weight), (gate_weight_hbm, gate_weight),
            (mid_gain_hbm, mid_gain), (out_weight_hbm, out_weight), (cot_hbm, cotangent),
        ))
    ]
    for load in loads:
        load.start()

    def send_part(phase, h, src_of, dst, targets=None):
        sem = phase * CHUNKS + h
        for target in targets or peers:
            pltpu.make_async_remote_copy(
                src_ref=src_of(target), dst_ref=dst,
                send_sem=send_sem.at[sem], recv_sem=recv_sem.at[sem],
                device_id={"pair": target}, device_id_type=MESH,
            ).start()

    def wait_part(phase, h, slots):
        fifteen = slots.at[pl.ds(0, PEERS - 1)]
        pltpu.make_async_copy(fifteen, fifteen, recv_sem.at[phase * CHUNKS + h]).wait()

    def wait_bytes(phase, sems, some):
        pltpu.make_async_copy(some, some, sems.at[phase * CHUNKS]).wait()

    def wait_sent(phase, h, slots):
        fifteen = slots.at[pl.ds(0, PEERS - 1)]
        pltpu.make_async_copy(fifteen, fifteen, send_sem.at[phase * CHUNKS + h]).wait()

    in_acc[...] = jnp.zeros_like(in_acc)
    mid_acc[...] = jnp.zeros_like(mid_acc)

    def lanes(p):
        return slice(p * WIDE, (p + 1) * WIDE)

    def put_rows(ref, first, values):
        parts = [values[:, i * N : (i + 1) * N].reshape(PEERS, ROWS, N) for i in range(2)]
        ref[:, first : first + 2 * ROWS, :] = jnp.concatenate(parts, axis=1).astype(BF16)

    def get_rows(ref, first):
        block = ref[:, first : first + 2 * ROWS, :].astype(F32)
        return jnp.concatenate([block[:, i * ROWS : (i + 1) * ROWS].reshape(N, N) for i in range(2)], axis=1)

    def project(l, p, state, left_ref, right_ref, left_row, right_row):
        at = lanes(p)
        unit_p, inverse_p = norm_forward(state)
        normed_p = (unit_p * gains[2 * l]).astype(BF16)
        unit[l, :, at] = unit_p
        inverse[l, :, at] = inverse_p
        normed[l, :, at] = normed_p
        projected = nn(weight_t[l], normed_p)
        sig = sigmoid(projected[0:N])
        val = projected[N : 2 * N]
        sig_l[l, :, at] = sig
        val_l[l, :, at] = val
        put_rows(left_ref, left_row, sig * val)
        sig = sigmoid(projected[2 * N : 3 * N])
        val = projected[3 * N : 4 * N]
        sig_r[l, :, at] = sig
        val_r[l, :, at] = val
        put_rows(right_ref, right_row, sig * val)
        gate[l, :, at] = projected[4 * N :]

    def after_project(l):
        for p in range(STEPS):
            at = lanes(p)
            gate_p = sigmoid(gate[l, :, at])
            gate[l, :, at] = gate_p
            for sig, val in ((sig_l, val_l), (sig_r, val_r)):
                sig_p = sig[l, :, at]
                val[l, :, at] = val[l, :, at] * sig_p * (1.0 - sig_p)
            if l == 1:
                gate_der[0, :, at] = output[:, at] * gate[0, :, at] * (1.0 - gate[0, :, at])
                cot_p = cot[:, at]
                gate_der[1, :, at] = cot_p * gate_p * (1.0 - gate_p)
                go_p = (cot_p * gate_p).astype(BF16)
                go[1, :, at] = go_p
                grad_mixed_p = nn(out_weight[1], go_p)
                grad_mixed[:, at] = grad_mixed_p
                scaled_p = grad_mixed_p * gains[3]
                scaled[:, at] = scaled_p
                scaled_mean[:, at] = mean_channels(scaled_p)

    def steps(h):
        return range(h * PER, (h + 1) * PER)

    def send2_part(slot, phase, h):
        send_part(phase, h, lambda d: send2.at[slot, h, d], recv2.at[slot, h, me])
        recv2[slot, h, me] = send2[slot, h, me]

    def send1_part(slot, phase, h):
        send_part(phase, h, lambda d: send1.at[slot, h, d], recv1.at[slot, h, me])
        recv1[slot, h, me] = send1[slot, h, me]

    def wait2_part(slot, phase, h):
        wait_part(phase, h, recv2.at[slot, h])

    def wait1_part(slot, phase, h):
        wait_part(phase, h, recv1.at[slot, h])

    def part_rows(d, h):
        return slice(d * ROWS * ROWS + h * PART, d * ROWS * ROWS + (h + 1) * PART)

    def part_of(h):
        return pl.ds(h * PART, PART)

    def own_part(d, h):
        first = h * PEERS * PART + d * PART
        return slice(first, first + PART)

    def channel_part(c, h):
        return pl.ds(h * PEERS * PART + c, N // CHUNKS, stride=ROWS)

    def half(h):
        return slice(h * N // CHUNKS, (h + 1) * N // CHUNKS)

    def channel(c):
        return pl.ds(c, N, stride=ROWS)

    def channel_forward_0():
        wait_part(RIGHT_0, 0, recv2.at[0, 0])
        for s in range(PEERS):
            turn_b[s * 64 : s * 64 + 64, :] = recv2[0, 0, s].astype(F32)
        for c in range(ROWS):
            chan_r[0, c] = turn_b[channel(c), :].astype(BF16)
        for h in range(CHUNKS):
            wait_part(TO_CH_0, h, recv2.at[0, 1, :, part_of(h)])
            for s in range(PEERS):
                turn_a[own_part(s, h), :] = recv2[0, 1, s, h * PART : (h + 1) * PART].astype(F32)
            for c in range(ROWS):
                left = turn_a[channel_part(c, h), :].astype(BF16)
                chan_l[0, c, half(h)] = left
                turn_a[channel_part(c, h), :] = nt(left, chan_r[0, c])
            for d in range(PEERS):
                send1[0, h, d] = turn_a[own_part(d, h), :].astype(BF16)
            send1_part(0, TO_ROW_0, h)

    def channel_forward_1():
        for h in range(CHUNKS):
            wait2_part(1, TO_CH_1, h)
            for s in range(PEERS):
                turn_a[part_rows(s, h), :] = recv2[1, h, s, :PART].astype(F32)
                turn_b[part_rows(s, h), :] = recv2[1, h, s, PART:].astype(F32)
        for c in range(ROWS):
            left = turn_a[channel(c), :].astype(BF16)
            right = turn_b[channel(c), :].astype(BF16)
            chan_l[1, c] = left
            chan_r[1, c] = right
            turn_a[channel(c), :] = tn(left, right)
        for h in range(CHUNKS):
            for d in range(PEERS):
                send1[1, h, d] = turn_a[part_rows(d, h), :].astype(BF16)
            send1_part(1, TO_ROW_1, h)

    def channel_backward_1():
        for h in range(CHUNKS):
            wait1_part(2, GRAD_CH_1, h)
            for s in range(PEERS):
                turn_a[part_rows(s, h), :] = recv1[2, h, s].astype(F32)
        for c in range(ROWS):
            grad = turn_a[channel(c), :].astype(BF16)
            turn_a[channel(c), :] = nt(chan_r[1, c], grad)
            turn_b[channel(c), :] = nn(chan_l[1, c], grad)
        for h in range(CHUNKS):
            for d in range(PEERS):
                send2[2, h, d, :PART] = turn_a[part_rows(d, h), :].astype(BF16)
                send2[2, h, d, PART:] = turn_b[part_rows(d, h), :].astype(BF16)
            send2_part(2, GRAD_ROW_1, h)

    def channel_backward_0():
        left_rows = pl.ds(0, PART)
        for h in range(CHUNKS):
            wait1_part(3, GRAD_CH_0, h)
            for s in range(PEERS):
                turn_a[own_part(s, h), :] = recv1[3, h, s].astype(F32)
            for c in range(ROWS):
                grad = turn_a[channel_part(c, h), :].astype(BF16)
                chan_g[c, half(h)] = grad
                turn_b[channel_part(c, h), :] = nn(grad, chan_r[0, c])
            for d in range(PEERS):
                send2[3, h, d, :PART] = turn_b[own_part(d, h), :].astype(BF16)
            if h == 0:
                send_part(GRAD_LEFT_0, 0, lambda d: send2.at[3, 0, d, left_rows], recv2.at[3, 0, me, left_rows])
        for c in range(ROWS):
            turn_a[channel(c), :] = tn(chan_g[c], chan_l[0, c])
        for h in range(CHUNKS):
            for d in range(PEERS):
                send2[3, h, d, PART:] = turn_a[part_rows(d, h), :].astype(BF16)
            if h == 0:
                right_rows = pl.ds(PART, PART)
                send_part(GRAD_ROW_0, 0, lambda d: send2.at[3, 0, d, right_rows], recv2.at[3, 0, me, right_rows])
                recv2[3, 0, me] = send2[3, 0, me]
            else:
                send2_part(3, GRAD_ROW_0, h)

    def fold(values):
        return values[:, :N] + values[:, N:]

    def back_pieces(l, p, ref):
        at = lanes(p)
        row = 2 * ROWS * (p % PER)
        for side, (sig, val) in enumerate(((sig_l, val_l), (sig_r, val_r))):
            grad = get_rows(ref, side * PART + row)
            first = 2 * N * side
            gp[l, first : first + N, at] = (grad * val[l, :, at]).astype(BF16)
            gp[l, first + N : first + 2 * N, at] = (grad * sig[l, :, at]).astype(BF16)

    def back_tail(l, p, gradient):
        at = lanes(p)
        grad_normed_p = nn(weight[l], gp[l, :, at])
        unit_p = unit[l, :, at]
        if l == 1:
            grad_normed[:, at] = grad_normed_p
        else:
            in_acc[l] += fold(grad_normed_p * unit_p)
        return gradient + norm_backward(grad_normed_p * gains[2 * l], unit_p, inverse[l, :, at])

    loads[0].wait()
    for a in range(ROWS):
        state0[:, a * N : (a + 1) * N] = pair_in[a].astype(F32).T
    for load in loads[1:4]:
        load.wait()

    def set_gain(index, source, l):
        row = jnp.broadcast_to(source[l : l + 1, :], (N, N)).T
        gains[index] = jnp.concatenate([row, row], axis=1)

    def set_weights(l):
        set_gain(2 * l, in_gain, l)
        for f in range(4):
            block = proj_weight[l, :, f * N : (f + 1) * N]
            weight[l, :, f * N : (f + 1) * N] = block
            weight_t[l, f * N : (f + 1) * N, :] = block.astype(F32).T.astype(BF16)
        weight[l, :, 4 * N :] = gate_weight[l]
        weight_t[l, 4 * N :, :] = gate_weight[l].astype(F32).T.astype(BF16)

    set_weights(0)
    for p in range(STEPS):
        project(0, p, state0[:, lanes(p)], send2.at[0, 1], send2.at[0, 0], 2 * ROWS * p, 2 * ROWS * p)
    pl.semaphore_wait(barrier, PEERS - 1)
    send_part(RIGHT_0, 0, lambda d: send2.at[0, 0, d], recv2.at[0, 0, me])
    for h in range(CHUNKS):
        rows = part_of(h)
        send_part(TO_CH_0, h, lambda d: send2.at[0, 1, d, rows], recv2.at[0, 1, me, rows])
    for i in range(2):
        recv2[0, i, me] = send2[0, i, me]

    for load in loads[4:]:
        load.wait()
    set_weights(1)
    for l in range(2):
        set_gain(2 * l + 1, mid_gain, l)
        out_t[l] = out_weight[l].astype(F32).T.astype(BF16)
    for a in range(ROWS):
        cot[:, a * N : (a + 1) * N] = cotangent[a].astype(F32).T

    after_project(0)

    channel_forward_0()

    for h in range(CHUNKS):
        wait1_part(0, TO_ROW_0, h)
        for p in steps(h):
            at = lanes(p)
            mix_unit_p, mix_inverse_p = norm_forward(get_rows(recv1.at[0, h], 2 * ROWS * (p % PER)))
            mixed_p = (mix_unit_p * gains[1]).astype(BF16)
            mix_unit[0, :, at] = mix_unit_p
            mix_inverse[:, at] = mix_inverse_p
            mixed[0, :, at] = mixed_p
            output_p = nn(out_t[0], mixed_p)
            output[:, at] = output_p
            state = (state0[:, at] + gate[0, :, at] * output_p).astype(BF16).astype(F32)
            row = 2 * ROWS * (p % PER)
            project(1, p, state, send2.at[1, h], send2.at[1, h], row, PART + row)
        send2_part(1, TO_CH_1, h)

    after_project(1)

    channel_forward_1()

    for h in range(CHUNKS):
        wait1_part(1, TO_ROW_1, h)
        for p in steps(h):
            at = lanes(p)
            row = 2 * ROWS * (p % PER)
            mix_unit_p, mix_inverse_p = norm_forward(get_rows(recv1.at[1, h], row))
            mix_unit[1, :, at] = mix_unit_p
            scaled_p = scaled[:, at]
            mean_two = mean_channels(scaled_p * mix_unit_p)
            put_rows(send1.at[2, h], row, mix_inverse_p * (scaled_p - scaled_mean[:, at] - mix_unit_p * mean_two))
        send1_part(2, GRAD_CH_1, h)

    for p in range(STEPS):
        at = lanes(p)
        mix_unit_p = mix_unit[1, :, at]
        mixed_p = (mix_unit_p * gains[3]).astype(BF16)
        mixed[1, :, at] = mixed_p
        gp[1, 4 * N :, at] = (gate_der[1, :, at] * nn(out_t[1], mixed_p)).astype(BF16)
        mid_acc[1] += fold(grad_mixed[:, at] * mix_unit_p)

    channel_backward_1()

    for h in range(CHUNKS):
        wait2_part(2, GRAD_ROW_1, h)
        for p in steps(h):
            at = lanes(p)
            back_pieces(1, p, recv2.at[2, h])
            gradient = back_tail(1, p, cot[:, at])
            grad1[:, at] = gradient
            go_p = (gradient * gate[0, :, at]).astype(BF16)
            go[0, :, at] = go_p
            grad_mixed_p = nn(out_weight[0], go_p)
            grad_mixed[:, at] = grad_mixed_p
            grad_product = norm_backward(grad_mixed_p * gains[1], mix_unit[0, :, at], mix_inverse[:, at])
            put_rows(send1.at[3, h], 2 * ROWS * (p % PER), grad_product)
        send1_part(3, GRAD_CH_0, h)

    for p in range(STEPS):
        at = lanes(p)
        gp[0, 4 * N :, at] = (grad1[:, at] * gate_der[0, :, at]).astype(BF16)
        mid_acc[0] += fold(grad_mixed[:, at] * mix_unit[0, :, at])
        in_acc[1] += fold(grad_normed[:, at] * unit[1, :, at])

    def put_early(first, values):
        for i in range(N // 64):
            sum_early_send[i, first // 2] = values[64 * i : 64 * i + 64, :].astype(BF16)

    for f in range(5):
        put_early(2 * f, nt(normed[1], gp[1, f * N : (f + 1) * N, :]))
    put_early(10, nt(mixed[1], go[1]))
    put_early(12, nt(normed[0], gp[0, 4 * N :, :]))
    put_early(14, nt(mixed[0], go[0]))
    send_part(PRE_EARLY, 0, lambda d: sum_early_send.at[1 - my_core], pre_early, [peer(1)])

    channel_backward_0()
    wait_bytes(PRE_EARLY, recv_sem, pre_early)
    sum_early_mid[...] = (sum_early_send[my_core].astype(F32) + pre_early[...].astype(F32)).astype(BF16)
    send_part(SUM_EARLY, 0, lambda d: sum_early_mid.at[d // 2], sum_early_recv.at[chip], same_core)
    sum_early_recv[chip] = sum_early_mid[chip]

    def last_rows(p):
        gradient = back_tail(0, p, grad1[:, lanes(p)])
        for i in range(2):
            pair_grad[2 * p + i] = gradient[:, i * N : (i + 1) * N].T.astype(BF16)

    for h in range(CHUNKS):
        if h == 0:
            wait_part(GRAD_LEFT_0, 0, recv2.at[3, 0, :, pl.ds(0, PART)])
            wait_part(GRAD_ROW_0, 0, recv2.at[3, 0, :, pl.ds(PART, PART)])
        else:
            wait2_part(3, GRAD_ROW_0, h)
        for p in steps(h):
            back_pieces(0, p, recv2.at[3, h])
        if h < CHUNKS - 1:
            for p in steps(h):
                last_rows(p)

    for f in range(4):
        values = nt(normed[0], gp[0, f * N : (f + 1) * N, :])
        for i in range(4):
            sum_late_send[4 * f + i] = values[32 * i : 32 * i + 32, :].astype(BF16)
    send_part(SUM_LATE, 0, lambda d: sum_late_send.at[d], sum_late_recv.at[me])
    sum_late_recv[me] = sum_late_send[me]

    wait_bytes(SUM_EARLY, recv_sem, sum_early_recv.at[pl.ds(0, 7)])
    all_early[my_core, chip] = jnp.sum(sum_early_recv[...].astype(F32), axis=0).astype(BF16)
    mine = all_early.at[my_core, chip]
    send_part(ALL_EARLY, 0, lambda d: mine, mine, same_core)

    for p in steps(CHUNKS - 1):
        last_rows(p)

    gain_rows = [jnp.sum(ref[l].T, axis=0, keepdims=True) for ref in (in_acc, mid_acc) for l in range(2)]
    gains_all[me] = jnp.concatenate(gain_rows + [jnp.zeros((4, N), F32)], axis=0)
    send_part(GAINS, 0, lambda d: gains_all.at[me], gains_all.at[me])

    wait_part(SUM_LATE, 0, sum_late_recv)
    all_late[me] = jnp.sum(sum_late_recv[...].astype(F32), axis=0).astype(BF16)
    send_part(ALL_LATE, 0, lambda d: all_late.at[me], all_late.at[me])

    wait_bytes(ALL_EARLY, recv_sem, all_early.at[0, pl.ds(0, 7)])
    send_part(SHARE_EARLY, 0, lambda d: all_early.at[my_core], all_early.at[my_core], [peer(1)])
    for h in range(CHUNKS):
        wait_sent(TO_CH_0, h, send2.at[0, 1, :, part_of(h)])
        wait_sent(TO_ROW_0, h, send1.at[0, h])
        for slot, two, one in ((1, TO_CH_1, TO_ROW_1), (2, GRAD_ROW_1, GRAD_CH_1)):
            wait_sent(two, h, send2.at[slot, h])
            wait_sent(one, h, send1.at[slot, h])
    wait_sent(RIGHT_0, 0, send2.at[0, 0])
    wait_sent(GRAD_LEFT_0, 0, send2.at[3, 0, :, pl.ds(0, PART)])
    wait_sent(GRAD_ROW_0, 0, send2.at[3, 0, :, pl.ds(PART, PART)])
    wait_sent(GRAD_ROW_0, 1, send2.at[3, 1])
    for h in range(CHUNKS):
        wait_sent(GRAD_CH_0, h, send1.at[3, h])
    wait_bytes(PRE_EARLY, send_sem, pre_early)
    wait_bytes(SUM_EARLY, send_sem, sum_early_mid.at[pl.ds(0, 7)])
    wait_bytes(ALL_EARLY, send_sem, all_early.at[0, pl.ds(0, 7)])
    wait_sent(SUM_LATE, 0, sum_late_send)
    wait_sent(GAINS, 0, gains_all)

    wait_bytes(SHARE_EARLY, recv_sem, all_early.at[0])
    early_out[...] = all_early[...]
    wait_bytes(SHARE_EARLY, send_sem, all_early.at[0])

    wait_part(GAINS, 0, gains_all)
    gains_out[...] = jnp.sum(gains_all[...], axis=0)

    wait_part(ALL_LATE, 0, all_late)
    late_out[...] = all_late[...]
    wait_sent(ALL_LATE, 0, all_late)


def write_kernel(
    pair, early_in, late_in, gains_in,
    pair_grad, proj_grad, gate_grad, out_grad, in_gain_grad, mid_gain_grad,
):
    scale = 1.0 / N
    pair_grad[...] = pair[...]

    def early(first):
        return early_in[:, first // 2].astype(F32).reshape(N, N) * scale

    for f in range(4):
        proj_grad[0, :, f * N : (f + 1) * N] = late_in[4 * f : 4 * f + 4].astype(F32).reshape(N, N) * scale
        proj_grad[1, :, f * N : (f + 1) * N] = early(2 * f)
    gate_grad[1] = early(8)
    out_grad[1] = early(10)
    gate_grad[0] = early(12)
    out_grad[0] = early(14)
    in_gain_grad[...] = gains_in[0:2, :] * scale
    mid_gain_grad[...] = gains_in[2:4, :] * scale


def on_device(*arrays):
    layer_f32 = pltpu.VMEM((2, N, CELLS), F32)
    layer_bf16 = pltpu.VMEM((2, N, CELLS), BF16)
    plain_f32 = pltpu.VMEM((N, CELLS), F32)
    vmem = pl.BlockSpec(memory_space=pltpu.VMEM)
    results = pl.pallas_call(
        kernel,
        out_shape=(
            pltpu.VMEM((ROWS, N, N), BF16),
            pltpu.VMEM((2, PEERS // 2, 64, N), BF16),
            pltpu.VMEM((PEERS, 32, N), BF16),
            pltpu.VMEM((8, N), F32),
        ),
        in_specs=[pl.BlockSpec(memory_space=pl.ANY)] * 7,
        out_specs=[vmem] * 4,
        scratch_shapes=[pltpu.VMEM(array.shape, array.dtype) for array in arrays] + [
            pltpu.VMEM((4, N, WIDE), F32),
            pltpu.VMEM((2, N, 5 * N), BF16),
            pltpu.VMEM((2, 5 * N, N), BF16),
            pltpu.VMEM((2, N, N), BF16),
            plain_f32, plain_f32, plain_f32,
            layer_f32,
            pltpu.VMEM((2, 1, CELLS), F32),
            layer_bf16,
            layer_f32, layer_f32, layer_f32, layer_f32,
            layer_f32, layer_f32, plain_f32, layer_f32,
            pltpu.VMEM((1, CELLS), F32),
            layer_bf16,
            plain_f32, plain_f32,
            pltpu.VMEM((1, CELLS), F32),
            plain_f32,
            layer_bf16,
            pltpu.VMEM((2, 5 * N, CELLS), BF16),
            pltpu.VMEM((2, N, N), F32),
            pltpu.VMEM((2, N, N), F32),
            pltpu.VMEM((CELLS + ROWS, N), F32),
            pltpu.VMEM((CELLS + ROWS, N), F32),
            pltpu.VMEM((2, ROWS, N, N), BF16),
            pltpu.VMEM((2, ROWS, N, N), BF16),
            pltpu.VMEM((ROWS, N, N), BF16),
            pltpu.VMEM((4, CHUNKS, PEERS, 2 * PART, N), BF16),
            pltpu.VMEM((4, CHUNKS, PEERS, 2 * PART, N), BF16),
            pltpu.VMEM((4, CHUNKS, PEERS, PART, N), BF16),
            pltpu.VMEM((4, CHUNKS, PEERS, PART, N), BF16),
            pltpu.VMEM((2, PEERS // 2, 64, N), BF16),
            pltpu.VMEM((PEERS // 2, 64, N), BF16),
            pltpu.VMEM((PEERS // 2, 64, N), BF16),
            pltpu.VMEM((PEERS // 2, 64, N), BF16),
            pltpu.VMEM((2, PEERS // 2, 64, N), BF16),
            pltpu.VMEM((PEERS, 32, N), BF16),
            pltpu.VMEM((PEERS, 32, N), BF16),
            pltpu.VMEM((PEERS, 32, N), BF16),
            pltpu.VMEM((PEERS, 8, N), F32),
            pltpu.SemaphoreType.DMA((7,)),
            pltpu.SemaphoreType.DMA((PHASES * CHUNKS,)),
            pltpu.SemaphoreType.DMA((PHASES * CHUNKS,)),
        ],
        compiler_params=pltpu.CompilerParams(
            collective_id=0, has_side_effects=True, vmem_limit_bytes=56 * 1024 * 1024
        ),
    )(*arrays)
    return pl.pallas_call(
        write_kernel,
        out_shape=(
            jax.ShapeDtypeStruct((ROWS, N, N), BF16),
            jax.ShapeDtypeStruct((2, N, 4 * N), F32),
            jax.ShapeDtypeStruct((2, N, N), F32),
            jax.ShapeDtypeStruct((2, N, N), F32),
            jax.ShapeDtypeStruct((2, N), F32),
            jax.ShapeDtypeStruct((2, N), F32),
        ),
        in_specs=[vmem] * 4,
        out_specs=[vmem] * 6,
        compiler_params=pltpu.CompilerParams(vmem_limit_bytes=4 * 1024 * 1024),
    )(*results)


def solution(mesh):
    return jax.shard_map(
        on_device,
        mesh=mesh,
        in_specs=(
            P(("dp", "pair"), None, None),
            P(("dp", "pair"), None, None),
            P(),
            P(),
            P(),
            P(),
            P(),
        ),
        out_specs=(
            P(("dp", "pair"), None, None),
            P("dp", None, None),
            P("dp", None, None),
            P("dp", None, None),
            P("dp", None),
            P("dp", None),
        ),
        check_vma=False,
    )
```

```python
import functools

import jax
import jax.numpy as jnp
from jax import lax
from jax.experimental import pallas as pl
from jax.experimental.pallas import tpu as pltpu
from jax.sharding import PartitionSpec as P

EPSILON = 1e-05
MESH = pl.DeviceIdType.MESH
F32 = jnp.float32
BF16 = jnp.bfloat16

N = 128
PEERS = 16
ROWS = N // PEERS
CELLS = ROWS * N
WIDE = 2 * N
STEPS = CELLS // WIDE
CHUNKS = 2
PER = STEPS // CHUNKS
PART = ROWS * ROWS // CHUNKS

TO_CH_0, TO_ROW_0, TO_CH_1, TO_ROW_1, GRAD_CH_1, GRAD_ROW_1, GRAD_CH_0, GRAD_ROW_0 = range(8)
SUM_EARLY, ALL_EARLY, SUM_LATE, ALL_LATE, GAINS, RIGHT_0, GRAD_LEFT_0, PRE_EARLY, SHARE_EARLY = range(8, 17)
PHASES = 17


def dot(first, second, dims):
    return lax.dot_general(first, second, (dims, ((), ())), preferred_element_type=F32)


def nn(first, second):
    return dot(first, second, ((1,), (0,)))


def nt(first, second):
    return dot(first, second, ((1,), (1,)))


def tn(first, second):
    return dot(first, second, ((0,), (0,)))


def sigmoid(values):
    return 0.5 * jnp.tanh(0.5 * values) + 0.5


def mean_channels(values):
    return jnp.sum(values, axis=0, keepdims=True) * (1.0 / N)


def norm_forward(values):
    shifted = values - mean_channels(values)
    inverse = lax.rsqrt(mean_channels(shifted * shifted) + EPSILON)
    return shifted * inverse, inverse


def norm_backward(scaled, unit, inverse):
    return inverse * (scaled - mean_channels(scaled) - unit * mean_channels(scaled * unit))


def kernel(
    pair_hbm, cot_hbm, in_gain_hbm, proj_weight_hbm, gate_weight_hbm, mid_gain_hbm, out_weight_hbm,
    pair_grad, early_out, late_out, gains_out,
    pair_in, cotangent, in_gain, proj_weight, gate_weight, mid_gain, out_weight,
    gains, weight, weight_t, out_t,
    state0, cot, grad1,
    unit, inverse, normed, sig_l, val_l, sig_r, val_r, gate, gate_der, output, mix_unit, mix_inverse, mixed,
    grad_mixed, scaled, scaled_mean, grad_normed,
    go, gp, in_acc, mid_acc,
    turn_a, turn_b, chan_l, chan_r, chan_g, late_sum,
    send2, recv2, send1, recv1,
    sum_early_send, pre_early, sum_early_mid, sum_early_recv, all_early, sum_late_send, sum_late_recv, all_late, gains_all,
    load_sem, send_sem, recv_sem,
):
    me = lax.axis_index("pair")
    my_x, my_y, my_core = me // 8, (me // 2) % 4, me % 2

    def peer(o):
        x = (my_x + o // 8) % 2
        y = (my_y + (o // 2) % 4) % 4
        core = (my_core + o % 2) % 2
        return x * 8 + y * 2 + core

    barrier = pltpu.get_barrier_semaphore()

    peers = [peer(o) for o in (4, 12, 5, 13, 2, 10, 6, 14, 3, 11, 7, 15, 8, 9, 1)]
    same_core = [peer(o) for o in (4, 12, 2, 10, 6, 14, 8)]
    chip = me // 2
    for target in peers:
        pl.semaphore_signal(barrier, inc=1, device_id={"pair": target}, device_id_type=MESH)

    loads = [
        pltpu.make_async_copy(source, target, load_sem.at[i])
        for i, (source, target) in enumerate((
            (pair_hbm, pair_in), (in_gain_hbm, in_gain), (proj_weight_hbm, proj_weight), (gate_weight_hbm, gate_weight),
            (mid_gain_hbm, mid_gain), (out_weight_hbm, out_weight), (cot_hbm, cotangent),
        ))
    ]
    for load in loads:
        load.start()

    def send_part(phase, h, src_of, dst, targets=None):
        sem = phase * CHUNKS + h
        for target in targets or peers:
            pltpu.make_async_remote_copy(
                src_ref=src_of(target), dst_ref=dst,
                send_sem=send_sem.at[sem], recv_sem=recv_sem.at[sem],
                device_id={"pair": target}, device_id_type=MESH,
            ).start()

    def wait_part(phase, h, slots):
        fifteen = slots.at[pl.ds(0, PEERS - 1)]
        pltpu.make_async_copy(fifteen, fifteen, recv_sem.at[phase * CHUNKS + h]).wait()

    def wait_bytes(phase, sems, some):
        pltpu.make_async_copy(some, some, sems.at[phase * CHUNKS]).wait()

    def wait_sent(phase, h, slots):
        fifteen = slots.at[pl.ds(0, PEERS - 1)]
        pltpu.make_async_copy(fifteen, fifteen, send_sem.at[phase * CHUNKS + h]).wait()

    in_acc[...] = jnp.zeros_like(in_acc)
    mid_acc[...] = jnp.zeros_like(mid_acc)

    def lanes(p):
        return slice(p * WIDE, (p + 1) * WIDE)

    def put_rows(ref, first, values):
        parts = [values[:, i * N : (i + 1) * N].reshape(PEERS, ROWS, N) for i in range(2)]
        ref[:, first : first + 2 * ROWS, :] = jnp.concatenate(parts, axis=1).astype(BF16)

    def get_rows(ref, first):
        block = ref[:, first : first + 2 * ROWS, :].astype(F32)
        return jnp.concatenate([block[:, i * ROWS : (i + 1) * ROWS].reshape(N, N) for i in range(2)], axis=1)

    def project(l, p, state, left_ref, right_ref, left_row, right_row):
        at = lanes(p)
        unit_p, inverse_p = norm_forward(state)
        normed_p = (unit_p * gains[2 * l]).astype(BF16)
        unit[l, :, at] = unit_p
        inverse[l, :, at] = inverse_p
        normed[l, :, at] = normed_p
        projected = nn(weight_t[l], normed_p)
        sig = sigmoid(projected[0:N])
        val = projected[N : 2 * N]
        sig_l[l, :, at] = sig
        val_l[l, :, at] = val
        put_rows(left_ref, left_row, sig * val)
        sig = sigmoid(projected[2 * N : 3 * N])
        val = projected[3 * N : 4 * N]
        sig_r[l, :, at] = sig
        val_r[l, :, at] = val
        put_rows(right_ref, right_row, sig * val)
        gate[l, :, at] = projected[4 * N :]

    def after_project(l):
        for p in range(STEPS):
            at = lanes(p)
            gate_p = sigmoid(gate[l, :, at])
            gate[l, :, at] = gate_p
            for sig, val in ((sig_l, val_l), (sig_r, val_r)):
                sig_p = sig[l, :, at]
                val[l, :, at] = val[l, :, at] * sig_p * (1.0 - sig_p)
            if l == 1:
                gate_der[0, :, at] = output[:, at] * gate[0, :, at] * (1.0 - gate[0, :, at])
                cot_p = cot[:, at]
                gate_der[1, :, at] = cot_p * gate_p * (1.0 - gate_p)
                go_p = (cot_p * gate_p).astype(BF16)
                go[1, :, at] = go_p
                grad_mixed_p = nn(out_weight[1], go_p)
                grad_mixed[:, at] = grad_mixed_p
                scaled_p = grad_mixed_p * gains[3]
                scaled[:, at] = scaled_p
                scaled_mean[:, at] = mean_channels(scaled_p)

    def steps(h):
        return range(h * PER, (h + 1) * PER)

    def send2_part(slot, phase, h):
        send_part(phase, h, lambda d: send2.at[slot, h, d], recv2.at[slot, h, me])
        recv2[slot, h, me] = send2[slot, h, me]

    def send1_part(slot, phase, h):
        send_part(phase, h, lambda d: send1.at[slot, h, d], recv1.at[slot, h, me])
        recv1[slot, h, me] = send1[slot, h, me]

    def wait2_part(slot, phase, h):
        wait_part(phase, h, recv2.at[slot, h])

    def wait1_part(slot, phase, h):
        wait_part(phase, h, recv1.at[slot, h])

    def part_rows(d, h):
        return slice(d * ROWS * ROWS + h * PART, d * ROWS * ROWS + (h + 1) * PART)

    def part_of(h):
        return pl.ds(h * PART, PART)

    def own_part(d, h):
        first = h * PEERS * PART + d * PART
        return slice(first, first + PART)

    def channel_part(c, h):
        return pl.ds(h * PEERS * PART + c, N // CHUNKS, stride=ROWS)

    def half(h):
        return slice(h * N // CHUNKS, (h + 1) * N // CHUNKS)

    def channel(c):
        return pl.ds(c, N, stride=ROWS)

    def channel_forward_0():
        wait_part(RIGHT_0, 0, recv2.at[0, 0])
        for s in range(PEERS):
            turn_b[s * 64 : s * 64 + 64, :] = recv2[0, 0, s].astype(F32)
        for c in range(ROWS):
            chan_r[0, c] = turn_b[channel(c), :].astype(BF16)
        for h in range(CHUNKS):
            wait_part(TO_CH_0, h, recv2.at[0, 1, :, part_of(h)])
            for s in range(PEERS):
                turn_a[own_part(s, h), :] = recv2[0, 1, s, h * PART : (h + 1) * PART].astype(F32)
            for c in range(ROWS):
                left = turn_a[channel_part(c, h), :].astype(BF16)
                chan_l[0, c, half(h)] = left
                turn_a[channel_part(c, h), :] = nt(left, chan_r[0, c])
            for d in range(PEERS):
                send1[0, h, d] = turn_a[own_part(d, h), :].astype(BF16)
            send1_part(0, TO_ROW_0, h)

    def channel_forward_1():
        for h in range(CHUNKS):
            wait2_part(1, TO_CH_1, h)
            for s in range(PEERS):
                turn_a[part_rows(s, h), :] = recv2[1, h, s, :PART].astype(F32)
                turn_b[part_rows(s, h), :] = recv2[1, h, s, PART:].astype(F32)
        for c in range(ROWS):
            left = turn_a[channel(c), :].astype(BF16)
            right = turn_b[channel(c), :].astype(BF16)
            chan_l[1, c] = left
            chan_r[1, c] = right
            turn_a[channel(c), :] = tn(left, right)
        for h in range(CHUNKS):
            for d in range(PEERS):
                send1[1, h, d] = turn_a[part_rows(d, h), :].astype(BF16)
            send1_part(1, TO_ROW_1, h)

    def channel_backward_1():
        for h in range(CHUNKS):
            wait1_part(2, GRAD_CH_1, h)
            for s in range(PEERS):
                turn_a[part_rows(s, h), :] = recv1[2, h, s].astype(F32)
        for c in range(ROWS):
            grad = turn_a[channel(c), :].astype(BF16)
            turn_a[channel(c), :] = nt(chan_r[1, c], grad)
            turn_b[channel(c), :] = nn(chan_l[1, c], grad)
        for h in range(CHUNKS):
            for d in range(PEERS):
                send2[2, h, d, :PART] = turn_a[part_rows(d, h), :].astype(BF16)
                send2[2, h, d, PART:] = turn_b[part_rows(d, h), :].astype(BF16)
            send2_part(2, GRAD_ROW_1, h)

    def channel_backward_0():
        left_rows = pl.ds(0, PART)
        for h in range(CHUNKS):
            wait1_part(3, GRAD_CH_0, h)
            for s in range(PEERS):
                turn_a[own_part(s, h), :] = recv1[3, h, s].astype(F32)
            for c in range(ROWS):
                grad = turn_a[channel_part(c, h), :].astype(BF16)
                chan_g[c, half(h)] = grad
                turn_b[channel_part(c, h), :] = nn(grad, chan_r[0, c])
            for d in range(PEERS):
                send2[3, h, d, :PART] = turn_b[own_part(d, h), :].astype(BF16)
            if h == 0:
                send_part(GRAD_LEFT_0, 0, lambda d: send2.at[3, 0, d, left_rows], recv2.at[3, 0, me, left_rows])
        for c in range(ROWS):
            turn_a[channel(c), :] = tn(chan_g[c], chan_l[0, c])
        for h in range(CHUNKS):
            for d in range(PEERS):
                send2[3, h, d, PART:] = turn_a[part_rows(d, h), :].astype(BF16)
            if h == 0:
                right_rows = pl.ds(PART, PART)
                send_part(GRAD_ROW_0, 0, lambda d: send2.at[3, 0, d, right_rows], recv2.at[3, 0, me, right_rows])
                recv2[3, 0, me] = send2[3, 0, me]
            else:
                send2_part(3, GRAD_ROW_0, h)

    def fold(values):
        return values[:, :N] + values[:, N:]

    def back_pieces(l, p, ref):
        at = lanes(p)
        row = 2 * ROWS * (p % PER)
        for side, (sig, val) in enumerate(((sig_l, val_l), (sig_r, val_r))):
            grad = get_rows(ref, side * PART + row)
            first = 2 * N * side
            gp[l, first : first + N, at] = (grad * val[l, :, at]).astype(BF16)
            gp[l, first + N : first + 2 * N, at] = (grad * sig[l, :, at]).astype(BF16)

    def back_tail(l, p, gradient):
        at = lanes(p)
        grad_normed_p = nn(weight[l], gp[l, :, at])
        unit_p = unit[l, :, at]
        if l == 1:
            grad_normed[:, at] = grad_normed_p
        else:
            in_acc[l] += fold(grad_normed_p * unit_p)
        return gradient + norm_backward(grad_normed_p * gains[2 * l], unit_p, inverse[l, :, at])

    loads[0].wait()
    for a in range(ROWS):
        state0[:, a * N : (a + 1) * N] = pair_in[a].astype(F32).T
    for load in loads[1:4]:
        load.wait()

    def set_gain(index, source, l):
        row = jnp.broadcast_to(source[l : l + 1, :], (N, N)).T
        gains[index] = jnp.concatenate([row, row], axis=1)

    def set_weights(l):
        set_gain(2 * l, in_gain, l)
        for f in range(4):
            block = proj_weight[l, :, f * N : (f + 1) * N]
            weight[l, :, f * N : (f + 1) * N] = block
            weight_t[l, f * N : (f + 1) * N, :] = block.astype(F32).T.astype(BF16)
        weight[l, :, 4 * N :] = gate_weight[l]
        weight_t[l, 4 * N :, :] = gate_weight[l].astype(F32).T.astype(BF16)

    set_weights(0)
    for p in range(STEPS):
        project(0, p, state0[:, lanes(p)], send2.at[0, 1], send2.at[0, 0], 2 * ROWS * p, 2 * ROWS * p)
    pl.semaphore_wait(barrier, PEERS - 1)
    send_part(RIGHT_0, 0, lambda d: send2.at[0, 0, d], recv2.at[0, 0, me])
    for h in range(CHUNKS):
        rows = part_of(h)
        send_part(TO_CH_0, h, lambda d: send2.at[0, 1, d, rows], recv2.at[0, 1, me, rows])
    for i in range(2):
        recv2[0, i, me] = send2[0, i, me]

    for load in loads[4:]:
        load.wait()
    set_weights(1)
    for l in range(2):
        set_gain(2 * l + 1, mid_gain, l)
        out_t[l] = out_weight[l].astype(F32).T.astype(BF16)
    for a in range(ROWS):
        cot[:, a * N : (a + 1) * N] = cotangent[a].astype(F32).T

    after_project(0)

    channel_forward_0()

    for h in range(CHUNKS):
        wait1_part(0, TO_ROW_0, h)
        for p in steps(h):
            at = lanes(p)
            mix_unit_p, mix_inverse_p = norm_forward(get_rows(recv1.at[0, h], 2 * ROWS * (p % PER)))
            mixed_p = (mix_unit_p * gains[1]).astype(BF16)
            mix_unit[0, :, at] = mix_unit_p
            mix_inverse[:, at] = mix_inverse_p
            mixed[0, :, at] = mixed_p
            output_p = nn(out_t[0], mixed_p)
            output[:, at] = output_p
            state = (state0[:, at] + gate[0, :, at] * output_p).astype(BF16).astype(F32)
            row = 2 * ROWS * (p % PER)
            project(1, p, state, send2.at[1, h], send2.at[1, h], row, PART + row)
        send2_part(1, TO_CH_1, h)

    after_project(1)

    channel_forward_1()

    for h in range(CHUNKS):
        wait1_part(1, TO_ROW_1, h)
        for p in steps(h):
            at = lanes(p)
            row = 2 * ROWS * (p % PER)
            mix_unit_p, mix_inverse_p = norm_forward(get_rows(recv1.at[1, h], row))
            mix_unit[1, :, at] = mix_unit_p
            scaled_p = scaled[:, at]
            mean_two = mean_channels(scaled_p * mix_unit_p)
            put_rows(send1.at[2, h], row, mix_inverse_p * (scaled_p - scaled_mean[:, at] - mix_unit_p * mean_two))
        send1_part(2, GRAD_CH_1, h)

    for p in range(STEPS):
        at = lanes(p)
        mix_unit_p = mix_unit[1, :, at]
        mixed_p = (mix_unit_p * gains[3]).astype(BF16)
        mixed[1, :, at] = mixed_p
        gp[1, 4 * N :, at] = (gate_der[1, :, at] * nn(out_t[1], mixed_p)).astype(BF16)
        mid_acc[1] += fold(grad_mixed[:, at] * mix_unit_p)

    channel_backward_1()

    for h in range(CHUNKS):
        wait2_part(2, GRAD_ROW_1, h)
        for p in steps(h):
            at = lanes(p)
            back_pieces(1, p, recv2.at[2, h])
            gradient = back_tail(1, p, cot[:, at])
            grad1[:, at] = gradient
            go_p = (gradient * gate[0, :, at]).astype(BF16)
            go[0, :, at] = go_p
            grad_mixed_p = nn(out_weight[0], go_p)
            grad_mixed[:, at] = grad_mixed_p
            grad_product = norm_backward(grad_mixed_p * gains[1], mix_unit[0, :, at], mix_inverse[:, at])
            put_rows(send1.at[3, h], 2 * ROWS * (p % PER), grad_product)
        send1_part(3, GRAD_CH_0, h)

    for p in range(STEPS):
        at = lanes(p)
        gp[0, 4 * N :, at] = (grad1[:, at] * gate_der[0, :, at]).astype(BF16)
        mid_acc[0] += fold(grad_mixed[:, at] * mix_unit[0, :, at])
        in_acc[1] += fold(grad_normed[:, at] * unit[1, :, at])

    def put_early(first, values):
        for i in range(N // 64):
            sum_early_send[i, first // 2] = values[64 * i : 64 * i + 64, :].astype(BF16)

    for f in range(5):
        put_early(2 * f, nt(normed[1], gp[1, f * N : (f + 1) * N, :]))
    put_early(10, nt(mixed[1], go[1]))
    put_early(12, nt(normed[0], gp[0, 4 * N :, :]))
    put_early(14, nt(mixed[0], go[0]))
    send_part(PRE_EARLY, 0, lambda d: sum_early_send.at[1 - my_core], pre_early, [peer(1)])

    wait_bytes(PRE_EARLY, recv_sem, pre_early)
    sum_early_mid[...] = (sum_early_send[my_core].astype(F32) + pre_early[...].astype(F32)).astype(BF16)
    send_part(SUM_EARLY, 0, lambda d: sum_early_mid.at[d // 2], sum_early_recv.at[chip], same_core)
    sum_early_recv[chip] = sum_early_mid[chip]

    channel_backward_0()

    def last_rows(p):
        gradient = back_tail(0, p, grad1[:, lanes(p)])
        for i in range(2):
            pair_grad[2 * p + i] = gradient[:, i * N : (i + 1) * N].T.astype(BF16)

    for h in range(CHUNKS):
        if h == 0:
            wait_part(GRAD_LEFT_0, 0, recv2.at[3, 0, :, pl.ds(0, PART)])
            wait_part(GRAD_ROW_0, 0, recv2.at[3, 0, :, pl.ds(PART, PART)])
        else:
            wait2_part(3, GRAD_ROW_0, h)
        for p in steps(h):
            back_pieces(0, p, recv2.at[3, h])
        if h < CHUNKS - 1:
            for p in steps(h):
                last_rows(p)
            for f in range(4):
                late_sum[f] = nt(normed[0, :, : CELLS // 2], gp[0, f * N : (f + 1) * N, : CELLS // 2])

    for f in range(4):
        values = late_sum[f] + nt(normed[0, :, CELLS // 2 :], gp[0, f * N : (f + 1) * N, CELLS // 2 :])
        for i in range(4):
            sum_late_send[4 * f + i] = values[32 * i : 32 * i + 32, :].astype(BF16)
    send_part(SUM_LATE, 0, lambda d: sum_late_send.at[d], sum_late_recv.at[me])
    sum_late_recv[me] = sum_late_send[me]

    wait_bytes(SUM_EARLY, recv_sem, sum_early_recv.at[pl.ds(0, 7)])
    all_early[my_core, chip] = jnp.sum(sum_early_recv[...].astype(F32), axis=0).astype(BF16)
    mine = all_early.at[my_core, chip]
    send_part(ALL_EARLY, 0, lambda d: mine, mine, same_core)

    for p in steps(CHUNKS - 1):
        last_rows(p)

    gain_rows = [jnp.sum(ref[l].T, axis=0, keepdims=True) for ref in (in_acc, mid_acc) for l in range(2)]
    gains_all[me] = jnp.concatenate(gain_rows + [jnp.zeros((4, N), F32)], axis=0)
    send_part(GAINS, 0, lambda d: gains_all.at[me], gains_all.at[me])

    wait_part(SUM_LATE, 0, sum_late_recv)
    all_late[me] = jnp.sum(sum_late_recv[...].astype(F32), axis=0).astype(BF16)
    send_part(ALL_LATE, 0, lambda d: all_late.at[me], all_late.at[me])

    wait_bytes(ALL_EARLY, recv_sem, all_early.at[0, pl.ds(0, 7)])
    send_part(SHARE_EARLY, 0, lambda d: all_early.at[my_core], all_early.at[my_core], [peer(1)])
    for h in range(CHUNKS):
        wait_sent(TO_CH_0, h, send2.at[0, 1, :, part_of(h)])
        wait_sent(TO_ROW_0, h, send1.at[0, h])
        for slot, two, one in ((1, TO_CH_1, TO_ROW_1), (2, GRAD_ROW_1, GRAD_CH_1)):
            wait_sent(two, h, send2.at[slot, h])
            wait_sent(one, h, send1.at[slot, h])
    wait_sent(RIGHT_0, 0, send2.at[0, 0])
    wait_sent(GRAD_LEFT_0, 0, send2.at[3, 0, :, pl.ds(0, PART)])
    wait_sent(GRAD_ROW_0, 0, send2.at[3, 0, :, pl.ds(PART, PART)])
    wait_sent(GRAD_ROW_0, 1, send2.at[3, 1])
    for h in range(CHUNKS):
        wait_sent(GRAD_CH_0, h, send1.at[3, h])
    wait_bytes(PRE_EARLY, send_sem, pre_early)
    wait_bytes(SUM_EARLY, send_sem, sum_early_mid.at[pl.ds(0, 7)])
    wait_bytes(ALL_EARLY, send_sem, all_early.at[0, pl.ds(0, 7)])
    wait_sent(SUM_LATE, 0, sum_late_send)
    wait_sent(GAINS, 0, gains_all)

    wait_bytes(SHARE_EARLY, recv_sem, all_early.at[0])
    early_out[...] = all_early[...]
    wait_bytes(SHARE_EARLY, send_sem, all_early.at[0])

    wait_part(GAINS, 0, gains_all)
    gains_out[...] = jnp.sum(gains_all[...], axis=0)

    wait_part(ALL_LATE, 0, all_late)
    late_out[...] = all_late[...]
    wait_sent(ALL_LATE, 0, all_late)


def write_kernel(
    pair, early_in, late_in, gains_in,
    pair_grad, proj_grad, gate_grad, out_grad, in_gain_grad, mid_gain_grad,
):
    scale = 1.0 / N
    pair_grad[...] = pair[...]

    def early(first):
        return early_in[:, first // 2].astype(F32).reshape(N, N) * scale

    for f in range(4):
        proj_grad[0, :, f * N : (f + 1) * N] = late_in[4 * f : 4 * f + 4].astype(F32).reshape(N, N) * scale
        proj_grad[1, :, f * N : (f + 1) * N] = early(2 * f)
    gate_grad[1] = early(8)
    out_grad[1] = early(10)
    gate_grad[0] = early(12)
    out_grad[0] = early(14)
    in_gain_grad[...] = gains_in[0:2, :] * scale
    mid_gain_grad[...] = gains_in[2:4, :] * scale


def on_device(*arrays):
    layer_f32 = pltpu.VMEM((2, N, CELLS), F32)
    layer_bf16 = pltpu.VMEM((2, N, CELLS), BF16)
    plain_f32 = pltpu.VMEM((N, CELLS), F32)
    vmem = pl.BlockSpec(memory_space=pltpu.VMEM)
    results = pl.pallas_call(
        kernel,
        out_shape=(
            pltpu.VMEM((ROWS, N, N), BF16),
            pltpu.VMEM((2, PEERS // 2, 64, N), BF16),
            pltpu.VMEM((PEERS, 32, N), BF16),
            pltpu.VMEM((8, N), F32),
        ),
        in_specs=[pl.BlockSpec(memory_space=pl.ANY)] * 7,
        out_specs=[vmem] * 4,
        scratch_shapes=[pltpu.VMEM(array.shape, array.dtype) for array in arrays] + [
            pltpu.VMEM((4, N, WIDE), F32),
            pltpu.VMEM((2, N, 5 * N), BF16),
            pltpu.VMEM((2, 5 * N, N), BF16),
            pltpu.VMEM((2, N, N), BF16),
            plain_f32, plain_f32, plain_f32,
            layer_f32,
            pltpu.VMEM((2, 1, CELLS), F32),
            layer_bf16,
            layer_f32, layer_f32, layer_f32, layer_f32,
            layer_f32, layer_f32, plain_f32, layer_f32,
            pltpu.VMEM((1, CELLS), F32),
            layer_bf16,
            plain_f32, plain_f32,
            pltpu.VMEM((1, CELLS), F32),
            plain_f32,
            layer_bf16,
            pltpu.VMEM((2, 5 * N, CELLS), BF16),
            pltpu.VMEM((2, N, N), F32),
            pltpu.VMEM((2, N, N), F32),
            pltpu.VMEM((CELLS + ROWS, N), F32),
            pltpu.VMEM((CELLS + ROWS, N), F32),
            pltpu.VMEM((2, ROWS, N, N), BF16),
            pltpu.VMEM((2, ROWS, N, N), BF16),
            pltpu.VMEM((ROWS, N, N), BF16),
            pltpu.VMEM((4, N, N), F32),
            pltpu.VMEM((4, CHUNKS, PEERS, 2 * PART, N), BF16),
            pltpu.VMEM((4, CHUNKS, PEERS, 2 * PART, N), BF16),
            pltpu.VMEM((4, CHUNKS, PEERS, PART, N), BF16),
            pltpu.VMEM((4, CHUNKS, PEERS, PART, N), BF16),
            pltpu.VMEM((2, PEERS // 2, 64, N), BF16),
            pltpu.VMEM((PEERS // 2, 64, N), BF16),
            pltpu.VMEM((PEERS // 2, 64, N), BF16),
            pltpu.VMEM((PEERS // 2, 64, N), BF16),
            pltpu.VMEM((2, PEERS // 2, 64, N), BF16),
            pltpu.VMEM((PEERS, 32, N), BF16),
            pltpu.VMEM((PEERS, 32, N), BF16),
            pltpu.VMEM((PEERS, 32, N), BF16),
            pltpu.VMEM((PEERS, 8, N), F32),
            pltpu.SemaphoreType.DMA((7,)),
            pltpu.SemaphoreType.DMA((PHASES * CHUNKS,)),
            pltpu.SemaphoreType.DMA((PHASES * CHUNKS,)),
        ],
        compiler_params=pltpu.CompilerParams(
            collective_id=0, has_side_effects=True, vmem_limit_bytes=56 * 1024 * 1024
        ),
    )(*arrays)
    return pl.pallas_call(
        write_kernel,
        out_shape=(
            jax.ShapeDtypeStruct((ROWS, N, N), BF16),
            jax.ShapeDtypeStruct((2, N, 4 * N), F32),
            jax.ShapeDtypeStruct((2, N, N), F32),
            jax.ShapeDtypeStruct((2, N, N), F32),
            jax.ShapeDtypeStruct((2, N), F32),
            jax.ShapeDtypeStruct((2, N), F32),
        ),
        in_specs=[vmem] * 4,
        out_specs=[vmem] * 6,
        compiler_params=pltpu.CompilerParams(vmem_limit_bytes=4 * 1024 * 1024),
    )(*results)


def solution(mesh):
    return jax.shard_map(
        on_device,
        mesh=mesh,
        in_specs=(
            P(("dp", "pair"), None, None),
            P(("dp", "pair"), None, None),
            P(),
            P(),
            P(),
            P(),
            P(),
        ),
        out_specs=(
            P(("dp", "pair"), None, None),
            P("dp", None, None),
            P("dp", None, None),
            P("dp", None, None),
            P("dp", None),
            P("dp", None),
        ),
        check_vma=False,
    )
```
